32 devices in a mesh: groups: 2 (over y), tensor: 16 (over z, x, core).
Axes of the slice: x: 2, y: 2, z: 4, core: 2. Of those that a mesh axis runs over, the one named last changes fastest.
Arguments:
- tapped: bfloat16 [256, 49152], P('groups', 'tensor'), parts along dimension 0, may hold values from -6 to 6
- join_weight: bfloat16 [49152, 8192], P('tensor'), may hold values from -0.02734375 to 0.02734375
- norm_gain: float32 [8192], replicated, may hold values from 0.25 to 1.75
- query_weight: bfloat16 [8192, 8192], P(None, 'tensor'), may hold values from -0.0625 to 0.0625
- kv_weight: bfloat16 [8192, 2048], P(None, 'tensor'), may hold values from -0.0625 to 0.0625
- out_weight: bfloat16 [8192, 8192], P('tensor'), may hold values from -0.0625 to 0.0625
- kv_cache: bfloat16 [4, 262144, 256], P('groups', 'tensor'), parts along dimension 0, may hold values from -360 to 360
- lengths: int32 [4], P('groups'), parts along dimension 0, may hold values from 1 to 32768, as said below
- parents: int32 [2, 256], P(None, 'groups'), parts along dimension 1, may hold values from 0 to 63
Outputs:
- draft_hidden: float32 [256, 8192], P(('groups', 'tensor')), parts along dimension 0
The draws below stay inside these ranges and needn't reach their ends.
There are 2 independent parts, one for each index of `groups`. The reference program is written for one: setup_inputs(seed, part) draws one part's arguments, and reference() takes and returns one part's arrays. A program takes and returns all parts, laid end to end along the dimension named above; an argument that names none is the same for every part. Nothing has to cross between parts.
Inputs may be any that keep to these rules, and one draw needn't show every extreme that they name: `lengths`: every sequence has at least one cached token, and in every part one sequence has exactly 32768. `parents`: node numbers within the row's sequence.
All inputs are finite; a program needn't handle non-finite values.
Results may differ from the reference program's by a relative error of at most 0.03.
Values may be sent and summed in bfloat16 or wider, within the bound.
No kernel may reach another device: no remote copies, remote signals or barrier semaphores. Data moves between devices by JAX's collectives and lax.ppermute only.
A program may use at most 384 MiB of HBM per device.

```python
import math
import jax
import jax.numpy as jnp
from jax import lax

H = 16384
DW = 8192
QH = 64
KVH = 8
HD = 128
QPK = 8
CTX = 32768
SEQS = 2
NODES = 64
STEPS = 3
ROWS = 128


def draw_lengths(key, part):
    key = jax.random.fold_in(key, 7)
    key_expo, key_value, key_full = jax.random.split(key, 3)
    exponent = jax.random.randint(key_expo, (SEQS,), 1, CTX.bit_length())
    ceiling = jnp.left_shift(jnp.ones((SEQS,), jnp.int32), exponent)
    values = jax.random.randint(key_value, (SEQS,), 1, ceiling + 1)
    full_seq = jax.random.randint(key_full, (), 0, SEQS)
    return jnp.where(jnp.arange(SEQS) == full_seq, CTX, jnp.minimum(values, CTX)).astype(jnp.int32)


def draw_kv_cache(key, part):
    key = jax.random.fold_in(key, 11)
    key_base, key_size = jax.random.split(key, 2)
    shape = (SEQS, KVH * CTX, 2 * HD)
    strength = jnp.exp(jax.random.uniform(key_size, (KVH,), jnp.float32, 0.0, math.log(2.5)))
    slot_scale = jnp.repeat(strength, CTX)
    base = jnp.clip(jax.random.normal(key_base, shape, jnp.float32), -6.0, 6.0)
    key_columns = jnp.arange(2 * HD) < HD
    scale = jnp.where(key_columns[None, :], slot_scale[:, None], 1.0)
    return (base * scale[None]).astype(jnp.bfloat16)


def touch_ends(entries, own_key, smallest, top_value):
    index_at = [jax.random.randint(jax.random.fold_in(own_key, axis), (), 0, length) for axis, length in enumerate(entries.shape)]
    longest = entries.shape.index(max(entries.shape))
    neighbour = index_at[:longest] + [(index_at[longest] + 1) % entries.shape[longest]] + index_at[longest + 1:]
    return entries.at[tuple(index_at)].set(smallest).at[tuple(neighbour)].set(top_value)


def levels(stream_key, dims, cuts, low, largest):
    def one(dim, blocks):
        steps = jax.random.uniform(jax.random.fold_in(jax.random.fold_in(stream_key, 6), dim), (blocks,), jnp.float32, low / len(cuts), largest / len(cuts))
        return jnp.repeat(jnp.exp(steps), dims[dim] // blocks).reshape((-1,) + (1,) * (len(dims) - dim - 1))

    factor_of = one(*cuts[0])
    for cut in cuts[1:]:
        factor_of = factor_of * one(*cut)
    return factor_of


def centred(stream_key, extent, spread, reach, cuts=(), kind=jnp.bfloat16):
    loudness = levels(stream_key, extent, cuts, -0.22, 0.18) if cuts else 1.0
    entries = jax.random.normal(stream_key, extent, jnp.float32) * spread * loudness
    return jnp.minimum(jnp.maximum(entries, -reach), reach).astype(kind)


def setup_inputs(seed: int = 0, part: int = 0) -> dict:
    keys = jax.random.split(jax.random.key(seed), 10)
    part_keys = jax.random.split(jax.random.fold_in(keys[9], part), 10)
    tapped = centred(part_keys[0], (ROWS, 3 * H), 1.0, 6.0, ((1, 16),))
    join_weight = centred(keys[1], (3 * H, DW), (3 * H) ** -0.5, 0.02734375, ((0, 16),))
    norm_gain = jnp.clip(1.0 + 0.15 * jax.random.normal(keys[2], (DW,), jnp.float32), 0.25, 1.75)
    query_weight = centred(keys[3], (DW, QH * HD), DW ** -0.5, 0.0625, ((1, 16),))
    kv_weight = centred(keys[4], (DW, 2 * KVH * HD), DW ** -0.5, 0.0625, ((1, 16),))
    out_weight = centred(keys[5], (QH * HD, DW), (QH * HD) ** -0.5, 0.0625, ((0, 16),))
    kv_cache = draw_kv_cache(jax.random.fold_in(jax.random.fold_in(keys[9], part), 71), part)
    lengths = draw_lengths(jax.random.fold_in(jax.random.fold_in(keys[9], part), 71), part)
    parents = touch_ends(jax.random.randint(part_keys[8], (STEPS - 1, ROWS), 0, NODES), jax.random.fold_in(part_keys[8], 1), 0, NODES - 1).astype(jnp.int32)
    return {"tapped": tapped, "join_weight": join_weight, "norm_gain": norm_gain, "query_weight": query_weight, "kv_weight": kv_weight, "out_weight": out_weight, "kv_cache": kv_cache, "lengths": lengths, "parents": parents}


epsilon = 1e-05
floor_score = -1e+30

def normalize(values, norm_gain):
    mean_square = lax.optimization_barrier(jnp.mean(values * values, axis=-1, keepdims=True))
    return (values * lax.rsqrt(mean_square + epsilon) * norm_gain).astype(jnp.bfloat16)

def attend_sequence(query_seq, new_seq, cache_seq, seq_length):
    score_scale = 1.0 / math.sqrt(HD)
    cache_heads = cache_seq.reshape(KVH, CTX, 2 * HD)
    visible = jnp.arange(CTX, dtype=jnp.int32) < seq_length

    def one_head(operands):
        query_head, new_head, cache_head = operands
        query_wide = query_head.astype(jnp.float32)
        keys_wide = cache_head[:, :HD].astype(jnp.float32)
        scores = jnp.einsum('nqd,cd->nqc', query_wide, keys_wide) * score_scale
        scores = jnp.where(visible, scores, floor_score)
        new_scores = jnp.einsum('nqd,ntd->nqt', query_wide, new_head[..., :HD].astype(jnp.float32)) * score_scale
        row_top = jnp.maximum(lax.optimization_barrier(jnp.max(scores, axis=-1)), lax.optimization_barrier(jnp.max(new_scores, axis=-1)))
        weights = jnp.where(visible, jnp.exp(scores - row_top[..., None]), 0.0)
        new_weights = jnp.exp(new_scores - row_top[..., None])
        row_sum = lax.optimization_barrier(jnp.sum(weights, axis=-1)) + lax.optimization_barrier(jnp.sum(new_weights, axis=-1))
        weights_low = lax.optimization_barrier(weights.astype(jnp.bfloat16)).astype(jnp.float32)
        new_low = lax.optimization_barrier(new_weights.astype(jnp.bfloat16)).astype(jnp.float32)
        numerator = jnp.einsum('nqc,cd->nqd', weights_low, cache_head[:, HD:].astype(jnp.float32))
        numerator = numerator + jnp.einsum('nqt,ntd->nqd', new_low, new_head[..., HD:].astype(jnp.float32))
        return (numerator / row_sum[..., None]).astype(jnp.bfloat16)
    results = lax.map(one_head, (query_seq.transpose(1, 0, 2, 3), new_seq.transpose(1, 0, 2, 3), cache_heads))
    return results.transpose(1, 0, 2, 3)

def reference(tapped, join_weight, norm_gain, query_weight, kv_weight, out_weight, kv_cache, lengths, parents):
    hidden = jnp.dot(tapped, join_weight, preferred_element_type=jnp.float32)
    row_ids = jnp.arange(ROWS, dtype=jnp.int32)
    seq_base = row_ids // NODES * NODES
    history = []
    for step_num in range(STEPS):
        normed = normalize(hidden, norm_gain)
        queries = jnp.dot(normed, query_weight, preferred_element_type=jnp.float32).astype(jnp.bfloat16)
        new_kv = jnp.dot(normed, kv_weight, preferred_element_type=jnp.float32).astype(jnp.bfloat16)
        history.append(new_kv.reshape(ROWS, KVH, 2 * HD))
        ancestors = [row_ids]
        current = row_ids
        for earlier in range(step_num - 1, -1, -1):
            current = seq_base + parents[earlier][current]
            ancestors.insert(0, current)
        gathered = jnp.stack([history[earlier][ancestors[earlier]] for earlier in range(step_num + 1)], axis=2)
        query_heads = queries.reshape(ROWS, KVH, QPK, HD)
        pieces = []
        for seq_num in range(SEQS):
            low_row = seq_num * NODES
            pieces.append(attend_sequence(query_heads[low_row:low_row + NODES], gathered[low_row:low_row + NODES], kv_cache[seq_num], lengths[seq_num]))
        attended = jnp.concatenate(pieces, axis=0).reshape(ROWS, QH * HD)
        hidden = hidden + jnp.dot(attended, out_weight, preferred_element_type=jnp.float32)
    return hidden
```

```python
import functools
import math

import jax
import jax.numpy as jnp
from jax import lax
from jax.experimental import pallas as pl
from jax.experimental.pallas import tpu as pltpu
from jax.sharding import PartitionSpec as P

KVH = 8
HD = 128
QPK = 8
STEPS = 3


epsilon = 1e-05
floor_score = -1e30


def partner(x, axis, distance):
    return lax.ppermute(x, axis, [(i, i ^ 1 << distance) for i in range(lax.axis_size(axis))])


def as_sent(x):

    def short(part):
        return part.astype(jnp.bfloat16) if part.dtype == jnp.float32 else part

    return jax.tree.map(short, x)


def normalize(values, norm_gain):
    mean_square = jnp.mean(values * values, axis=-1, keepdims=True)
    return (values * lax.rsqrt(mean_square + epsilon) * norm_gain).astype(jnp.bfloat16)


def merge_parts(mine, theirs):
    row_top = jnp.maximum(mine[0], theirs[0])
    mine_factor = jnp.exp(mine[0] - row_top)
    their_factor = jnp.exp(theirs[0] - row_top)
    row_sum = mine_factor * mine[1] + their_factor * theirs[1]
    numerator = mine_factor[..., None] * mine[2] + their_factor[..., None] * theirs[2]
    return (row_top, row_sum, numerator)


def local_general(
    tapped, join_weight, norm_gain, query_weight, kv_weight, out_weight, kv_cache, lengths, parents
):
    tensor_size = lax.axis_size("tensor")
    device = lax.axis_index("tensor")
    group_size = tensor_size // KVH
    hop_count = group_size.bit_length() - 1
    piece_index = device % group_size
    row_count_all = tapped.shape[0]
    seq_count = kv_cache.shape[0]
    node_count = row_count_all // seq_count
    query_cols = query_weight.shape[1]
    proj_weight = jnp.concatenate([query_weight, kv_weight], axis=1)
    score_scale = 1.0 / math.sqrt(HD)
    hidden_rows = lax.psum_scatter(
        jnp.dot(tapped, join_weight, preferred_element_type=jnp.float32),
        "tensor",
        scatter_dimension=0,
        tiled=True,
    )
    piece_len = kv_cache.shape[1]
    positions = piece_index * piece_len + jnp.arange(piece_len, dtype=jnp.int32)
    visible = positions[None, :] < lengths[:, None]
    is_first = piece_index == 0
    keys_cache = kv_cache[:, :, :HD]
    values_cache = kv_cache[:, :, HD:]
    row_ids = jnp.arange(row_count_all, dtype=jnp.int32)
    seq_base = row_ids // node_count * node_count
    head_rows = node_count * QPK
    width = out_weight.shape[0]
    history = []
    for step_num in range(STEPS):
        projected = jnp.dot(
            lax.all_gather(normalize(hidden_rows, norm_gain), "tensor", axis=0, tiled=True),
            proj_weight,
            preferred_element_type=jnp.float32,
        ).astype(jnp.bfloat16)
        query_group = projected[:, :query_cols]
        kv_group = projected[:, query_cols:]
        for bit_num in range(hop_count):
            other_query, other_kv = partner((query_group, kv_group), "tensor", bit_num)
            is_upper = device // (1 << bit_num) % 2 == 1
            query_group = jnp.where(
                is_upper,
                jnp.concatenate([other_query, query_group], axis=1),
                jnp.concatenate([query_group, other_query], axis=1),
            )
            kv_group = jnp.where(
                is_upper,
                jnp.concatenate([other_kv, kv_group], axis=1),
                jnp.concatenate([kv_group, other_kv], axis=1),
            )
        history.append(kv_group)
        ancestors = [row_ids]
        current = row_ids
        for earlier in range(step_num - 1, -1, -1):
            current = seq_base + jnp.take(parents[earlier], current, axis=0)
            ancestors.insert(0, current)
        new_depth = step_num + 1
        new_kv = jnp.stack(
            [
                jnp.take(history[earlier], ancestors[earlier], axis=0)
                for earlier in range(new_depth)
            ],
            axis=1,
        )
        new_keys = new_kv[..., :HD].reshape(seq_count, node_count, new_depth, HD)
        new_values = new_kv[..., HD:].reshape(seq_count, node_count, new_depth, HD)
        query_blocks = query_group.reshape(seq_count, head_rows, HD)
        scores = (
            jnp.einsum("brd,bcd->brc", query_blocks, keys_cache, preferred_element_type=jnp.float32)
            * score_scale
        )
        scores = jnp.where(visible[:, None, :], scores, floor_score)
        query_nodes = query_group.reshape(seq_count, node_count, QPK, HD)
        new_scores = (
            jnp.einsum("bnqd,bntd->bnqt", query_nodes, new_keys, preferred_element_type=jnp.float32)
            * score_scale
        )
        new_scores = jnp.where(is_first, new_scores, floor_score)
        row_top = jnp.maximum(
            jnp.max(scores, axis=-1), jnp.max(new_scores, axis=-1).reshape(seq_count, head_rows)
        )
        weights = jnp.where(visible[:, None, :], jnp.exp(scores - row_top[..., None]), 0.0)
        top_nodes = row_top.reshape(seq_count, node_count, QPK)
        new_weights = jnp.where(is_first, jnp.exp(new_scores - top_nodes[..., None]), 0.0)
        row_sum = jnp.sum(weights, axis=-1) + jnp.sum(new_weights, axis=-1).reshape(
            seq_count, head_rows
        )
        numerator = jnp.einsum(
            "brc,bcd->brd",
            weights.astype(jnp.bfloat16),
            values_cache,
            preferred_element_type=jnp.float32,
        )
        new_part = jnp.einsum(
            "bnqt,bntd->bnqd",
            new_weights.astype(jnp.bfloat16),
            new_values,
            preferred_element_type=jnp.float32,
        )
        numerator = numerator + new_part.reshape(seq_count, head_rows, HD)
        partial_value = (row_top, row_sum, numerator)
        for bit_num in range(hop_count):
            theirs = partner(
                (as_sent(partial_value[0]), as_sent(partial_value[1]), as_sent(partial_value[2])),
                "tensor",
                bit_num,
            )
            partial_value = merge_parts(partial_value, theirs)
        attended = (
            (partial_value[2] / partial_value[1][..., None])
            .astype(jnp.bfloat16)
            .reshape(row_count_all, QPK * HD)
        )
        attended_mine = lax.dynamic_slice_in_dim(attended, piece_index * width, width, 1)
        hidden_rows = hidden_rows + lax.psum_scatter(
            jnp.dot(attended_mine, out_weight, preferred_element_type=jnp.float32),
            "tensor",
            scatter_dimension=0,
            tiled=True,
        )
    return hidden_rows


BLOCK = 2048
CHUNK = 1024
GROUP = 256


def attend_kernel(depth, info_ref, mine_ref, other_ref, *refs):
    key_refs, value_refs, bias_refs = refs[:depth], refs[depth:2 * depth], refs[2 * depth:3 * depth]
    cache_ref, keep_ref, keep_lse_ref, send_ref = refs[3 * depth:3 * depth + 4]
    query_s, score_s, next_s, top_s, sum_s, cache_s, sems = refs[3 * depth + 4:]
    seq_count = cache_ref.shape[0]
    node_count = mine_ref.shape[0] // seq_count
    half_heads = mine_ref.shape[1] // HD
    seq_rows = 2 * half_heads * node_count
    groups = seq_rows // GROUP
    to_log2 = math.log2(math.e) / math.sqrt(HD)
    steps = [lax.div(info_ref[b] + BLOCK - 1, BLOCK) for b in range(seq_count)]
    total = sum(steps)

    def place(i):
        seq = jnp.int32(0)
        block = i
        for b in range(seq_count - 1):
            passed = block >= steps[b]
            later = jnp.logical_and(passed, seq == b)
            seq = jnp.where(later, b + 1, seq)
            block = jnp.where(later, block - steps[b], block)
        return seq, block

    def fetch(i, slot):
        seq, block = place(i)
        start = pl.multiple_of(block * BLOCK, BLOCK)
        return pltpu.make_async_copy(
            cache_ref.at[seq, pl.ds(start, BLOCK), :], cache_s.at[slot], sems.at[slot]
        )

    @pl.when(total > 0)
    def _():
        fetch(0, 0).start()

    for b in range(seq_count):
        rows = slice(b * node_count, (b + 1) * node_count)
        for h in range(2 * half_heads):
            ref = mine_ref if h < half_heads else other_ref
            col = h % half_heads * HD
            row = b * seq_rows + h * node_count
            query_s[row:row + node_count, :] = ref[rows, col:col + HD]

    @pl.when(info_ref[seq_count] == 0)
    def _():
        top_s[...] = jnp.full(top_s.shape, floor_score, jnp.float32)
        sum_s[...] = jnp.zeros(sum_s.shape, jnp.float32)

    @pl.when(info_ref[seq_count] != 0)
    def _():
        for b in range(seq_count):
            rows = slice(b * seq_rows, (b + 1) * seq_rows)
            query = query_s[rows, :]
            scores = []
            for t in range(depth):
                bias = bias_refs[t][b * node_count:(b + 1) * node_count, :]
                score = lax.dot_general(
                    query, key_refs[t][...], (((1,), (1,)), ((), ())),
                    preferred_element_type=jnp.float32,
                )
                scores.append(score * to_log2 + jnp.concatenate([bias] * (2 * half_heads), axis=0))
            top = functools.reduce(jnp.maximum, scores)
            top = jnp.broadcast_to(jnp.max(top, axis=1, keepdims=True), top.shape)
            gathered = jnp.zeros((seq_rows, 2 * HD), jnp.float32)
            for t in range(depth):
                weight = jnp.exp2(scores[t] - top).astype(jnp.bfloat16)
                value = value_refs[t][...]
                value = jnp.concatenate([value, jnp.ones_like(value)], axis=1)
                gathered = gathered + jnp.dot(weight, value, preferred_element_type=jnp.float32)
            top_s[rows, :] = top
            sum_s[rows, :] = gathered

    def process(seq, slot, left):
        def score_pass(masked):
            for g in range(groups):
                rows = pl.ds(pl.multiple_of(seq * seq_rows + g * GROUP, GROUP), GROUP)
                query = query_s[rows, :]
                high = None
                for c in range(0, BLOCK, CHUNK):
                    score = lax.dot_general(
                        query, cache_s[slot, c:c + CHUNK, :HD], (((1,), (1,)), ((), ())),
                        preferred_element_type=jnp.float32,
                    )
                    if masked:
                        at = lax.broadcasted_iota(jnp.int32, (1, CHUNK), 1) + c
                        score = jnp.where(at < left, score, floor_score)
                    score_s[g * GROUP:(g + 1) * GROUP, c:c + CHUNK] = score
                    for k in range(0, CHUNK, HD):
                        piece = score[:, k:k + HD]
                        high = piece if high is None else jnp.maximum(high, piece)
                high = jnp.broadcast_to(jnp.max(high, axis=1, keepdims=True), (GROUP, HD))
                next_s[g * GROUP:(g + 1) * GROUP, :] = high * to_log2

        pl.when(left >= BLOCK)(lambda: score_pass(False))
        pl.when(left < BLOCK)(lambda: score_pass(True))
        for g in range(groups):
            rows = pl.ds(pl.multiple_of(seq * seq_rows + g * GROUP, GROUP), GROUP)
            old = top_s[rows, :]
            top = jnp.maximum(old, next_s[g * GROUP:(g + 1) * GROUP, :])
            top_s[rows, :] = top
            factor = jnp.exp2(old - top)
            gathered = sum_s[rows, :] * jnp.concatenate([factor, factor], axis=1)
            tops = jnp.concatenate([top] * (CHUNK // HD), axis=1)
            for c in range(0, BLOCK, CHUNK):
                weight = jnp.exp2(score_s[g * GROUP:(g + 1) * GROUP, c:c + CHUNK] * to_log2 - tops)
                value = cache_s[slot, c:c + CHUNK, HD:]
                value = jnp.concatenate([value, jnp.ones_like(value)], axis=1)
                gathered = gathered + jnp.dot(
                    weight.astype(jnp.bfloat16), value, preferred_element_type=jnp.float32
                )
            sum_s[rows, :] = gathered

    @pl.loop(0, total)
    def _(i):
        slot = lax.rem(i, 2)

        @pl.when(i + 1 < total)
        def _():
            fetch(i + 1, 1 - slot).start()

        fetch(i, slot).wait()
        seq, block = place(i)
        process(seq, slot, info_ref[seq] - block * BLOCK)

    for b in range(seq_count):
        rows = slice(b * node_count, (b + 1) * node_count)
        for h in range(2 * half_heads):
            row = b * seq_rows + h * node_count
            weight_sum = sum_s[row:row + node_count, HD:]
            result = sum_s[row:row + node_count, :HD] / jnp.maximum(weight_sum, 1e-30)
            lse = top_s[row:row + node_count, :] + jnp.log2(jnp.maximum(weight_sum, 1e-30))
            col = h % half_heads * HD
            if h < half_heads:
                keep_ref[rows, col:col + HD] = result
                keep_lse_ref[rows, col:col + HD] = lse
            else:
                send_ref[rows, col:col + HD] = result
                send_ref[rows, half_heads * HD + col:half_heads * HD + col + HD] = lse


def attend(info, mine, other, keys, values, biases, cache):
    depth = len(keys)
    row_count, width = mine.shape
    seq_count, slot_count = cache.shape[:2]
    all_rows = 2 * width // HD * row_count
    vmem = pl.BlockSpec(memory_space=pltpu.VMEM)
    return pl.pallas_call(
        functools.partial(attend_kernel, depth),
        out_shape=(
            jax.ShapeDtypeStruct((row_count, width), jnp.float32),
            jax.ShapeDtypeStruct((row_count, width), jnp.float32),
            jax.ShapeDtypeStruct((row_count, 2 * width), jnp.float32),
        ),
        in_specs=[pl.BlockSpec(memory_space=pltpu.SMEM)]
        + [vmem] * (2 + 3 * depth)
        + [pl.BlockSpec(memory_space=pl.ANY)],
        out_specs=(vmem, vmem, vmem),
        scratch_shapes=[
            pltpu.VMEM((all_rows, HD), jnp.bfloat16),
            pltpu.VMEM((all_rows // seq_count, BLOCK), jnp.float32),
            pltpu.VMEM((all_rows // seq_count, HD), jnp.float32),
            pltpu.VMEM((all_rows, HD), jnp.float32),
            pltpu.VMEM((all_rows, 2 * HD), jnp.float32),
            pltpu.VMEM((2, BLOCK, 2 * HD), jnp.bfloat16),
            pltpu.SemaphoreType.DMA((2,)),
        ],
        compiler_params=pltpu.CompilerParams(vmem_limit_bytes=40 * 1024 * 1024),
        cost_estimate=pl.CostEstimate(
            flops=4 * all_rows * slot_count * HD,
            bytes_accessed=2 * cache.size,
            transcendentals=all_rows * slot_count,
        ),
        name="attend",
    )(info, mine, other, *keys, *values, *biases, cache)


def bit_of(distance):
    return lax.axis_index("tensor") // (1 << distance) % 2


def fold(x, axis, distance, kind):
    bit = bit_of(distance)
    keep = lax.dynamic_index_in_dim(x, bit, axis, keepdims=False)
    send = lax.dynamic_index_in_dim(x, 1 - bit, axis, keepdims=False).astype(kind)
    return keep + partner(send, "tensor", distance).astype(jnp.float32)


def unfold(x, axis, distance):
    other = partner(x, "tensor", distance)
    upper = bit_of(distance) == 1
    return jnp.where(upper, jnp.stack([other, x], axis), jnp.stack([x, other], axis))


def sum_to_rows(partial, bits):
    rows, columns = partial.shape
    parts = partial.reshape((2,) * bits + (rows >> bits, columns))
    parts = fold(parts, bits - 1, 0, jnp.float32)
    half = columns // 2
    first, second = parts[..., :half], parts[..., half:]
    for distance in range(1, bits):
        first = fold(first, bits - 1 - distance, distance, jnp.bfloat16)
    order = list(range(2, bits)) + [1]
    left = list(range(bits - 1, 0, -1))
    for distance in order:
        second = fold(second, left.index(distance), distance, jnp.bfloat16)
        left.remove(distance)
    return jnp.concatenate([first, second], axis=-1)


def rows_to_all(rows, bits):
    count, columns = rows.shape
    half = columns // 2
    first, second = rows[:, :half], rows[:, half:]
    for distance in range(bits - 1, 0, -1):
        first = unfold(first, bits - 1 - distance, distance)
    have = []
    for distance in [1] + list(range(bits - 1, 1, -1)):
        have = sorted(have + [distance], reverse=True)
        second = unfold(second, have.index(distance), distance)
    both = jnp.concatenate([first, second], axis=-1)
    return unfold(both, bits - 1, 0).reshape(count << bits, columns)


def local_pairs(
    tapped, join_weight, norm_gain, query_weight, kv_weight, out_weight, kv_cache, lengths, parents
):
    tensor_size = lax.axis_size("tensor")
    bits = tensor_size.bit_length() - 1
    side = lax.axis_index("tensor") % 2
    row_count = tapped.shape[0]
    seq_count, piece_len = kv_cache.shape[:2]
    node_count = row_count // seq_count
    row_ids = jnp.arange(row_count, dtype=jnp.int32)
    valid = jnp.clip(lengths - side * piece_len, 0, piece_len)
    info = jnp.concatenate([valid, (1 - side)[None]]).astype(jnp.int32)
    parent_rows = row_ids // node_count * node_count + parents
    from_row = (parent_rows[:, :, None] == row_ids).astype(jnp.float32)
    hops = {}
    for step in range(STEPS):
        hops[step, step] = jnp.eye(row_count, dtype=jnp.float32)
        for earlier in range(step - 1, -1, -1):
            hops[step, earlier] = jnp.dot(hops[step, earlier + 1], from_row[earlier])
    bias = {at: (hop - 1.0) * -floor_score for at, hop in hops.items()}
    hidden = sum_to_rows(jnp.dot(tapped, join_weight, preferred_element_type=jnp.float32), bits)
    keys, values = [], []
    for step in range(STEPS):
        normed = rows_to_all(normalize(hidden, norm_gain), bits)
        new_kv = jnp.dot(normed, kv_weight, preferred_element_type=jnp.float32)
        new_kv = new_kv.astype(jnp.bfloat16)
        query = jnp.dot(normed, query_weight, preferred_element_type=jnp.float32)
        query = query.astype(jnp.bfloat16)
        keys.append(new_kv)
        values.append(partner(new_kv, "tensor", 0))
        kept, kept_lse, sent = attend(
            info, query, partner(query, "tensor", 0), keys, values,
            [bias[step, t] for t in range(step + 1)], kv_cache,
        )
        came = partner(sent, "tensor", 0)
        width = kept.shape[1]
        top = jnp.maximum(kept_lse, came[:, width:])
        mine = jnp.exp2(kept_lse - top)
        theirs = jnp.exp2(came[:, width:] - top)
        attended = (mine * kept + theirs * came[:, :width]) / (mine + theirs)
        update = jnp.dot(
            attended.astype(jnp.bfloat16), out_weight, preferred_element_type=jnp.float32
        )
        hidden = hidden + sum_to_rows(update, bits)
    return hidden


def solution(mesh):
    body = local_pairs if mesh.shape["tensor"] == 2 * KVH else local_general
    placed = (
        P("groups", "tensor"),
        P("tensor", None),
        P(),
        P(None, "tensor"),
        P(None, "tensor"),
        P("tensor", None),
        P("groups", "tensor", None),
        P("groups"),
        P(None, "groups"),
    )
    return jax.shard_map(
        body, mesh=mesh, in_specs=placed, out_specs=P(("groups", "tensor"), None), check_vma=False
    )
```

```python
import functools
import math

import jax
import jax.numpy as jnp
from jax import lax
from jax.experimental import pallas as pl
from jax.experimental.pallas import tpu as pltpu
from jax.sharding import PartitionSpec as P

KVH = 8
HD = 128
QPK = 8
STEPS = 3


epsilon = 1e-05
floor_score = -1e30


def partner(x, axis, distance):
    return lax.ppermute(x, axis, [(i, i ^ 1 << distance) for i in range(lax.axis_size(axis))])


def as_sent(x):

    def short(part):
        return part.astype(jnp.bfloat16) if part.dtype == jnp.float32 else part

    return jax.tree.map(short, x)


def normalize(values, norm_gain):
    mean_square = jnp.mean(values * values, axis=-1, keepdims=True)
    return (values * lax.rsqrt(mean_square + epsilon) * norm_gain).astype(jnp.bfloat16)


def merge_parts(mine, theirs):
    row_top = jnp.maximum(mine[0], theirs[0])
    mine_factor = jnp.exp(mine[0] - row_top)
    their_factor = jnp.exp(theirs[0] - row_top)
    row_sum = mine_factor * mine[1] + their_factor * theirs[1]
    numerator = mine_factor[..., None] * mine[2] + their_factor[..., None] * theirs[2]
    return (row_top, row_sum, numerator)


def local_general(
    tapped, join_weight, norm_gain, query_weight, kv_weight, out_weight, kv_cache, lengths, parents
):
    tensor_size = lax.axis_size("tensor")
    device = lax.axis_index("tensor")
    group_size = tensor_size // KVH
    hop_count = group_size.bit_length() - 1
    piece_index = device % group_size
    row_count_all = tapped.shape[0]
    seq_count = kv_cache.shape[0]
    node_count = row_count_all // seq_count
    query_cols = query_weight.shape[1]
    proj_weight = jnp.concatenate([query_weight, kv_weight], axis=1)
    score_scale = 1.0 / math.sqrt(HD)
    hidden_rows = lax.psum_scatter(
        jnp.dot(tapped, join_weight, preferred_element_type=jnp.float32),
        "tensor",
        scatter_dimension=0,
        tiled=True,
    )
    piece_len = kv_cache.shape[1]
    positions = piece_index * piece_len + jnp.arange(piece_len, dtype=jnp.int32)
    visible = positions[None, :] < lengths[:, None]
    is_first = piece_index == 0
    keys_cache = kv_cache[:, :, :HD]
    values_cache = kv_cache[:, :, HD:]
    row_ids = jnp.arange(row_count_all, dtype=jnp.int32)
    seq_base = row_ids // node_count * node_count
    head_rows = node_count * QPK
    width = out_weight.shape[0]
    history = []
    for step_num in range(STEPS):
        projected = jnp.dot(
            lax.all_gather(normalize(hidden_rows, norm_gain), "tensor", axis=0, tiled=True),
            proj_weight,
            preferred_element_type=jnp.float32,
        ).astype(jnp.bfloat16)
        query_group = projected[:, :query_cols]
        kv_group = projected[:, query_cols:]
        for bit_num in range(hop_count):
            other_query, other_kv = partner((query_group, kv_group), "tensor", bit_num)
            is_upper = device // (1 << bit_num) % 2 == 1
            query_group = jnp.where(
                is_upper,
                jnp.concatenate([other_query, query_group], axis=1),
                jnp.concatenate([query_group, other_query], axis=1),
            )
            kv_group = jnp.where(
                is_upper,
                jnp.concatenate([other_kv, kv_group], axis=1),
                jnp.concatenate([kv_group, other_kv], axis=1),
            )
        history.append(kv_group)
        ancestors = [row_ids]
        current = row_ids
        for earlier in range(step_num - 1, -1, -1):
            current = seq_base + jnp.take(parents[earlier], current, axis=0)
            ancestors.insert(0, current)
        new_depth = step_num + 1
        new_kv = jnp.stack(
            [
                jnp.take(history[earlier], ancestors[earlier], axis=0)
                for earlier in range(new_depth)
            ],
            axis=1,
        )
        new_keys = new_kv[..., :HD].reshape(seq_count, node_count, new_depth, HD)
        new_values = new_kv[..., HD:].reshape(seq_count, node_count, new_depth, HD)
        query_blocks = query_group.reshape(seq_count, head_rows, HD)
        scores = (
            jnp.einsum("brd,bcd->brc", query_blocks, keys_cache, preferred_element_type=jnp.float32)
            * score_scale
        )
        scores = jnp.where(visible[:, None, :], scores, floor_score)
        query_nodes = query_group.reshape(seq_count, node_count, QPK, HD)
        new_scores = (
            jnp.einsum("bnqd,bntd->bnqt", query_nodes, new_keys, preferred_element_type=jnp.float32)
            * score_scale
        )
        new_scores = jnp.where(is_first, new_scores, floor_score)
        row_top = jnp.maximum(
            jnp.max(scores, axis=-1), jnp.max(new_scores, axis=-1).reshape(seq_count, head_rows)
        )
        weights = jnp.where(visible[:, None, :], jnp.exp(scores - row_top[..., None]), 0.0)
        top_nodes = row_top.reshape(seq_count, node_count, QPK)
        new_weights = jnp.where(is_first, jnp.exp(new_scores - top_nodes[..., None]), 0.0)
        row_sum = jnp.sum(weights, axis=-1) + jnp.sum(new_weights, axis=-1).reshape(
            seq_count, head_rows
        )
        numerator = jnp.einsum(
            "brc,bcd->brd",
            weights.astype(jnp.bfloat16),
            values_cache,
            preferred_element_type=jnp.float32,
        )
        new_part = jnp.einsum(
            "bnqt,bntd->bnqd",
            new_weights.astype(jnp.bfloat16),
            new_values,
            preferred_element_type=jnp.float32,
        )
        numerator = numerator + new_part.reshape(seq_count, head_rows, HD)
        partial_value = (row_top, row_sum, numerator)
        for bit_num in range(hop_count):
            theirs = partner(
                (as_sent(partial_value[0]), as_sent(partial_value[1]), as_sent(partial_value[2])),
                "tensor",
                bit_num,
            )
            partial_value = merge_parts(partial_value, theirs)
        attended = (
            (partial_value[2] / partial_value[1][..., None])
            .astype(jnp.bfloat16)
            .reshape(row_count_all, QPK * HD)
        )
        attended_mine = lax.dynamic_slice_in_dim(attended, piece_index * width, width, 1)
        hidden_rows = hidden_rows + lax.psum_scatter(
            jnp.dot(attended_mine, out_weight, preferred_element_type=jnp.float32),
            "tensor",
            scatter_dimension=0,
            tiled=True,
        )
    return hidden_rows


BLOCK = 2048
CHUNK = 1024
TO_LOG2 = math.log2(math.e) / math.sqrt(HD)


def score_dot(query, key):
    return lax.dot_general(
        query, key, (((1,), (1,)), ((), ())), preferred_element_type=jnp.float32
    )


def spread_max(x):
    return jnp.broadcast_to(jnp.max(x, axis=1, keepdims=True), (x.shape[0], HD))


def wide(x, width):
    return jnp.concatenate([x] * (width // HD), axis=1)


def with_ones(value):
    return jnp.concatenate([value, jnp.ones_like(value)], axis=1)


def attend_kernel(depth, seq, info_ref, mine_ref, other_ref, *refs):
    key_refs, value_refs = refs[:depth], refs[depth:2 * depth]
    bias_ref, cache_ref, keep_ref, keep_lse_ref, send_ref = refs[2 * depth:2 * depth + 5]
    query_s, score_s, high_s, top_s, sum_s = (refs[i:i + 2] for i in range(2 * depth + 5, 2 * depth + 15, 2))
    cache_s, live_s, sems = refs[2 * depth + 15:]
    node_count = mine_ref.shape[0]
    heads = mine_ref.shape[1] // HD
    valid = info_ref[0]
    total = lax.div(valid + BLOCK - 1, BLOCK)
    slots = cache_s.shape[0]

    def fetch(i):
        slot = lax.rem(i, slots)
        start = pl.multiple_of(i * BLOCK, BLOCK)
        return pltpu.make_async_copy(
            cache_ref.at[seq, pl.ds(start, BLOCK), :], cache_s.at[slot], sems.at[slot]
        )

    for i in range(2):
        pl.when(i < total)(lambda i=i: fetch(jnp.int32(i)).start())

    for g, ref in enumerate((mine_ref, other_ref)):
        for h in range(heads):
            query_s[g][h * node_count:(h + 1) * node_count, :] = ref[:, h * HD:(h + 1) * HD]
    live_s[0] = jnp.ones((BLOCK, HD), jnp.bfloat16)

    @pl.when(info_ref[1] == 0)
    def _():
        for g in range(2):
            top_s[g][...] = jnp.full(top_s[g].shape, floor_score, jnp.float32)
            sum_s[g][...] = jnp.zeros(sum_s[g].shape, jnp.float32)

    @pl.when(info_ref[1] != 0)
    def _():
        def joined(parts):
            spare = bias_ref.shape[1] - depth * node_count
            parts = [part[...] for part in parts]
            if spare:
                parts.append(jnp.zeros((spare, HD), jnp.bfloat16))
            return jnp.concatenate(parts, axis=0)

        key, value = joined(key_refs), with_ones(joined(value_refs))
        bias = jnp.concatenate([bias_ref[...]] * heads, axis=0)
        for g in range(2):
            score = score_dot(query_s[g][...], key) * TO_LOG2 + bias
            top = spread_max(score)
            weight = jnp.exp2(score - wide(top, score.shape[1])).astype(jnp.bfloat16)
            top_s[g][...] = top
            sum_s[g][...] = jnp.dot(weight, value, preferred_element_type=jnp.float32)

    def patch(i):
        left = valid - i * BLOCK
        slot = lax.rem(i, slots)

        @pl.when(left < BLOCK)
        def _():
            inside = lax.broadcasted_iota(jnp.int32, (BLOCK, HD), 0) < left
            key = cache_s[slot, :, :HD].astype(jnp.float32)
            value = cache_s[slot, :, HD:].astype(jnp.float32)
            key = jnp.where(inside, key, jnp.broadcast_to(key[:1, :], key.shape))
            cache_s[slot, :, :HD] = key.astype(jnp.bfloat16)
            cache_s[slot, :, HD:] = jnp.where(inside, value, 0.0).astype(jnp.bfloat16)
            live_s[1] = jnp.where(inside, 1.0, 0.0).astype(jnp.bfloat16)

    def score_chunk(g, slot, c, high):
        score = score_dot(query_s[g][...], cache_s[slot, c:c + CHUNK, :HD])
        score_s[g][:, c:c + CHUNK] = score
        for k in range(0, CHUNK, HD):
            piece = score[:, k:k + HD]
            high = piece if high is None else jnp.maximum(high, piece)
        return high

    def scores_of(g, slot):
        high = None
        for c in range(0, BLOCK, CHUNK):
            high = score_chunk(g, slot, c, high)
        high_s[g][...] = spread_max(high) * TO_LOG2

    def weigh_and_score(g, slot, part, ahead, ahead_slot):
        old = top_s[g][...]
        top = jnp.maximum(old, high_s[g][...])
        top_s[g][...] = top
        total_sum = sum_s[g][...] * wide(jnp.exp2(old - top), 2 * HD)
        tops = wide(top, CHUNK)
        high = None
        for c in range(0, BLOCK, CHUNK):
            weight = jnp.exp2(score_s[g][:, c:c + CHUNK] * TO_LOG2 - tops).astype(jnp.bfloat16)
            high = score_chunk(ahead, ahead_slot, c, high)
            value = jnp.concatenate(
                [cache_s[slot, c:c + CHUNK, HD:], live_s[part, c:c + CHUNK, :]], axis=1
            )
            total_sum = total_sum + jnp.dot(weight, value, preferred_element_type=jnp.float32)
        sum_s[g][...] = total_sum
        high_s[ahead][...] = spread_max(high) * TO_LOG2

    @pl.when(total > 0)
    def _():
        fetch(jnp.int32(0)).wait()
        patch(jnp.int32(0))
        scores_of(0, 0)

    @pl.loop(0, total)
    def _(i):
        slot = lax.rem(i, slots)
        more = i + 1 < total

        @pl.when(more)
        def _():
            fetch(i + 1).wait()
            patch(i + 1)

        pl.when(i + 2 < total)(lambda: fetch(i + 2).start())
        part = jnp.where(valid - i * BLOCK < BLOCK, 1, 0)
        weigh_and_score(0, slot, part, 1, slot)
        weigh_and_score(1, slot, part, 0, jnp.where(more, lax.rem(i + 1, slots), slot))

    for g in range(2):
        for h in range(heads):
            rows = slice(h * node_count, (h + 1) * node_count)
            weight_sum = jnp.maximum(sum_s[g][rows, HD:], 1e-30)
            result = sum_s[g][rows, :HD] / weight_sum
            lse = top_s[g][rows, :] + jnp.log2(weight_sum)
            col = h * HD
            if g == 0:
                keep_ref[:, col:col + HD] = result
                keep_lse_ref[:, col:col + HD] = lse
            else:
                send_ref[:, col:col + HD] = result
                send_ref[:, heads * HD + col:heads * HD + col + HD] = lse


def attend(info, seq, mine, other, keys, values, bias, cache):
    depth = len(keys)
    node_count, width = mine.shape
    half_rows = width // HD * node_count
    slot_count = cache.shape[1]
    vmem = pl.BlockSpec(memory_space=pltpu.VMEM)

    def pair(shape, kind):
        return [pltpu.VMEM(shape, kind)] * 2

    return pl.pallas_call(
        functools.partial(attend_kernel, depth, seq),
        out_shape=(
            jax.ShapeDtypeStruct((node_count, width), jnp.float32),
            jax.ShapeDtypeStruct((node_count, width), jnp.float32),
            jax.ShapeDtypeStruct((node_count, 2 * width), jnp.float32),
        ),
        in_specs=[pl.BlockSpec(memory_space=pltpu.SMEM)]
        + [vmem] * (3 + 2 * depth)
        + [pl.BlockSpec(memory_space=pl.ANY)],
        out_specs=(vmem, vmem, vmem),
        scratch_shapes=pair((half_rows, HD), jnp.bfloat16)
        + pair((half_rows, BLOCK), jnp.float32)
        + pair((half_rows, HD), jnp.float32)
        + pair((half_rows, HD), jnp.float32)
        + pair((half_rows, 2 * HD), jnp.float32)
        + [
            pltpu.VMEM((3, BLOCK, 2 * HD), jnp.bfloat16),
            pltpu.VMEM((2, BLOCK, HD), jnp.bfloat16),
            pltpu.SemaphoreType.DMA((3,)),
        ],
        compiler_params=pltpu.CompilerParams(vmem_limit_bytes=24 * 1024 * 1024),
        cost_estimate=pl.CostEstimate(
            flops=8 * half_rows * slot_count * HD,
            bytes_accessed=cache.size,
            transcendentals=2 * half_rows * slot_count,
        ),
        name="attend",
    )(info, mine, other, *keys, *values, bias, cache)


CORE, ACROSS, NEAR, FAR = range(4)
PIECE = 1024


def bit_of(distance):
    return lax.axis_index("tensor") // (1 << distance) % 2


def fold(x, axis, distance, kind=jnp.bfloat16):
    bit = bit_of(distance)
    keep = lax.dynamic_index_in_dim(x, bit, axis, keepdims=False)
    send = lax.dynamic_index_in_dim(x, 1 - bit, axis, keepdims=False).astype(kind)
    return keep + partner(send, "tensor", distance).astype(jnp.float32)


def column_halves(x):
    low = [x[..., c:c + PIECE] for c in range(0, x.shape[-1], 2 * PIECE)]
    high = [x[..., c + PIECE:c + 2 * PIECE] for c in range(0, x.shape[-1], 2 * PIECE)]
    return jnp.concatenate(low, axis=-1), jnp.concatenate(high, axis=-1)


def fold_columns(x, distance):
    low, high = column_halves(x)
    upper = bit_of(distance) == 1
    send = jnp.where(upper, low, high).astype(jnp.bfloat16)
    return jnp.where(upper, high, low) + partner(send, "tensor", distance).astype(jnp.float32)


def unfold(x, axis, distance):
    other = partner(x, "tensor", distance)
    upper = bit_of(distance) == 1
    return jnp.where(upper, jnp.stack([other, x], axis), jnp.stack([x, other], axis))


def unfold_columns(x, distance):
    other = partner(x, "tensor", distance)
    upper = bit_of(distance) == 1
    parts = []
    for c in range(0, x.shape[-1], PIECE):
        mine, theirs = x[..., c:c + PIECE], other[..., c:c + PIECE]
        parts += [jnp.where(upper, theirs, mine), jnp.where(upper, mine, theirs)]
    return jnp.concatenate(parts, axis=-1)


def one_way(x, distance, target):
    size = lax.axis_size("tensor")
    pairs = [(i, i ^ 1 << distance) for i in range(size) if i >> distance & 1 != target]
    return lax.ppermute(x, "tensor", pairs)


def spread_out(x, first_order):
    if first_order:
        x = fold(x, -3, ACROSS)
        x = fold(x, -3, NEAR)
        return fold_columns(x, FAR)
    x = fold(x, -4, NEAR)
    x = fold_columns(x, FAR)
    return fold(x, -3, ACROSS)


def final_sum(x, first_order, target):
    def far(part):
        return part + one_way(part.astype(jnp.bfloat16), FAR, target).astype(jnp.float32)

    if first_order:
        return far(fold(fold(x, -3, ACROSS), -3, NEAR))
    return fold(far(fold(x, -4, NEAR)), -3, ACROSS)


def collect(first, second):
    first = unfold(unfold(unfold_columns(first, FAR), -3, NEAR), -3, ACROSS)
    second = unfold(unfold_columns(unfold(second, -3, ACROSS), FAR), -4, NEAR)
    both = jnp.concatenate([first, second], axis=-1)
    both = unfold(both, -3, CORE)
    return both.reshape(-1, both.shape[-1])


def local_pairs(
    tapped, join_weight, norm_gain, query_weight, kv_weight, out_weight, kv_cache, lengths, parents
):
    side = lax.axis_index("tensor") % 2
    row_count = tapped.shape[0]
    columns = join_weight.shape[1]
    seq_count, piece_len = kv_cache.shape[:2]
    node_count = row_count // seq_count
    own_rows = node_count // 8
    half = columns // 2
    valid = jnp.clip(lengths - side * piece_len, 0, piece_len).astype(jnp.int32)
    infos = [jnp.stack([valid[b], (1 - side).astype(jnp.int32)]) for b in range(seq_count)]
    node_ids = jnp.arange(node_count, dtype=jnp.int32)
    biases = {}
    for b in range(seq_count):
        nodes = parents[:, b * node_count:(b + 1) * node_count]
        from_node = (nodes[:, :, None] == node_ids).astype(jnp.float32)
        for step in range(STEPS):
            hops = [jnp.eye(node_count, dtype=jnp.float32)]
            for earlier in range(step - 1, -1, -1):
                hops.insert(0, jnp.dot(hops[0], from_node[earlier]))
            spare = -(step + 1) * node_count % HD
            hops.append(jnp.zeros((node_count, spare), jnp.float32))
            biases[b, step] = (jnp.concatenate(hops, axis=1) - 1.0) * -floor_score

    pieces = []
    for c in range(0, columns, 2 * PIECE):
        partial = jnp.dot(
            tapped, join_weight[:, c:c + 2 * PIECE], preferred_element_type=jnp.float32
        )
        parts = partial.reshape(seq_count, 2, 2, 2, own_rows, 2 * PIECE)
        pieces.append(spread_out(fold(parts, -3, CORE, jnp.float32), c < half))
    count = len(pieces) // 2
    hidden = {}
    for b in range(seq_count):
        hidden[b, 0] = jnp.concatenate([piece[b] for piece in pieces[:count]], axis=-1)
        hidden[b, 1] = jnp.concatenate([piece[b] for piece in pieces[count:]], axis=-1)
    far_upper = bit_of(FAR) == 1
    gains = [jnp.where(far_upper, *column_halves(norm_gain[c:c + half])[::-1]) for c in (0, half)]
    unscale = 1.0 / norm_gain

    keys = {b: [] for b in range(seq_count)}
    values = {b: [] for b in range(seq_count)}
    results = {}
    for step in range(STEPS):
        last = step == STEPS - 1
        for b in range(seq_count):
            gained = collect(*[(hidden[b, i] * gains[i]).astype(jnp.bfloat16) for i in range(2)])
            plain = gained.astype(jnp.float32) * unscale
            scale = lax.rsqrt(jnp.mean(plain * plain, axis=-1, keepdims=True) + epsilon)
            new_kv = jnp.dot(gained, kv_weight, preferred_element_type=jnp.float32) * scale
            new_kv = new_kv.astype(jnp.bfloat16)
            query = jnp.dot(gained, query_weight, preferred_element_type=jnp.float32) * scale
            query = query.astype(jnp.bfloat16)
            keys[b].append(new_kv)
            values[b].append(partner(new_kv, "tensor", CORE))
            kept, kept_lse, sent = attend(
                infos[b], b, query, partner(query, "tensor", CORE),
                keys[b], values[b], biases[b, step], kv_cache,
            )
            came = partner(sent, "tensor", CORE)
            width = kept.shape[1]
            top = jnp.maximum(kept_lse, came[:, width:])
            mine = jnp.exp2(kept_lse - top)
            theirs = jnp.exp2(came[:, width:] - top)
            attended = (mine * kept + theirs * came[:, :width]) / (mine + theirs)
            update = jnp.dot(
                attended.astype(jnp.bfloat16), out_weight, preferred_element_type=jnp.float32
            )
            parts = fold(update.reshape(2, 2, 2, own_rows, columns), -3, CORE, jnp.float32)
            first, second = parts[..., :half], parts[..., half:]
            if not last:
                hidden[b, 0] = hidden[b, 0] + spread_out(first, True)
                hidden[b, 1] = hidden[b, 1] + spread_out(second, False)
                continue
            before = jnp.concatenate(
                [unfold_columns(hidden[b, i], FAR) for i in range(2)], axis=-1
            )
            after = jnp.concatenate(
                [final_sum(first, True, b), final_sum(second, False, b)], axis=-1
            )
            results[b] = before + after
    return jnp.where(far_upper, results[1], results[0])


def solution(mesh):
    body = local_pairs if mesh.shape["tensor"] == 2 * KVH else local_general
    placed = (
        P("groups", "tensor"),
        P("tensor", None),
        P(),
        P(None, "tensor"),
        P(None, "tensor"),
        P("tensor", None),
        P("groups", "tensor", None),
        P("groups"),
        P(None, "groups"),
    )
    return jax.shard_map(
        body, mesh=mesh, in_specs=placed, out_specs=P(("groups", "tensor"), None), check_vma=False
    )
```

```python
import functools
import math

import jax
import jax.numpy as jnp
from jax import lax
from jax.experimental import pallas as pl
from jax.experimental.pallas import tpu as pltpu
from jax.sharding import PartitionSpec as P

KVH = 8
HD = 128
QPK = 8
STEPS = 3


epsilon = 1e-05
floor_score = -1e30


def partner(x, axis, distance):
    return lax.ppermute(x, axis, [(i, i ^ 1 << distance) for i in range(lax.axis_size(axis))])


def as_sent(x):

    def short(part):
        return part.astype(jnp.bfloat16) if part.dtype == jnp.float32 else part

    return jax.tree.map(short, x)


def normalize(values, norm_gain):
    mean_square = jnp.mean(values * values, axis=-1, keepdims=True)
    return (values * lax.rsqrt(mean_square + epsilon) * norm_gain).astype(jnp.bfloat16)


def merge_parts(mine, theirs):
    row_top = jnp.maximum(mine[0], theirs[0])
    mine_factor = jnp.exp(mine[0] - row_top)
    their_factor = jnp.exp(theirs[0] - row_top)
    row_sum = mine_factor * mine[1] + their_factor * theirs[1]
    numerator = mine_factor[..., None] * mine[2] + their_factor[..., None] * theirs[2]
    return (row_top, row_sum, numerator)


def local_general(
    tapped, join_weight, norm_gain, query_weight, kv_weight, out_weight, kv_cache, lengths, parents
):
    tensor_size = lax.axis_size("tensor")
    device = lax.axis_index("tensor")
    group_size = tensor_size // KVH
    hop_count = group_size.bit_length() - 1
    piece_index = device % group_size
    row_count_all = tapped.shape[0]
    seq_count = kv_cache.shape[0]
    node_count = row_count_all // seq_count
    query_cols = query_weight.shape[1]
    proj_weight = jnp.concatenate([query_weight, kv_weight], axis=1)
    score_scale = 1.0 / math.sqrt(HD)
    hidden_rows = lax.psum_scatter(
        jnp.dot(tapped, join_weight, preferred_element_type=jnp.float32),
        "tensor",
        scatter_dimension=0,
        tiled=True,
    )
    piece_len = kv_cache.shape[1]
    positions = piece_index * piece_len + jnp.arange(piece_len, dtype=jnp.int32)
    visible = positions[None, :] < lengths[:, None]
    is_first = piece_index == 0
    keys_cache = kv_cache[:, :, :HD]
    values_cache = kv_cache[:, :, HD:]
    row_ids = jnp.arange(row_count_all, dtype=jnp.int32)
    seq_base = row_ids // node_count * node_count
    head_rows = node_count * QPK
    width = out_weight.shape[0]
    history = []
    for step_num in range(STEPS):
        projected = jnp.dot(
            lax.all_gather(normalize(hidden_rows, norm_gain), "tensor", axis=0, tiled=True),
            proj_weight,
            preferred_element_type=jnp.float32,
        ).astype(jnp.bfloat16)
        query_group = projected[:, :query_cols]
        kv_group = projected[:, query_cols:]
        for bit_num in range(hop_count):
            other_query, other_kv = partner((query_group, kv_group), "tensor", bit_num)
            is_upper = device // (1 << bit_num) % 2 == 1
            query_group = jnp.where(
                is_upper,
                jnp.concatenate([other_query, query_group], axis=1),
                jnp.concatenate([query_group, other_query], axis=1),
            )
            kv_group = jnp.where(
                is_upper,
                jnp.concatenate([other_kv, kv_group], axis=1),
                jnp.concatenate([kv_group, other_kv], axis=1),
            )
        history.append(kv_group)
        ancestors = [row_ids]
        current = row_ids
        for earlier in range(step_num - 1, -1, -1):
            current = seq_base + jnp.take(parents[earlier], current, axis=0)
            ancestors.insert(0, current)
        new_depth = step_num + 1
        new_kv = jnp.stack(
            [
                jnp.take(history[earlier], ancestors[earlier], axis=0)
                for earlier in range(new_depth)
            ],
            axis=1,
        )
        new_keys = new_kv[..., :HD].reshape(seq_count, node_count, new_depth, HD)
        new_values = new_kv[..., HD:].reshape(seq_count, node_count, new_depth, HD)
        query_blocks = query_group.reshape(seq_count, head_rows, HD)
        scores = (
            jnp.einsum("brd,bcd->brc", query_blocks, keys_cache, preferred_element_type=jnp.float32)
            * score_scale
        )
        scores = jnp.where(visible[:, None, :], scores, floor_score)
        query_nodes = query_group.reshape(seq_count, node_count, QPK, HD)
        new_scores = (
            jnp.einsum("bnqd,bntd->bnqt", query_nodes, new_keys, preferred_element_type=jnp.float32)
            * score_scale
        )
        new_scores = jnp.where(is_first, new_scores, floor_score)
        row_top = jnp.maximum(
            jnp.max(scores, axis=-1), jnp.max(new_scores, axis=-1).reshape(seq_count, head_rows)
        )
        weights = jnp.where(visible[:, None, :], jnp.exp(scores - row_top[..., None]), 0.0)
        top_nodes = row_top.reshape(seq_count, node_count, QPK)
        new_weights = jnp.where(is_first, jnp.exp(new_scores - top_nodes[..., None]), 0.0)
        row_sum = jnp.sum(weights, axis=-1) + jnp.sum(new_weights, axis=-1).reshape(
            seq_count, head_rows
        )
        numerator = jnp.einsum(
            "brc,bcd->brd",
            weights.astype(jnp.bfloat16),
            values_cache,
            preferred_element_type=jnp.float32,
        )
        new_part = jnp.einsum(
            "bnqt,bntd->bnqd",
            new_weights.astype(jnp.bfloat16),
            new_values,
            preferred_element_type=jnp.float32,
        )
        numerator = numerator + new_part.reshape(seq_count, head_rows, HD)
        partial_value = (row_top, row_sum, numerator)
        for bit_num in range(hop_count):
            theirs = partner(
                (as_sent(partial_value[0]), as_sent(partial_value[1]), as_sent(partial_value[2])),
                "tensor",
                bit_num,
            )
            partial_value = merge_parts(partial_value, theirs)
        attended = (
            (partial_value[2] / partial_value[1][..., None])
            .astype(jnp.bfloat16)
            .reshape(row_count_all, QPK * HD)
        )
        attended_mine = lax.dynamic_slice_in_dim(attended, piece_index * width, width, 1)
        hidden_rows = hidden_rows + lax.psum_scatter(
            jnp.dot(attended_mine, out_weight, preferred_element_type=jnp.float32),
            "tensor",
            scatter_dimension=0,
            tiled=True,
        )
    return hidden_rows


BLOCK = 2048
SUB = BLOCK // 2
CHUNK = 256
TO_LOG2 = math.log2(math.e) / math.sqrt(HD)


def score_dot(query, key):
    return lax.dot_general(
        query, key, (((1,), (1,)), ((), ())), preferred_element_type=jnp.float32
    )


def wide(x, width):
    return jnp.concatenate([x] * (width // HD), axis=1)


def attend_kernel(depth, info_ref, mine_ref, other_ref, *refs):
    key_refs, value_refs, bias_refs = refs[:depth], refs[depth:2 * depth], refs[2 * depth:3 * depth]
    cache_ref, keep_ref, keep_lse_ref, send_ref, query_s = refs[3 * depth:3 * depth + 5]
    score_s, weight_s = refs[3 * depth + 5:3 * depth + 7], refs[3 * depth + 7:3 * depth + 9]
    top_s, sum_s, cache_s, live_s, sems = refs[3 * depth + 9:]
    seq_count = cache_ref.shape[0]
    node_count = mine_ref.shape[0] // seq_count
    half_heads = mine_ref.shape[1] // HD
    seq_rows = 2 * half_heads * node_count
    half_rows = seq_rows // 2
    slots = cache_s.shape[0]
    steps = [lax.div(info_ref[b] + BLOCK - 1, BLOCK) for b in range(seq_count)]
    total = sum(steps)

    def place(i):
        seq = jnp.int32(0)
        block = i
        for b in range(seq_count - 1):
            later = jnp.logical_and(block >= steps[b], seq == b)
            seq = jnp.where(later, b + 1, seq)
            block = jnp.where(later, block - steps[b], block)
        return seq, block

    def left_of(i):
        seq, block = place(i)
        return info_ref[seq] - block * BLOCK

    def fetch(i):
        seq, block = place(i)
        slot = lax.rem(i, slots)
        start = pl.multiple_of(block * BLOCK, BLOCK)
        return pltpu.make_async_copy(
            cache_ref.at[seq, pl.ds(start, BLOCK), :], cache_s.at[slot], sems.at[slot]
        )

    for i in range(2):
        pl.when(i < total)(lambda i=i: fetch(jnp.int32(i)).start())

    for b in range(seq_count):
        rows = slice(b * node_count, (b + 1) * node_count)
        for h in range(2 * half_heads):
            ref = mine_ref if h < half_heads else other_ref
            col = h % half_heads * HD
            row = b * seq_rows + h * node_count
            query_s[row:row + node_count, :] = ref[rows, col:col + HD]
    live_s[0] = jnp.ones((BLOCK, HD), jnp.bfloat16)

    @pl.when(info_ref[seq_count] == 0)
    def _():
        top_s[...] = jnp.full(top_s.shape, floor_score, jnp.float32)
        sum_s[...] = jnp.zeros(sum_s.shape, jnp.float32)

    @pl.when(info_ref[seq_count] != 0)
    def _():
        for b in range(seq_count):
            rows = slice(b * seq_rows, (b + 1) * seq_rows)
            query = query_s[rows, :]
            scores = []
            for t in range(depth):
                bias = bias_refs[t][b * node_count:(b + 1) * node_count, :]
                score = score_dot(query, key_refs[t][...])
                scores.append(score * TO_LOG2 + jnp.concatenate([bias] * (2 * half_heads), axis=0))
            top = functools.reduce(jnp.maximum, scores)
            top = jnp.broadcast_to(jnp.max(top, axis=1, keepdims=True), top.shape)
            gathered = jnp.zeros((seq_rows, 2 * HD), jnp.float32)
            for t in range(depth):
                weight = jnp.exp2(scores[t] - top).astype(jnp.bfloat16)
                value = value_refs[t][...]
                value = jnp.concatenate([value, jnp.ones_like(value)], axis=1)
                gathered = gathered + jnp.dot(weight, value, preferred_element_type=jnp.float32)
            top_s[rows, :] = top
            sum_s[rows, :] = gathered

    def patch(i):
        left = left_of(i)
        slot = lax.rem(i, slots)

        @pl.when(left < BLOCK)
        def _():
            inside = lax.broadcasted_iota(jnp.int32, (BLOCK, HD), 0) < left
            key = cache_s[slot, :, :HD].astype(jnp.float32)
            value = cache_s[slot, :, HD:].astype(jnp.float32)
            key = jnp.where(inside, key, jnp.broadcast_to(key[:1, :], key.shape))
            cache_s[slot, :, :HD] = key.astype(jnp.bfloat16)
            cache_s[slot, :, HD:] = jnp.where(inside, value, 0.0).astype(jnp.bfloat16)

    def score_chunk(seq, slot, sub, c):
        rows = pl.ds(pl.multiple_of(seq * seq_rows, seq_rows), seq_rows)
        at = sub * SUB + c
        score_s[sub][:, c:c + CHUNK] = score_dot(query_s[rows, :], cache_s[slot, at:at + CHUNK, :HD])

    def weigh(seq, slot, part, sub, half, between):
        rows = pl.ds(pl.multiple_of(seq * seq_rows + half * half_rows, half_rows), half_rows)
        here = slice(half * half_rows, (half + 1) * half_rows)
        high = score_s[sub][here, :HD]
        for c in range(HD, SUB, HD):
            high = jnp.maximum(high, score_s[sub][here, c:c + HD])
        high = jnp.broadcast_to(jnp.max(high, axis=1, keepdims=True), high.shape) * TO_LOG2
        old = top_s[rows, :]
        top = jnp.maximum(old, high)
        top_s[rows, :] = top
        factor = jnp.exp2(old - top)
        between[0]()
        tops = wide(top, CHUNK)
        for c in range(0, SUB, CHUNK):
            weight = jnp.exp2(score_s[sub][here, c:c + CHUNK] * TO_LOG2 - tops)
            weight_s[sub][here, c:c + CHUNK] = weight.astype(jnp.bfloat16)
            if c == SUB // 2:
                between[1]()
        keys = slice(sub * SUB, (sub + 1) * SUB)
        value = jnp.concatenate([cache_s[slot, keys, HD:], live_s[part, keys, :]], axis=1)
        sum_s[rows, :] = sum_s[rows, :] * wide(factor, 2 * HD) + jnp.dot(
            weight_s[sub][here, :], value, preferred_element_type=jnp.float32
        )

    def phase(seq, slot, part, sub, next_seq, next_slot):
        ahead = [
            functools.partial(score_chunk, next_seq, next_slot, 1 - sub, c)
            for c in range(0, SUB, CHUNK)
        ]
        weigh(seq, slot, part, sub, 0, ahead[:2])
        weigh(seq, slot, part, sub, 1, ahead[2:])

    @pl.when(total > 0)
    def _():
        fetch(jnp.int32(0)).wait()
        patch(jnp.int32(0))
        seq, _ = place(jnp.int32(0))
        for c in range(0, SUB, CHUNK):
            score_chunk(seq, 0, 0, c)

    @pl.loop(0, total)
    def _(i):
        slot = lax.rem(i, slots)
        more = i + 1 < total

        @pl.when(more)
        def _():
            fetch(i + 1).wait()
            patch(i + 1)

        pl.when(i + 2 < total)(lambda: fetch(i + 2).start())
        seq, _ = place(i)
        left = left_of(i)
        part = jnp.where(left < BLOCK, 1, 0)

        @pl.when(left < BLOCK)
        def _():
            inside = lax.broadcasted_iota(jnp.int32, (BLOCK, HD), 0) < left
            live_s[1] = jnp.where(inside, 1.0, 0.0).astype(jnp.bfloat16)

        next_slot = jnp.where(more, lax.rem(i + 1, slots), slot)
        next_seq, _ = place(jnp.where(more, i + 1, i))
        phase(seq, slot, part, 0, seq, slot)
        phase(seq, slot, part, 1, next_seq, next_slot)

    for b in range(seq_count):
        rows = slice(b * node_count, (b + 1) * node_count)
        for h in range(2 * half_heads):
            row = b * seq_rows + h * node_count
            weight_sum = jnp.maximum(sum_s[row:row + node_count, HD:], 1e-30)
            result = sum_s[row:row + node_count, :HD] / weight_sum
            lse = top_s[row:row + node_count, :] + jnp.log2(weight_sum)
            col = h % half_heads * HD
            if h < half_heads:
                keep_ref[rows, col:col + HD] = result
                keep_lse_ref[rows, col:col + HD] = lse
            else:
                send_ref[rows, col:col + HD] = result
                send_ref[rows, half_heads * HD + col:half_heads * HD + col + HD] = lse


def attend(info, mine, other, keys, values, biases, cache):
    depth = len(keys)
    row_count, width = mine.shape
    seq_count, slot_count = cache.shape[:2]
    all_rows = 2 * width // HD * row_count
    seq_rows = all_rows // seq_count
    vmem = pl.BlockSpec(memory_space=pltpu.VMEM)
    return pl.pallas_call(
        functools.partial(attend_kernel, depth),
        out_shape=(
            jax.ShapeDtypeStruct((row_count, width), jnp.float32),
            jax.ShapeDtypeStruct((row_count, width), jnp.float32),
            jax.ShapeDtypeStruct((row_count, 2 * width), jnp.float32),
        ),
        in_specs=[pl.BlockSpec(memory_space=pltpu.SMEM)]
        + [vmem] * (2 + 3 * depth)
        + [pl.BlockSpec(memory_space=pltpu.HBM)],
        out_specs=(vmem, vmem, vmem),
        scratch_shapes=[
            pltpu.VMEM((all_rows, HD), jnp.bfloat16),
            pltpu.VMEM((seq_rows, SUB), jnp.float32),
            pltpu.VMEM((seq_rows, SUB), jnp.float32),
            pltpu.VMEM((seq_rows, SUB), jnp.bfloat16),
            pltpu.VMEM((seq_rows, SUB), jnp.bfloat16),
            pltpu.VMEM((all_rows, HD), jnp.float32),
            pltpu.VMEM((all_rows, 2 * HD), jnp.float32),
            pltpu.VMEM((3, BLOCK, 2 * HD), jnp.bfloat16),
            pltpu.VMEM((2, BLOCK, HD), jnp.bfloat16),
            pltpu.SemaphoreType.DMA((3,)),
        ],
        compiler_params=pltpu.CompilerParams(vmem_limit_bytes=32 * 1024 * 1024),
        cost_estimate=pl.CostEstimate(
            flops=4 * all_rows * slot_count * HD,
            bytes_accessed=2 * cache.size,
            transcendentals=all_rows * slot_count,
        ),
        name="attend",
    )(info, mine, other, *keys, *values, *biases, cache)


JOIN_COLUMNS = 512


def join_kernel(side_ref, x_ref, weight_ref, keep_ref, send_ref, product_s):
    side = side_ref[0]
    own = 8
    product_s[...] = jnp.dot(x_ref[...], weight_ref[...], preferred_element_type=jnp.float32)
    for block in range(keep_ref.shape[0] // own):
        rows = slice(block * own, (block + 1) * own)
        keep_at = pl.multiple_of(2 * block * own + side * own, own)
        send_at = pl.multiple_of(2 * block * own + (1 - side) * own, own)
        keep_ref[rows, :] = product_s[pl.ds(keep_at, own), :]
        send_ref[rows, :] = product_s[pl.ds(send_at, own), :]


def join(side, x, weight, start, columns):
    rows, depth = x.shape
    first = start // JOIN_COLUMNS
    out = jax.ShapeDtypeStruct((rows // 2, columns), jnp.float32)
    out_spec = pl.BlockSpec((rows // 2, JOIN_COLUMNS), lambda i: (0, i))
    return pl.pallas_call(
        join_kernel,
        out_shape=(out, out),
        grid=(columns // JOIN_COLUMNS,),
        in_specs=[
            pl.BlockSpec(memory_space=pltpu.SMEM),
            pl.BlockSpec((rows, depth), lambda i: (0, 0)),
            pl.BlockSpec((depth, JOIN_COLUMNS), lambda i: (0, first + i)),
        ],
        out_specs=(out_spec, out_spec),
        scratch_shapes=[pltpu.VMEM((rows, JOIN_COLUMNS), jnp.float32)],
        compiler_params=pltpu.CompilerParams(vmem_limit_bytes=24 * 1024 * 1024),
        cost_estimate=pl.CostEstimate(
            flops=2 * rows * depth * columns, bytes_accessed=2 * depth * columns, transcendentals=0
        ),
        name="join",
    )(side[None], x, weight)


CORE, ACROSS, NEAR, FAR = range(4)


def bit_of(distance):
    return lax.axis_index("tensor") // (1 << distance) % 2


def fold(x, axis, distance, kind=jnp.bfloat16):
    bit = bit_of(distance)
    keep = lax.dynamic_index_in_dim(x, bit, axis, keepdims=False)
    send = lax.dynamic_index_in_dim(x, 1 - bit, axis, keepdims=False).astype(kind)
    return keep + partner(send, "tensor", distance).astype(jnp.float32)


def unfold(x, axis, distance):
    other = partner(x, "tensor", distance)
    upper = bit_of(distance) == 1
    return jnp.where(upper, jnp.stack([other, x], axis), jnp.stack([x, other], axis))


def sum_chips(first, second):
    first = fold(fold(fold(first, -3, ACROSS), -3, NEAR), -3, FAR)
    second = fold(fold(fold(second, -4, NEAR), -4, FAR), -3, ACROSS)
    return jnp.concatenate([first, second], axis=-1)


def collect(rows):
    half = rows.shape[1] // 2
    first, second = rows[:, :half], rows[:, half:]
    first = unfold(unfold(unfold(first, -3, FAR), -3, NEAR), -3, ACROSS)
    second = unfold(unfold(unfold(second, -3, ACROSS), -4, FAR), -4, NEAR)
    both = unfold(jnp.concatenate([first, second], axis=-1), -3, CORE)
    return both.reshape(-1, both.shape[-1])


def local_pairs(
    tapped, join_weight, norm_gain, query_weight, kv_weight, out_weight, kv_cache, lengths, parents
):
    side = (lax.axis_index("tensor") % 2).astype(jnp.int32)
    row_count = tapped.shape[0]
    columns = join_weight.shape[1]
    half = columns // 2
    seq_count, piece_len = kv_cache.shape[:2]
    node_count = row_count // seq_count
    own_rows = row_count // 16
    row_ids = jnp.arange(row_count, dtype=jnp.int32)
    valid = jnp.clip(lengths - side * piece_len, 0, piece_len)
    info = jnp.concatenate([valid, (1 - side)[None]]).astype(jnp.int32)
    parent_rows = row_ids // node_count * node_count + parents
    from_row = (parent_rows[:, :, None] == row_ids).astype(jnp.float32)
    hops = {}
    for step in range(STEPS):
        hops[step, step] = jnp.eye(row_count, dtype=jnp.float32)
        for earlier in range(step - 1, -1, -1):
            hops[step, earlier] = jnp.dot(hops[step, earlier + 1], from_row[earlier])
    bias = {at: (hop - 1.0) * -floor_score for at, hop in hops.items()}

    folded = []
    for start in (0, half):
        kept, sent = join(side, tapped, join_weight, start, half)
        part = kept + partner(sent, "tensor", CORE)
        folded.append(part.reshape(2, 2, 2, own_rows, half))
    hidden = sum_chips(*folded)

    keys, values = [], []
    for step in range(STEPS):
        normed = collect(normalize(hidden, norm_gain))
        new_kv = jnp.dot(normed, kv_weight, preferred_element_type=jnp.float32)
        new_kv = new_kv.astype(jnp.bfloat16)
        query = jnp.dot(normed, query_weight, preferred_element_type=jnp.float32)
        query = query.astype(jnp.bfloat16)
        keys.append(new_kv)
        values.append(partner(new_kv, "tensor", CORE))
        kept, kept_lse, sent = attend(
            info, query, partner(query, "tensor", CORE), keys, values,
            [bias[step, t] for t in range(step + 1)], kv_cache,
        )
        came = partner(sent, "tensor", CORE)
        width = kept.shape[1]
        top = jnp.maximum(kept_lse, came[:, width:])
        mine = jnp.exp2(kept_lse - top)
        theirs = jnp.exp2(came[:, width:] - top)
        attended = (mine * kept + theirs * came[:, :width]) / (mine + theirs)
        update = jnp.dot(
            attended.astype(jnp.bfloat16), out_weight, preferred_element_type=jnp.float32
        ).reshape(2, 2, 2, 2, own_rows, columns)
        hidden = hidden + sum_chips(*[
            fold(update[..., start:start + half], -3, CORE, jnp.float32) for start in (0, half)
        ])
    return hidden


def solution(mesh):
    body = local_pairs if mesh.shape["tensor"] == 2 * KVH else local_general
    placed = (
        P("groups", "tensor"),
        P("tensor", None),
        P(),
        P(None, "tensor"),
        P(None, "tensor"),
        P("tensor", None),
        P("groups", "tensor", None),
        P("groups"),
        P(None, "groups"),
    )
    return jax.shard_map(
        body, mesh=mesh, in_specs=placed, out_specs=P(("groups", "tensor"), None), check_vma=False
    )
```

```python
import functools
import math

import jax
import jax.numpy as jnp
from jax import lax
from jax.experimental import pallas as pl
from jax.experimental.pallas import tpu as pltpu
from jax.sharding import PartitionSpec as P

KVH = 8
HD = 128
QPK = 8
STEPS = 3


epsilon = 1e-05
floor_score = -1e30


def partner(x, axis, distance):
    return lax.ppermute(x, axis, [(i, i ^ 1 << distance) for i in range(lax.axis_size(axis))])


def as_sent(x):

    def short(part):
        return part.astype(jnp.bfloat16) if part.dtype == jnp.float32 else part

    return jax.tree.map(short, x)


def normalize(values, norm_gain):
    mean_square = jnp.mean(values * values, axis=-1, keepdims=True)
    return (values * lax.rsqrt(mean_square + epsilon) * norm_gain).astype(jnp.bfloat16)


def merge_parts(mine, theirs):
    row_top = jnp.maximum(mine[0], theirs[0])
    mine_factor = jnp.exp(mine[0] - row_top)
    their_factor = jnp.exp(theirs[0] - row_top)
    row_sum = mine_factor * mine[1] + their_factor * theirs[1]
    numerator = mine_factor[..., None] * mine[2] + their_factor[..., None] * theirs[2]
    return (row_top, row_sum, numerator)


def local_general(
    tapped, join_weight, norm_gain, query_weight, kv_weight, out_weight, kv_cache, lengths, parents
):
    tensor_size = lax.axis_size("tensor")
    device = lax.axis_index("tensor")
    group_size = tensor_size // KVH
    hop_count = group_size.bit_length() - 1
    piece_index = device % group_size
    row_count_all = tapped.shape[0]
    seq_count = kv_cache.shape[0]
    node_count = row_count_all // seq_count
    query_cols = query_weight.shape[1]
    proj_weight = jnp.concatenate([query_weight, kv_weight], axis=1)
    score_scale = 1.0 / math.sqrt(HD)
    hidden_rows = lax.psum_scatter(
        jnp.dot(tapped, join_weight, preferred_element_type=jnp.float32),
        "tensor",
        scatter_dimension=0,
        tiled=True,
    )
    piece_len = kv_cache.shape[1]
    positions = piece_index * piece_len + jnp.arange(piece_len, dtype=jnp.int32)
    visible = positions[None, :] < lengths[:, None]
    is_first = piece_index == 0
    keys_cache = kv_cache[:, :, :HD]
    values_cache = kv_cache[:, :, HD:]
    row_ids = jnp.arange(row_count_all, dtype=jnp.int32)
    seq_base = row_ids // node_count * node_count
    head_rows = node_count * QPK
    width = out_weight.shape[0]
    history = []
    for step_num in range(STEPS):
        projected = jnp.dot(
            lax.all_gather(normalize(hidden_rows, norm_gain), "tensor", axis=0, tiled=True),
            proj_weight,
            preferred_element_type=jnp.float32,
        ).astype(jnp.bfloat16)
        query_group = projected[:, :query_cols]
        kv_group = projected[:, query_cols:]
        for bit_num in range(hop_count):
            other_query, other_kv = partner((query_group, kv_group), "tensor", bit_num)
            is_upper = device // (1 << bit_num) % 2 == 1
            query_group = jnp.where(
                is_upper,
                jnp.concatenate([other_query, query_group], axis=1),
                jnp.concatenate([query_group, other_query], axis=1),
            )
            kv_group = jnp.where(
                is_upper,
                jnp.concatenate([other_kv, kv_group], axis=1),
                jnp.concatenate([kv_group, other_kv], axis=1),
            )
        history.append(kv_group)
        ancestors = [row_ids]
        current = row_ids
        for earlier in range(step_num - 1, -1, -1):
            current = seq_base + jnp.take(parents[earlier], current, axis=0)
            ancestors.insert(0, current)
        new_depth = step_num + 1
        new_kv = jnp.stack(
            [
                jnp.take(history[earlier], ancestors[earlier], axis=0)
                for earlier in range(new_depth)
            ],
            axis=1,
        )
        new_keys = new_kv[..., :HD].reshape(seq_count, node_count, new_depth, HD)
        new_values = new_kv[..., HD:].reshape(seq_count, node_count, new_depth, HD)
        query_blocks = query_group.reshape(seq_count, head_rows, HD)
        scores = (
            jnp.einsum("brd,bcd->brc", query_blocks, keys_cache, preferred_element_type=jnp.float32)
            * score_scale
        )
        scores = jnp.where(visible[:, None, :], scores, floor_score)
        query_nodes = query_group.reshape(seq_count, node_count, QPK, HD)
        new_scores = (
            jnp.einsum("bnqd,bntd->bnqt", query_nodes, new_keys, preferred_element_type=jnp.float32)
            * score_scale
        )
        new_scores = jnp.where(is_first, new_scores, floor_score)
        row_top = jnp.maximum(
            jnp.max(scores, axis=-1), jnp.max(new_scores, axis=-1).reshape(seq_count, head_rows)
        )
        weights = jnp.where(visible[:, None, :], jnp.exp(scores - row_top[..., None]), 0.0)
        top_nodes = row_top.reshape(seq_count, node_count, QPK)
        new_weights = jnp.where(is_first, jnp.exp(new_scores - top_nodes[..., None]), 0.0)
        row_sum = jnp.sum(weights, axis=-1) + jnp.sum(new_weights, axis=-1).reshape(
            seq_count, head_rows
        )
        numerator = jnp.einsum(
            "brc,bcd->brd",
            weights.astype(jnp.bfloat16),
            values_cache,
            preferred_element_type=jnp.float32,
        )
        new_part = jnp.einsum(
            "bnqt,bntd->bnqd",
            new_weights.astype(jnp.bfloat16),
            new_values,
            preferred_element_type=jnp.float32,
        )
        numerator = numerator + new_part.reshape(seq_count, head_rows, HD)
        partial_value = (row_top, row_sum, numerator)
        for bit_num in range(hop_count):
            theirs = partner(
                (as_sent(partial_value[0]), as_sent(partial_value[1]), as_sent(partial_value[2])),
                "tensor",
                bit_num,
            )
            partial_value = merge_parts(partial_value, theirs)
        attended = (
            (partial_value[2] / partial_value[1][..., None])
            .astype(jnp.bfloat16)
            .reshape(row_count_all, QPK * HD)
        )
        attended_mine = lax.dynamic_slice_in_dim(attended, piece_index * width, width, 1)
        hidden_rows = hidden_rows + lax.psum_scatter(
            jnp.dot(attended_mine, out_weight, preferred_element_type=jnp.float32),
            "tensor",
            scatter_dimension=0,
            tiled=True,
        )
    return hidden_rows


BLOCK = 2048
SUB = BLOCK // 2
CHUNK = 256
TO_LOG2 = math.log2(math.e) / math.sqrt(HD)


def score_dot(query, key):
    return lax.dot_general(
        query, key, (((1,), (1,)), ((), ())), preferred_element_type=jnp.float32
    )


def wide(x, width):
    return jnp.concatenate([x] * (width // HD), axis=1)


def attend_kernel(depth, info_ref, mine_ref, other_ref, *refs):
    key_refs, value_refs, bias_refs = refs[:depth], refs[depth:2 * depth], refs[2 * depth:3 * depth]
    cache_ref, keep_ref, keep_lse_ref, send_ref, query_s = refs[3 * depth:3 * depth + 5]
    score_s, weight_s = refs[3 * depth + 5:3 * depth + 7], refs[3 * depth + 7:3 * depth + 9]
    top_s, sum_s, cache_s, live_s, sems = refs[3 * depth + 9:]
    seq_count = cache_ref.shape[0]
    node_count = mine_ref.shape[0] // seq_count
    half_heads = mine_ref.shape[1] // HD
    seq_rows = 2 * half_heads * node_count
    half_rows = seq_rows // 2
    slots = cache_s.shape[0]
    steps = [lax.div(info_ref[b] + BLOCK - 1, BLOCK) for b in range(seq_count)]
    total = sum(steps)

    def place(i):
        seq = jnp.int32(0)
        block = i
        for b in range(seq_count - 1):
            later = jnp.logical_and(block >= steps[b], seq == b)
            seq = jnp.where(later, b + 1, seq)
            block = jnp.where(later, block - steps[b], block)
        return seq, block

    def left_of(i):
        seq, block = place(i)
        return info_ref[seq] - block * BLOCK

    def fetch(i):
        seq, block = place(i)
        slot = lax.rem(i, slots)
        start = pl.multiple_of(block * BLOCK, BLOCK)
        return pltpu.make_async_copy(
            cache_ref.at[seq, pl.ds(start, BLOCK), :], cache_s.at[slot], sems.at[slot]
        )

    for i in range(2):
        pl.when(i < total)(lambda i=i: fetch(jnp.int32(i)).start())

    for b in range(seq_count):
        rows = slice(b * node_count, (b + 1) * node_count)
        for h in range(2 * half_heads):
            ref = mine_ref if h < half_heads else other_ref
            col = h % half_heads * HD
            row = b * seq_rows + h * node_count
            query_s[row:row + node_count, :] = ref[rows, col:col + HD]
    live_s[0] = jnp.ones((BLOCK, HD), jnp.bfloat16)

    @pl.when(info_ref[seq_count] == 0)
    def _():
        top_s[...] = jnp.full(top_s.shape, floor_score, jnp.float32)
        sum_s[...] = jnp.zeros(sum_s.shape, jnp.float32)

    @pl.when(info_ref[seq_count] != 0)
    def _():
        for b in range(seq_count):
            rows = slice(b * seq_rows, (b + 1) * seq_rows)
            query = query_s[rows, :]
            scores = []
            for t in range(depth):
                bias = bias_refs[t][b * node_count:(b + 1) * node_count, :]
                score = score_dot(query, key_refs[t][...])
                scores.append(score * TO_LOG2 + jnp.concatenate([bias] * (2 * half_heads), axis=0))
            top = functools.reduce(jnp.maximum, scores)
            top = jnp.broadcast_to(jnp.max(top, axis=1, keepdims=True), top.shape)
            gathered = jnp.zeros((seq_rows, 2 * HD), jnp.float32)
            for t in range(depth):
                weight = jnp.exp2(scores[t] - top).astype(jnp.bfloat16)
                value = value_refs[t][...]
                value = jnp.concatenate([value, jnp.ones_like(value)], axis=1)
                gathered = gathered + jnp.dot(weight, value, preferred_element_type=jnp.float32)
            top_s[rows, :] = top
            sum_s[rows, :] = gathered

    def patch(i):
        left = left_of(i)
        slot = lax.rem(i, slots)

        @pl.when(left < BLOCK)
        def _():
            inside = lax.broadcasted_iota(jnp.int32, (BLOCK, HD), 0) < left
            key = cache_s[slot, :, :HD].astype(jnp.float32)
            value = cache_s[slot, :, HD:].astype(jnp.float32)
            key = jnp.where(inside, key, jnp.broadcast_to(key[:1, :], key.shape))
            cache_s[slot, :, :HD] = key.astype(jnp.bfloat16)
            cache_s[slot, :, HD:] = jnp.where(inside, value, 0.0).astype(jnp.bfloat16)

    def score_chunk(seq, slot, sub, c):
        rows = pl.ds(pl.multiple_of(seq * seq_rows, seq_rows), seq_rows)
        at = sub * SUB + c
        score_s[sub][:, c:c + CHUNK] = score_dot(query_s[rows, :], cache_s[slot, at:at + CHUNK, :HD])

    def weigh(seq, slot, part, sub, half, between):
        rows = pl.ds(pl.multiple_of(seq * seq_rows + half * half_rows, half_rows), half_rows)
        here = slice(half * half_rows, (half + 1) * half_rows)
        high = score_s[sub][here, :HD]
        for c in range(HD, SUB, HD):
            high = jnp.maximum(high, score_s[sub][here, c:c + HD])
        high = jnp.broadcast_to(jnp.max(high, axis=1, keepdims=True), high.shape) * TO_LOG2
        old = top_s[rows, :]
        top = jnp.maximum(old, high)
        top_s[rows, :] = top
        factor = jnp.exp2(old - top)
        between[0]()
        tops = wide(top, CHUNK)
        for c in range(0, SUB, CHUNK):
            weight = jnp.exp2(score_s[sub][here, c:c + CHUNK] * TO_LOG2 - tops)
            weight_s[sub][here, c:c + CHUNK] = weight.astype(jnp.bfloat16)
            if c == SUB // 2:
                between[1]()
        keys = slice(sub * SUB, (sub + 1) * SUB)
        value = jnp.concatenate([cache_s[slot, keys, HD:], live_s[part, keys, :]], axis=1)
        sum_s[rows, :] = sum_s[rows, :] * wide(factor, 2 * HD) + jnp.dot(
            weight_s[sub][here, :], value, preferred_element_type=jnp.float32
        )

    def phase(seq, slot, part, sub, next_seq, next_slot):
        ahead = [
            functools.partial(score_chunk, next_seq, next_slot, 1 - sub, c)
            for c in range(0, SUB, CHUNK)
        ]
        weigh(seq, slot, part, sub, 0, ahead[:2])
        weigh(seq, slot, part, sub, 1, ahead[2:])

    @pl.when(total > 0)
    def _():
        fetch(jnp.int32(0)).wait()
        patch(jnp.int32(0))
        seq, _ = place(jnp.int32(0))
        for c in range(0, SUB, CHUNK):
            score_chunk(seq, 0, 0, c)

    @pl.loop(0, total)
    def _(i):
        slot = lax.rem(i, slots)
        more = i + 1 < total

        @pl.when(more)
        def _():
            fetch(i + 1).wait()
            patch(i + 1)

        pl.when(i + 2 < total)(lambda: fetch(i + 2).start())
        seq, _ = place(i)
        left = left_of(i)
        part = jnp.where(left < BLOCK, 1, 0)

        @pl.when(left < BLOCK)
        def _():
            inside = lax.broadcasted_iota(jnp.int32, (BLOCK, HD), 0) < left
            live_s[1] = jnp.where(inside, 1.0, 0.0).astype(jnp.bfloat16)

        next_slot = jnp.where(more, lax.rem(i + 1, slots), slot)
        next_seq, _ = place(jnp.where(more, i + 1, i))
        phase(seq, slot, part, 0, seq, slot)
        phase(seq, slot, part, 1, next_seq, next_slot)

    for b in range(seq_count):
        rows = slice(b * node_count, (b + 1) * node_count)
        for h in range(2 * half_heads):
            row = b * seq_rows + h * node_count
            weight_sum = jnp.maximum(sum_s[row:row + node_count, HD:], 1e-30)
            result = sum_s[row:row + node_count, :HD] / weight_sum
            lse = top_s[row:row + node_count, :] + jnp.log2(weight_sum)
            col = h % half_heads * HD
            if h < half_heads:
                keep_ref[rows, col:col + HD] = result
                keep_lse_ref[rows, col:col + HD] = lse
            else:
                send_ref[rows, col:col + HD] = result
                send_ref[rows, half_heads * HD + col:half_heads * HD + col + HD] = lse


def attend(info, mine, other, keys, values, biases, cache):
    depth = len(keys)
    row_count, width = mine.shape
    seq_count, slot_count = cache.shape[:2]
    all_rows = 2 * width // HD * row_count
    seq_rows = all_rows // seq_count
    vmem = pl.BlockSpec(memory_space=pltpu.VMEM)
    return pl.pallas_call(
        functools.partial(attend_kernel, depth),
        out_shape=(
            jax.ShapeDtypeStruct((row_count, width), jnp.float32),
            jax.ShapeDtypeStruct((row_count, width), jnp.float32),
            jax.ShapeDtypeStruct((row_count, 2 * width), jnp.float32),
        ),
        in_specs=[pl.BlockSpec(memory_space=pltpu.SMEM)]
        + [vmem] * (2 + 3 * depth)
        + [pl.BlockSpec(memory_space=pltpu.HBM)],
        out_specs=(vmem, vmem, vmem),
        scratch_shapes=[
            pltpu.VMEM((all_rows, HD), jnp.bfloat16),
            pltpu.VMEM((seq_rows, SUB), jnp.float32),
            pltpu.VMEM((seq_rows, SUB), jnp.float32),
            pltpu.VMEM((seq_rows, SUB), jnp.bfloat16),
            pltpu.VMEM((seq_rows, SUB), jnp.bfloat16),
            pltpu.VMEM((all_rows, HD), jnp.float32),
            pltpu.VMEM((all_rows, 2 * HD), jnp.float32),
            pltpu.VMEM((3, BLOCK, 2 * HD), jnp.bfloat16),
            pltpu.VMEM((2, BLOCK, HD), jnp.bfloat16),
            pltpu.SemaphoreType.DMA((3,)),
        ],
        compiler_params=pltpu.CompilerParams(vmem_limit_bytes=46 * 1024 * 1024),
        cost_estimate=pl.CostEstimate(
            flops=4 * all_rows * slot_count * HD,
            bytes_accessed=2 * cache.size,
            transcendentals=all_rows * slot_count,
        ),
        name="attend",
    )(info, mine, other, *keys, *values, *biases, cache)


STRIP = 256
STRIPS = 4
TILE = 1024


def join_kernel(start, side_ref, x_ref, weight_ref, keep_ref, send_ref, x_s, strip_s, total_s, x_sem, sems):
    side = side_ref[0]
    depth = x_s.shape[1]
    columns = total_s.shape[1]
    count = depth // STRIP
    own = 8

    def strip(i):
        slot = lax.rem(i, STRIPS)
        rows = pl.ds(pl.multiple_of(i * STRIP, STRIP), STRIP)
        return pltpu.make_async_copy(
            weight_ref.at[rows, pl.ds(start, columns)], strip_s.at[slot], sems.at[slot]
        )

    x_copy = pltpu.make_async_copy(x_ref, x_s, x_sem)
    x_copy.start()
    for i in range(STRIPS - 1):
        strip(jnp.int32(i)).start()
    total_s[...] = jnp.zeros(total_s.shape, jnp.float32)
    x_copy.wait()

    @pl.loop(0, count)
    def _(i):
        slot = lax.rem(i, STRIPS)
        pl.when(i + STRIPS - 1 < count)(lambda: strip(i + STRIPS - 1).start())
        strip(i).wait()
        x = x_s[:, pl.ds(pl.multiple_of(i * STRIP, STRIP), STRIP)]
        for c in range(0, columns, TILE):
            total_s[:, c:c + TILE] += jnp.dot(
                x, strip_s[slot, :, c:c + TILE], preferred_element_type=jnp.float32
            )

    for block in range(keep_ref.shape[0] // own):
        rows = slice(block * own, (block + 1) * own)
        keep_at = pl.multiple_of(2 * block * own + side * own, own)
        send_at = pl.multiple_of(2 * block * own + (1 - side) * own, own)
        keep_ref[rows, :] = total_s[pl.ds(keep_at, own), :]
        send_ref[rows, :] = total_s[pl.ds(send_at, own), :]


def join(side, x, weight, start, columns):
    rows, depth = x.shape
    out = jax.ShapeDtypeStruct((rows // 2, columns), jnp.float32)
    vmem = pl.BlockSpec(memory_space=pltpu.VMEM)
    return pl.pallas_call(
        functools.partial(join_kernel, start),
        out_shape=(out, out),
        in_specs=[
            pl.BlockSpec(memory_space=pltpu.SMEM),
            pl.BlockSpec(memory_space=pl.ANY),
            pl.BlockSpec(memory_space=pl.ANY),
        ],
        out_specs=(vmem, vmem),
        scratch_shapes=[
            pltpu.VMEM((rows, depth), x.dtype),
            pltpu.VMEM((STRIPS, STRIP, columns), weight.dtype),
            pltpu.VMEM((rows, columns), jnp.float32),
            pltpu.SemaphoreType.DMA,
            pltpu.SemaphoreType.DMA((STRIPS,)),
        ],
        compiler_params=pltpu.CompilerParams(vmem_limit_bytes=32 * 1024 * 1024),
        cost_estimate=pl.CostEstimate(
            flops=2 * rows * depth * columns, bytes_accessed=2 * depth * columns, transcendentals=0
        ),
        name="join",
    )(side[None], x, weight)


CORE, ACROSS, DEEP = range(3)


def bit_of(distance):
    return lax.axis_index("tensor") // (1 << distance) % 2


def fold(x, axis, distance, kind=jnp.bfloat16):
    bit = bit_of(distance)
    keep = lax.dynamic_index_in_dim(x, bit, axis, keepdims=False)
    send = lax.dynamic_index_in_dim(x, 1 - bit, axis, keepdims=False).astype(kind)
    return keep + partner(send, "tensor", distance).astype(jnp.float32)


def unfold(x, axis, distance):
    other = partner(x, "tensor", distance)
    upper = bit_of(distance) == 1
    return jnp.where(upper, jnp.stack([other, x], axis), jnp.stack([x, other], axis))


def depth_index():
    return lax.axis_index("tensor") >> DEEP


def depth_size():
    return lax.axis_size("tensor") >> DEEP


def across_depth(x, k):
    return lax.ppermute(x, "tensor", [(i, i ^ k << DEEP) for i in range(lax.axis_size("tensor"))])


def fold_depth(x, axis):
    at = depth_index()
    total = lax.dynamic_index_in_dim(x, at, axis, keepdims=False)
    for k in range(1, depth_size()):
        send = lax.dynamic_index_in_dim(x, at ^ k, axis, keepdims=False).astype(jnp.bfloat16)
        total = total + across_depth(send, k).astype(jnp.float32)
    return total


def unfold_depth(x, axis):
    at = depth_index()
    got = [x] + [across_depth(x, k) for k in range(1, depth_size())]
    parts = []
    for place in range(depth_size()):
        part = got[-1]
        for k in range(depth_size() - 1):
            part = jnp.where(at ^ place == k, got[k], part)
        parts.append(part)
    return jnp.stack(parts, axis)


def sum_chips(first, second):
    return jnp.concatenate(
        [fold_depth(fold(first, 1, ACROSS), 0), fold(fold_depth(second, 0), 0, ACROSS)], axis=-1
    )


def collect(rows, cut):
    first = unfold(unfold_depth(rows[:, :cut], 0), 1, ACROSS)
    second = unfold_depth(unfold(rows[:, cut:], 0, ACROSS), 0)
    both = unfold(jnp.concatenate([first, second], axis=-1), 2, CORE)
    return both.reshape(-1, both.shape[-1])


def local_pairs(
    tapped, join_weight, norm_gain, query_weight, kv_weight, out_weight, kv_cache, lengths, parents
):
    side = (lax.axis_index("tensor") % 2).astype(jnp.int32)
    row_count = tapped.shape[0]
    columns = join_weight.shape[1]
    cut = columns * 5 // 8
    spans = ((0, cut), (cut, columns))
    seq_count, piece_len = kv_cache.shape[:2]
    node_count = row_count // seq_count
    own_rows = row_count // 16
    row_ids = jnp.arange(row_count, dtype=jnp.int32)
    valid = jnp.clip(lengths - side * piece_len, 0, piece_len)
    info = jnp.concatenate([valid, side[None]]).astype(jnp.int32)
    parent_rows = row_ids // node_count * node_count + parents
    from_row = (parent_rows[:, :, None] == row_ids).astype(jnp.float32)
    hops = {}
    for step in range(STEPS):
        hops[step, step] = jnp.eye(row_count, dtype=jnp.float32)
        for earlier in range(step - 1, -1, -1):
            hops[step, earlier] = jnp.dot(hops[step, earlier + 1], from_row[earlier])
    bias = {at: (hop - 1.0) * -floor_score for at, hop in hops.items()}

    folded = []
    for start, end in spans:
        kept, sent = join(side, tapped, join_weight, start, end - start)
        part = kept + partner(sent, "tensor", CORE)
        folded.append(part.reshape(-1, 2, own_rows, end - start))
    hidden = sum_chips(*folded)

    keys, values = [], []
    for step in range(STEPS):
        normed = collect(normalize(hidden, norm_gain), cut)
        new_kv = jnp.dot(normed, kv_weight, preferred_element_type=jnp.float32)
        new_kv = new_kv.astype(jnp.bfloat16)
        query = jnp.dot(normed, query_weight, preferred_element_type=jnp.float32)
        query = query.astype(jnp.bfloat16)
        keys.append(partner(new_kv, "tensor", CORE))
        values.append(new_kv)
        kept, kept_lse, sent = attend(
            info, query, partner(query, "tensor", CORE), keys, values,
            [bias[step, t] for t in range(step + 1)], kv_cache,
        )
        came = partner(sent, "tensor", CORE)
        width = kept.shape[1]
        top = jnp.maximum(kept_lse, came[:, width:])
        mine = jnp.exp2(kept_lse - top)
        theirs = jnp.exp2(came[:, width:] - top)
        attended = (mine * kept + theirs * came[:, :width]) / (mine + theirs)
        update = jnp.dot(
            attended.astype(jnp.bfloat16), out_weight, preferred_element_type=jnp.float32
        ).reshape(-1, 2, 2, own_rows, columns)
        hidden = hidden + sum_chips(*[
            fold(update[..., start:end], 2, CORE, jnp.float32) for start, end in spans
        ])
    return hidden


def solution(mesh):
    body = local_pairs if mesh.shape["tensor"] == 2 * KVH else local_general
    placed = (
        P("groups", "tensor"),
        P("tensor", None),
        P(),
        P(None, "tensor"),
        P(None, "tensor"),
        P("tensor", None),
        P("groups", "tensor", None),
        P("groups"),
        P(None, "groups"),
    )
    return jax.shard_map(
        body, mesh=mesh, in_specs=placed, out_specs=P(("groups", "tensor"), None), check_vma=False
    )
```

```python
import functools
import math

import jax
import jax.numpy as jnp
from jax import lax
from jax.experimental import pallas as pl
from jax.experimental.pallas import tpu as pltpu
from jax.sharding import PartitionSpec as P

KVH = 8
HD = 128
QPK = 8
STEPS = 3


epsilon = 1e-05
floor_score = -1e30


def partner(x, axis, distance):
    return lax.ppermute(x, axis, [(i, i ^ 1 << distance) for i in range(lax.axis_size(axis))])


def as_sent(x):

    def short(part):
        return part.astype(jnp.bfloat16) if part.dtype == jnp.float32 else part

    return jax.tree.map(short, x)


def normalize(values, norm_gain):
    mean_square = jnp.mean(values * values, axis=-1, keepdims=True)
    return (values * lax.rsqrt(mean_square + epsilon) * norm_gain).astype(jnp.bfloat16)


def merge_parts(mine, theirs):
    row_top = jnp.maximum(mine[0], theirs[0])
    mine_factor = jnp.exp(mine[0] - row_top)
    their_factor = jnp.exp(theirs[0] - row_top)
    row_sum = mine_factor * mine[1] + their_factor * theirs[1]
    numerator = mine_factor[..., None] * mine[2] + their_factor[..., None] * theirs[2]
    return (row_top, row_sum, numerator)


def local_general(
    tapped, join_weight, norm_gain, query_weight, kv_weight, out_weight, kv_cache, lengths, parents
):
    tensor_size = lax.axis_size("tensor")
    device = lax.axis_index("tensor")
    group_size = tensor_size // KVH
    hop_count = group_size.bit_length() - 1
    piece_index = device % group_size
    row_count_all = tapped.shape[0]
    seq_count = kv_cache.shape[0]
    node_count = row_count_all // seq_count
    query_cols = query_weight.shape[1]
    proj_weight = jnp.concatenate([query_weight, kv_weight], axis=1)
    score_scale = 1.0 / math.sqrt(HD)
    hidden_rows = lax.psum_scatter(
        jnp.dot(tapped, join_weight, preferred_element_type=jnp.float32),
        "tensor",
        scatter_dimension=0,
        tiled=True,
    )
    piece_len = kv_cache.shape[1]
    positions = piece_index * piece_len + jnp.arange(piece_len, dtype=jnp.int32)
    visible = positions[None, :] < lengths[:, None]
    is_first = piece_index == 0
    keys_cache = kv_cache[:, :, :HD]
    values_cache = kv_cache[:, :, HD:]
    row_ids = jnp.arange(row_count_all, dtype=jnp.int32)
    seq_base = row_ids // node_count * node_count
    head_rows = node_count * QPK
    width = out_weight.shape[0]
    history = []
    for step_num in range(STEPS):
        projected = jnp.dot(
            lax.all_gather(normalize(hidden_rows, norm_gain), "tensor", axis=0, tiled=True),
            proj_weight,
            preferred_element_type=jnp.float32,
        ).astype(jnp.bfloat16)
        query_group = projected[:, :query_cols]
        kv_group = projected[:, query_cols:]
        for bit_num in range(hop_count):
            other_query, other_kv = partner((query_group, kv_group), "tensor", bit_num)
            is_upper = device // (1 << bit_num) % 2 == 1
            query_group = jnp.where(
                is_upper,
                jnp.concatenate([other_query, query_group], axis=1),
                jnp.concatenate([query_group, other_query], axis=1),
            )
            kv_group = jnp.where(
                is_upper,
                jnp.concatenate([other_kv, kv_group], axis=1),
                jnp.concatenate([kv_group, other_kv], axis=1),
            )
        history.append(kv_group)
        ancestors = [row_ids]
        current = row_ids
        for earlier in range(step_num - 1, -1, -1):
            current = seq_base + jnp.take(parents[earlier], current, axis=0)
            ancestors.insert(0, current)
        new_depth = step_num + 1
        new_kv = jnp.stack(
            [
                jnp.take(history[earlier], ancestors[earlier], axis=0)
                for earlier in range(new_depth)
            ],
            axis=1,
        )
        new_keys = new_kv[..., :HD].reshape(seq_count, node_count, new_depth, HD)
        new_values = new_kv[..., HD:].reshape(seq_count, node_count, new_depth, HD)
        query_blocks = query_group.reshape(seq_count, head_rows, HD)
        scores = (
            jnp.einsum("brd,bcd->brc", query_blocks, keys_cache, preferred_element_type=jnp.float32)
            * score_scale
        )
        scores = jnp.where(visible[:, None, :], scores, floor_score)
        query_nodes = query_group.reshape(seq_count, node_count, QPK, HD)
        new_scores = (
            jnp.einsum("bnqd,bntd->bnqt", query_nodes, new_keys, preferred_element_type=jnp.float32)
            * score_scale
        )
        new_scores = jnp.where(is_first, new_scores, floor_score)
        row_top = jnp.maximum(
            jnp.max(scores, axis=-1), jnp.max(new_scores, axis=-1).reshape(seq_count, head_rows)
        )
        weights = jnp.where(visible[:, None, :], jnp.exp(scores - row_top[..., None]), 0.0)
        top_nodes = row_top.reshape(seq_count, node_count, QPK)
        new_weights = jnp.where(is_first, jnp.exp(new_scores - top_nodes[..., None]), 0.0)
        row_sum = jnp.sum(weights, axis=-1) + jnp.sum(new_weights, axis=-1).reshape(
            seq_count, head_rows
        )
        numerator = jnp.einsum(
            "brc,bcd->brd",
            weights.astype(jnp.bfloat16),
            values_cache,
            preferred_element_type=jnp.float32,
        )
        new_part = jnp.einsum(
            "bnqt,bntd->bnqd",
            new_weights.astype(jnp.bfloat16),
            new_values,
            preferred_element_type=jnp.float32,
        )
        numerator = numerator + new_part.reshape(seq_count, head_rows, HD)
        partial_value = (row_top, row_sum, numerator)
        for bit_num in range(hop_count):
            theirs = partner(
                (as_sent(partial_value[0]), as_sent(partial_value[1]), as_sent(partial_value[2])),
                "tensor",
                bit_num,
            )
            partial_value = merge_parts(partial_value, theirs)
        attended = (
            (partial_value[2] / partial_value[1][..., None])
            .astype(jnp.bfloat16)
            .reshape(row_count_all, QPK * HD)
        )
        attended_mine = lax.dynamic_slice_in_dim(attended, piece_index * width, width, 1)
        hidden_rows = hidden_rows + lax.psum_scatter(
            jnp.dot(attended_mine, out_weight, preferred_element_type=jnp.float32),
            "tensor",
            scatter_dimension=0,
            tiled=True,
        )
    return hidden_rows


BLOCK = 2048
SUB = BLOCK // 2
CHUNK = 256
TO_LOG2 = math.log2(math.e) / math.sqrt(HD)


def score_dot(query, key):
    return lax.dot_general(
        query, key, (((1,), (1,)), ((), ())), preferred_element_type=jnp.float32
    )


def wide(x, width):
    return jnp.concatenate([x] * (width // HD), axis=1)


def attend_kernel(depth, info_ref, mine_ref, other_ref, *refs):
    key_refs, value_refs, bias_refs = refs[:depth], refs[depth:2 * depth], refs[2 * depth:3 * depth]
    cache_ref, keep_ref, keep_lse_ref, send_ref, query_s = refs[3 * depth:3 * depth + 5]
    score_s, weight_s = refs[3 * depth + 5:3 * depth + 7], refs[3 * depth + 7:3 * depth + 9]
    top_s, sum_s, cache_s, live_s, sems = refs[3 * depth + 9:]
    seq_count = cache_ref.shape[0]
    node_count = mine_ref.shape[0] // seq_count
    half_heads = mine_ref.shape[1] // HD
    seq_rows = 2 * half_heads * node_count
    half_rows = seq_rows // 2
    slots = cache_s.shape[0]
    steps = [lax.div(info_ref[b] + BLOCK - 1, BLOCK) for b in range(seq_count)]
    total = sum(steps)

    def place(i):
        seq = jnp.int32(0)
        block = i
        for b in range(seq_count - 1):
            later = jnp.logical_and(block >= steps[b], seq == b)
            seq = jnp.where(later, b + 1, seq)
            block = jnp.where(later, block - steps[b], block)
        return seq, block

    def left_of(i):
        seq, block = place(i)
        return info_ref[seq] - block * BLOCK

    def fetch(i):
        seq, block = place(i)
        slot = lax.rem(i, slots)
        start = pl.multiple_of(block * BLOCK, BLOCK)
        return pltpu.make_async_copy(
            cache_ref.at[seq, pl.ds(start, BLOCK), :], cache_s.at[slot], sems.at[slot]
        )

    for i in range(2):
        pl.when(i < total)(lambda i=i: fetch(jnp.int32(i)).start())

    for b in range(seq_count):
        rows = slice(b * node_count, (b + 1) * node_count)
        for h in range(2 * half_heads):
            ref = mine_ref if h < half_heads else other_ref
            col = h % half_heads * HD
            row = b * seq_rows + h * node_count
            query_s[row:row + node_count, :] = ref[rows, col:col + HD]
    live_s[0] = jnp.ones((BLOCK, HD), jnp.bfloat16)

    @pl.when(info_ref[seq_count] == 0)
    def _():
        top_s[...] = jnp.full(top_s.shape, floor_score, jnp.float32)
        sum_s[...] = jnp.zeros(sum_s.shape, jnp.float32)

    @pl.when(info_ref[seq_count] != 0)
    def _():
        for b in range(seq_count):
            rows = slice(b * seq_rows, (b + 1) * seq_rows)
            query = query_s[rows, :]
            scores = []
            for t in range(depth):
                bias = bias_refs[t][b * node_count:(b + 1) * node_count, :]
                score = score_dot(query, key_refs[t][...])
                scores.append(score * TO_LOG2 + jnp.concatenate([bias] * (2 * half_heads), axis=0))
            top = functools.reduce(jnp.maximum, scores)
            top = jnp.broadcast_to(jnp.max(top, axis=1, keepdims=True), top.shape)
            gathered = jnp.zeros((seq_rows, 2 * HD), jnp.float32)
            for t in range(depth):
                weight = jnp.exp2(scores[t] - top).astype(jnp.bfloat16)
                value = value_refs[t][...]
                value = jnp.concatenate([value, jnp.ones_like(value)], axis=1)
                gathered = gathered + jnp.dot(weight, value, preferred_element_type=jnp.float32)
            top_s[rows, :] = top
            sum_s[rows, :] = gathered

    def patch(i):
        left = left_of(i)
        slot = lax.rem(i, slots)

        @pl.when(left < BLOCK)
        def _():
            inside = lax.broadcasted_iota(jnp.int32, (BLOCK, HD), 0) < left
            key = cache_s[slot, :, :HD].astype(jnp.float32)
            value = cache_s[slot, :, HD:].astype(jnp.float32)
            key = jnp.where(inside, key, jnp.broadcast_to(key[:1, :], key.shape))
            cache_s[slot, :, :HD] = key.astype(jnp.bfloat16)
            cache_s[slot, :, HD:] = jnp.where(inside, value, 0.0).astype(jnp.bfloat16)

    def score_chunk(seq, slot, sub, c):
        rows = pl.ds(pl.multiple_of(seq * seq_rows, seq_rows), seq_rows)
        at = sub * SUB + c
        score_s[sub][:, c:c + CHUNK] = score_dot(query_s[rows, :], cache_s[slot, at:at + CHUNK, :HD])

    def weigh(seq, slot, part, sub, half, between):
        rows = pl.ds(pl.multiple_of(seq * seq_rows + half * half_rows, half_rows), half_rows)
        here = slice(half * half_rows, (half + 1) * half_rows)
        high = score_s[sub][here, :HD]
        for c in range(HD, SUB, HD):
            high = jnp.maximum(high, score_s[sub][here, c:c + HD])
        high = jnp.broadcast_to(jnp.max(high, axis=1, keepdims=True), high.shape) * TO_LOG2
        old = top_s[rows, :]
        top = jnp.maximum(old, high)
        top_s[rows, :] = top
        factor = jnp.exp2(old - top)
        between[0]()
        tops = wide(top, CHUNK)
        for c in range(0, SUB, CHUNK):
            weight = jnp.exp2(score_s[sub][here, c:c + CHUNK] * TO_LOG2 - tops)
            weight_s[sub][here, c:c + CHUNK] = weight.astype(jnp.bfloat16)
            if c == SUB // 2:
                between[1]()
        keys = slice(sub * SUB, (sub + 1) * SUB)
        value = jnp.concatenate([cache_s[slot, keys, HD:], live_s[part, keys, :]], axis=1)
        sum_s[rows, :] = sum_s[rows, :] * wide(factor, 2 * HD) + jnp.dot(
            weight_s[sub][here, :], value, preferred_element_type=jnp.float32
        )

    def phase(seq, slot, part, sub, next_seq, next_slot):
        ahead = [
            functools.partial(score_chunk, next_seq, next_slot, 1 - sub, c)
            for c in range(0, SUB, CHUNK)
        ]
        weigh(seq, slot, part, sub, 0, ahead[:2])
        weigh(seq, slot, part, sub, 1, ahead[2:])

    @pl.when(total > 0)
    def _():
        fetch(jnp.int32(0)).wait()
        patch(jnp.int32(0))
        seq, _ = place(jnp.int32(0))
        for c in range(0, SUB, CHUNK):
            score_chunk(seq, 0, 0, c)

    @pl.loop(0, total)
    def _(i):
        slot = lax.rem(i, slots)
        more = i + 1 < total

        @pl.when(more)
        def _():
            fetch(i + 1).wait()
            patch(i + 1)

        pl.when(i + 2 < total)(lambda: fetch(i + 2).start())
        seq, _ = place(i)
        left = left_of(i)
        part = jnp.where(left < BLOCK, 1, 0)

        @pl.when(left < BLOCK)
        def _():
            inside = lax.broadcasted_iota(jnp.int32, (BLOCK, HD), 0) < left
            live_s[1] = jnp.where(inside, 1.0, 0.0).astype(jnp.bfloat16)

        next_slot = jnp.where(more, lax.rem(i + 1, slots), slot)
        next_seq, _ = place(jnp.where(more, i + 1, i))
        phase(seq, slot, part, 0, seq, slot)
        phase(seq, slot, part, 1, next_seq, next_slot)

    for b in range(seq_count):
        rows = slice(b * node_count, (b + 1) * node_count)
        for h in range(2 * half_heads):
            row = b * seq_rows + h * node_count
            weight_sum = jnp.maximum(sum_s[row:row + node_count, HD:], 1e-30)
            result = sum_s[row:row + node_count, :HD] / weight_sum
            lse = top_s[row:row + node_count, :] + jnp.log2(weight_sum)
            col = h % half_heads * HD
            if h < half_heads:
                keep_ref[rows, col:col + HD] = result
                keep_lse_ref[rows, col:col + HD] = lse
            else:
                send_ref[rows, col:col + HD] = result
                send_ref[rows, half_heads * HD + col:half_heads * HD + col + HD] = lse


def attend(info, mine, other, keys, values, biases, cache):
    depth = len(keys)
    row_count, width = mine.shape
    seq_count, slot_count = cache.shape[:2]
    all_rows = 2 * width // HD * row_count
    seq_rows = all_rows // seq_count
    vmem = pl.BlockSpec(memory_space=pltpu.VMEM)
    return pl.pallas_call(
        functools.partial(attend_kernel, depth),
        out_shape=(
            jax.ShapeDtypeStruct((row_count, width), jnp.float32),
            jax.ShapeDtypeStruct((row_count, width), jnp.float32),
            jax.ShapeDtypeStruct((row_count, 2 * width), jnp.float32),
        ),
        in_specs=[pl.BlockSpec(memory_space=pltpu.SMEM)]
        + [vmem] * (2 + 3 * depth)
        + [pl.BlockSpec(memory_space=pltpu.HBM)],
        out_specs=(vmem, vmem, vmem),
        scratch_shapes=[
            pltpu.VMEM((all_rows, HD), jnp.bfloat16),
            pltpu.VMEM((seq_rows, SUB), jnp.float32),
            pltpu.VMEM((seq_rows, SUB), jnp.float32),
            pltpu.VMEM((seq_rows, SUB), jnp.bfloat16),
            pltpu.VMEM((seq_rows, SUB), jnp.bfloat16),
            pltpu.VMEM((all_rows, HD), jnp.float32),
            pltpu.VMEM((all_rows, 2 * HD), jnp.float32),
            pltpu.VMEM((3, BLOCK, 2 * HD), jnp.bfloat16),
            pltpu.VMEM((2, BLOCK, HD), jnp.bfloat16),
            pltpu.SemaphoreType.DMA((3,)),
        ],
        compiler_params=pltpu.CompilerParams(vmem_limit_bytes=24 * 1024 * 1024),
        cost_estimate=pl.CostEstimate(
            flops=4 * all_rows * slot_count * HD,
            bytes_accessed=2 * cache.size,
            transcendentals=all_rows * slot_count,
        ),
        name="attend",
    )(
        info, mine, other, *keys, *values, *biases,
        pltpu.with_memory_space_constraint(cache, pltpu.HBM),
    )


STRIP = 256
STRIPS = 4
TILE = 512


def join_kernel(start, side_ref, x_ref, weight_ref, keep_ref, send_ref, x_s, strip_s, total_s, x_sem, sems):
    side = side_ref[0]
    depth = x_s.shape[1]
    columns = total_s.shape[1]
    count = depth // STRIP
    own = 8

    def strip(i):
        slot = lax.rem(i, STRIPS)
        rows = pl.ds(pl.multiple_of(i * STRIP, STRIP), STRIP)
        return pltpu.make_async_copy(
            weight_ref.at[rows, pl.ds(start, columns)], strip_s.at[slot], sems.at[slot]
        )

    x_copy = pltpu.make_async_copy(x_ref, x_s, x_sem)
    x_copy.start()
    for i in range(STRIPS - 1):
        strip(jnp.int32(i)).start()
    total_s[...] = jnp.zeros(total_s.shape, jnp.float32)
    x_copy.wait()

    @pl.loop(0, count)
    def _(i):
        slot = lax.rem(i, STRIPS)
        pl.when(i + STRIPS - 1 < count)(lambda: strip(i + STRIPS - 1).start())
        strip(i).wait()
        x = x_s[:, pl.ds(pl.multiple_of(i * STRIP, STRIP), STRIP)]
        for c in range(0, columns, TILE):
            total_s[:, c:c + TILE] += jnp.dot(
                x, strip_s[slot, :, c:c + TILE], preferred_element_type=jnp.float32
            )

    for block in range(keep_ref.shape[0] // own):
        rows = slice(block * own, (block + 1) * own)
        keep_at = pl.multiple_of(2 * block * own + side * own, own)
        send_at = pl.multiple_of(2 * block * own + (1 - side) * own, own)
        keep_ref[rows, :] = total_s[pl.ds(keep_at, own), :]
        send_ref[rows, :] = total_s[pl.ds(send_at, own), :]


def join(side, x, weight, start, columns):
    rows, depth = x.shape
    out = jax.ShapeDtypeStruct((rows // 2, columns), jnp.float32)
    vmem = pl.BlockSpec(memory_space=pltpu.VMEM)
    return pl.pallas_call(
        functools.partial(join_kernel, start),
        out_shape=(out, out),
        in_specs=[
            pl.BlockSpec(memory_space=pltpu.SMEM),
            pl.BlockSpec(memory_space=pl.ANY),
            pl.BlockSpec(memory_space=pl.ANY),
        ],
        out_specs=(vmem, vmem),
        scratch_shapes=[
            pltpu.VMEM((rows, depth), x.dtype),
            pltpu.VMEM((STRIPS, STRIP, columns), weight.dtype),
            pltpu.VMEM((rows, columns), jnp.float32),
            pltpu.SemaphoreType.DMA,
            pltpu.SemaphoreType.DMA((STRIPS,)),
        ],
        compiler_params=pltpu.CompilerParams(vmem_limit_bytes=32 * 1024 * 1024),
        cost_estimate=pl.CostEstimate(
            flops=2 * rows * depth * columns, bytes_accessed=2 * depth * columns, transcendentals=0
        ),
        name="join",
    )(side[None], x, weight)


CORE, ACROSS, DEEP = range(3)


def bit_of(distance):
    return lax.axis_index("tensor") // (1 << distance) % 2


def fold(x, axis, distance, kind=jnp.bfloat16):
    bit = bit_of(distance)
    keep = lax.dynamic_index_in_dim(x, bit, axis, keepdims=False)
    send = lax.dynamic_index_in_dim(x, 1 - bit, axis, keepdims=False).astype(kind)
    return keep + partner(send, "tensor", distance).astype(jnp.float32)


def unfold(x, axis, distance):
    other = partner(x, "tensor", distance)
    upper = bit_of(distance) == 1
    return jnp.where(upper, jnp.stack([other, x], axis), jnp.stack([x, other], axis))


def depth_index():
    return lax.axis_index("tensor") >> DEEP


def depth_size():
    return lax.axis_size("tensor") >> DEEP


def across_depth(x, k):
    return lax.ppermute(x, "tensor", [(i, i ^ k << DEEP) for i in range(lax.axis_size("tensor"))])


def fold_depth(x, axis):
    at = depth_index()
    total = lax.dynamic_index_in_dim(x, at, axis, keepdims=False)
    for k in range(1, depth_size()):
        send = lax.dynamic_index_in_dim(x, at ^ k, axis, keepdims=False).astype(jnp.bfloat16)
        total = total + across_depth(send, k).astype(jnp.float32)
    return total


def unfold_depth(x, axis):
    at = depth_index()
    got = [x] + [across_depth(x, k) for k in range(1, depth_size())]
    parts = []
    for place in range(depth_size()):
        part = got[-1]
        for k in range(depth_size() - 1):
            part = jnp.where(at ^ place == k, got[k], part)
        parts.append(part)
    return jnp.stack(parts, axis)


def sum_chips(first, second):
    first, second = lax.optimization_barrier((first, second))
    return jnp.concatenate(
        [fold_depth(fold(first, 1, ACROSS), 0), fold(fold_depth(second, 0), 0, ACROSS)], axis=-1
    )


def collect(rows, cut):
    first = unfold(unfold_depth(rows[:, :cut], 0), 1, ACROSS)
    second = unfold_depth(unfold(rows[:, cut:], 0, ACROSS), 0)
    both = unfold(jnp.concatenate([first, second], axis=-1), 2, CORE)
    return both.reshape(-1, both.shape[-1])


def local_pairs(
    tapped, join_weight, norm_gain, query_weight, kv_weight, out_weight, kv_cache, lengths, parents
):
    side = (lax.axis_index("tensor") % 2).astype(jnp.int32)
    row_count = tapped.shape[0]
    columns = join_weight.shape[1]
    sum_cut, cut = columns * 11 // 16, columns * 5 // 8
    spans = ((0, sum_cut), (sum_cut, columns))
    seq_count, piece_len = kv_cache.shape[:2]
    node_count = row_count // seq_count
    own_rows = row_count // 16
    row_ids = jnp.arange(row_count, dtype=jnp.int32)
    valid = jnp.clip(lengths - side * piece_len, 0, piece_len)
    info = jnp.concatenate([valid, side[None]]).astype(jnp.int32)
    parent_rows = row_ids // node_count * node_count + parents
    from_row = (parent_rows[:, :, None] == row_ids).astype(jnp.float32)
    hops = {}
    for step in range(STEPS):
        hops[step, step] = jnp.eye(row_count, dtype=jnp.float32)
        for earlier in range(step - 1, -1, -1):
            hops[step, earlier] = jnp.dot(hops[step, earlier + 1], from_row[earlier])
    bias = {at: (hop - 1.0) * -floor_score for at, hop in hops.items()}

    folded = []
    for start, end in spans:
        kept, sent = join(side, tapped, join_weight, start, end - start)
        part = kept + partner(sent, "tensor", CORE)
        folded.append(part.reshape(-1, 2, own_rows, end - start))
    hidden = sum_chips(*folded)

    keys, values = [], []
    for step in range(STEPS):
        normed = collect(normalize(hidden, norm_gain), cut)
        new_kv = jnp.dot(normed, kv_weight, preferred_element_type=jnp.float32)
        new_kv = new_kv.astype(jnp.bfloat16)
        query = jnp.dot(normed, query_weight, preferred_element_type=jnp.float32)
        query = query.astype(jnp.bfloat16)
        keys.append(partner(new_kv, "tensor", CORE))
        values.append(new_kv)
        kept, kept_lse, sent = attend(
            info, query, partner(query, "tensor", CORE), keys, values,
            [bias[step, t] for t in range(step + 1)], kv_cache,
        )
        came = partner(sent, "tensor", CORE)
        width = kept.shape[1]
        top = jnp.maximum(kept_lse, came[:, width:])
        mine = jnp.exp2(kept_lse - top)
        theirs = jnp.exp2(came[:, width:] - top)
        attended = (mine * kept + theirs * came[:, :width]) / (mine + theirs)
        update = jnp.dot(
            attended.astype(jnp.bfloat16), out_weight, preferred_element_type=jnp.float32
        ).reshape(-1, 2, 2, own_rows, columns)
        hidden = hidden + sum_chips(*[
            fold(update[..., start:end], 2, CORE, jnp.float32) for start, end in spans
        ])
    return hidden


def solution(mesh):
    body = local_pairs if mesh.shape["tensor"] == 2 * KVH else local_general
    placed = (
        P("groups", "tensor"),
        P("tensor", None),
        P(),
        P(None, "tensor"),
        P(None, "tensor"),
        P("tensor", None),
        P("groups", "tensor", None),
        P("groups"),
        P(None, "groups"),
    )
    return jax.shard_map(
        body, mesh=mesh, in_specs=placed, out_specs=P(("groups", "tensor"), None), check_vma=False
    )
```

```python
import functools
import math

import jax
import jax.numpy as jnp
from jax import lax
from jax.experimental import pallas as pl
from jax.experimental.pallas import tpu as pltpu
from jax.sharding import PartitionSpec as P

KVH = 8
HD = 128
QPK = 8
STEPS = 3


epsilon = 1e-05
floor_score = -1e30


def partner(x, axis, distance):
    return lax.ppermute(x, axis, [(i, i ^ 1 << distance) for i in range(lax.axis_size(axis))])


def as_sent(x):

    def short(part):
        return part.astype(jnp.bfloat16) if part.dtype == jnp.float32 else part

    return jax.tree.map(short, x)


def normalize(values, norm_gain):
    mean_square = jnp.mean(values * values, axis=-1, keepdims=True)
    return (values * lax.rsqrt(mean_square + epsilon) * norm_gain).astype(jnp.bfloat16)


def merge_parts(mine, theirs):
    row_top = jnp.maximum(mine[0], theirs[0])
    mine_factor = jnp.exp(mine[0] - row_top)
    their_factor = jnp.exp(theirs[0] - row_top)
    row_sum = mine_factor * mine[1] + their_factor * theirs[1]
    numerator = mine_factor[..., None] * mine[2] + their_factor[..., None] * theirs[2]
    return (row_top, row_sum, numerator)


def local_general(
    tapped, join_weight, norm_gain, query_weight, kv_weight, out_weight, kv_cache, lengths, parents
):
    tensor_size = lax.axis_size("tensor")
    device = lax.axis_index("tensor")
    group_size = tensor_size // KVH
    hop_count = group_size.bit_length() - 1
    piece_index = device % group_size
    row_count_all = tapped.shape[0]
    seq_count = kv_cache.shape[0]
    node_count = row_count_all // seq_count
    query_cols = query_weight.shape[1]
    proj_weight = jnp.concatenate([query_weight, kv_weight], axis=1)
    score_scale = 1.0 / math.sqrt(HD)
    hidden_rows = lax.psum_scatter(
        jnp.dot(tapped, join_weight, preferred_element_type=jnp.float32),
        "tensor",
        scatter_dimension=0,
        tiled=True,
    )
    piece_len = kv_cache.shape[1]
    positions = piece_index * piece_len + jnp.arange(piece_len, dtype=jnp.int32)
    visible = positions[None, :] < lengths[:, None]
    is_first = piece_index == 0
    keys_cache = kv_cache[:, :, :HD]
    values_cache = kv_cache[:, :, HD:]
    row_ids = jnp.arange(row_count_all, dtype=jnp.int32)
    seq_base = row_ids // node_count * node_count
    head_rows = node_count * QPK
    width = out_weight.shape[0]
    history = []
    for step_num in range(STEPS):
        projected = jnp.dot(
            lax.all_gather(normalize(hidden_rows, norm_gain), "tensor", axis=0, tiled=True),
            proj_weight,
            preferred_element_type=jnp.float32,
        ).astype(jnp.bfloat16)
        query_group = projected[:, :query_cols]
        kv_group = projected[:, query_cols:]
        for bit_num in range(hop_count):
            other_query, other_kv = partner((query_group, kv_group), "tensor", bit_num)
            is_upper = device // (1 << bit_num) % 2 == 1
            query_group = jnp.where(
                is_upper,
                jnp.concatenate([other_query, query_group], axis=1),
                jnp.concatenate([query_group, other_query], axis=1),
            )
            kv_group = jnp.where(
                is_upper,
                jnp.concatenate([other_kv, kv_group], axis=1),
                jnp.concatenate([kv_group, other_kv], axis=1),
            )
        history.append(kv_group)
        ancestors = [row_ids]
        current = row_ids
        for earlier in range(step_num - 1, -1, -1):
            current = seq_base + jnp.take(parents[earlier], current, axis=0)
            ancestors.insert(0, current)
        new_depth = step_num + 1
        new_kv = jnp.stack(
            [
                jnp.take(history[earlier], ancestors[earlier], axis=0)
                for earlier in range(new_depth)
            ],
            axis=1,
        )
        new_keys = new_kv[..., :HD].reshape(seq_count, node_count, new_depth, HD)
        new_values = new_kv[..., HD:].reshape(seq_count, node_count, new_depth, HD)
        query_blocks = query_group.reshape(seq_count, head_rows, HD)
        scores = (
            jnp.einsum("brd,bcd->brc", query_blocks, keys_cache, preferred_element_type=jnp.float32)
            * score_scale
        )
        scores = jnp.where(visible[:, None, :], scores, floor_score)
        query_nodes = query_group.reshape(seq_count, node_count, QPK, HD)
        new_scores = (
            jnp.einsum("bnqd,bntd->bnqt", query_nodes, new_keys, preferred_element_type=jnp.float32)
            * score_scale
        )
        new_scores = jnp.where(is_first, new_scores, floor_score)
        row_top = jnp.maximum(
            jnp.max(scores, axis=-1), jnp.max(new_scores, axis=-1).reshape(seq_count, head_rows)
        )
        weights = jnp.where(visible[:, None, :], jnp.exp(scores - row_top[..., None]), 0.0)
        top_nodes = row_top.reshape(seq_count, node_count, QPK)
        new_weights = jnp.where(is_first, jnp.exp(new_scores - top_nodes[..., None]), 0.0)
        row_sum = jnp.sum(weights, axis=-1) + jnp.sum(new_weights, axis=-1).reshape(
            seq_count, head_rows
        )
        numerator = jnp.einsum(
            "brc,bcd->brd",
            weights.astype(jnp.bfloat16),
            values_cache,
            preferred_element_type=jnp.float32,
        )
        new_part = jnp.einsum(
            "bnqt,bntd->bnqd",
            new_weights.astype(jnp.bfloat16),
            new_values,
            preferred_element_type=jnp.float32,
        )
        numerator = numerator + new_part.reshape(seq_count, head_rows, HD)
        partial_value = (row_top, row_sum, numerator)
        for bit_num in range(hop_count):
            theirs = partner(
                (as_sent(partial_value[0]), as_sent(partial_value[1]), as_sent(partial_value[2])),
                "tensor",
                bit_num,
            )
            partial_value = merge_parts(partial_value, theirs)
        attended = (
            (partial_value[2] / partial_value[1][..., None])
            .astype(jnp.bfloat16)
            .reshape(row_count_all, QPK * HD)
        )
        attended_mine = lax.dynamic_slice_in_dim(attended, piece_index * width, width, 1)
        hidden_rows = hidden_rows + lax.psum_scatter(
            jnp.dot(attended_mine, out_weight, preferred_element_type=jnp.float32),
            "tensor",
            scatter_dimension=0,
            tiled=True,
        )
    return hidden_rows


BLOCK = 2048
SUB = BLOCK // 2
CHUNK = 256
TO_LOG2 = math.log2(math.e) / math.sqrt(HD)


def score_dot(query, key):
    return lax.dot_general(
        query, key, (((1,), (1,)), ((), ())), preferred_element_type=jnp.float32
    )


def wide(x, width):
    return jnp.concatenate([x] * (width // HD), axis=1)


def attend_kernel(depth, info_ref, mine_ref, other_ref, *refs):
    key_refs, value_refs, bias_refs = refs[:depth], refs[depth:2 * depth], refs[2 * depth:3 * depth]
    cache_ref, keep_ref, keep_lse_ref, send_ref, query_s = refs[3 * depth:3 * depth + 5]
    score_s, weight_s = refs[3 * depth + 5:3 * depth + 7], refs[3 * depth + 7:3 * depth + 9]
    top_s, sum_s, cache_s, live_s, sems = refs[3 * depth + 9:]
    seq_count = cache_ref.shape[0]
    node_count = mine_ref.shape[0] // seq_count
    half_heads = mine_ref.shape[1] // HD
    seq_rows = 2 * half_heads * node_count
    half_rows = seq_rows // 2
    slots = cache_s.shape[0]
    steps = [lax.div(info_ref[b] + BLOCK - 1, BLOCK) for b in range(seq_count)]
    total = sum(steps)

    def place(i):
        seq = jnp.int32(0)
        block = i
        for b in range(seq_count - 1):
            later = jnp.logical_and(block >= steps[b], seq == b)
            seq = jnp.where(later, b + 1, seq)
            block = jnp.where(later, block - steps[b], block)
        return seq, block

    def left_of(i):
        seq, block = place(i)
        return info_ref[seq] - block * BLOCK

    def fetch(i):
        seq, block = place(i)
        slot = lax.rem(i, slots)
        start = pl.multiple_of(block * BLOCK, BLOCK)
        return pltpu.make_async_copy(
            cache_ref.at[seq, pl.ds(start, BLOCK), :], cache_s.at[slot], sems.at[slot]
        )

    for i in range(2):
        pl.when(i < total)(lambda i=i: fetch(jnp.int32(i)).start())

    for b in range(seq_count):
        rows = slice(b * node_count, (b + 1) * node_count)
        for h in range(2 * half_heads):
            ref = mine_ref if h < half_heads else other_ref
            col = h % half_heads * HD
            row = b * seq_rows + h * node_count
            query_s[row:row + node_count, :] = ref[rows, col:col + HD]
    live_s[0] = jnp.ones((BLOCK, HD), jnp.bfloat16)

    @pl.when(info_ref[seq_count] == 0)
    def _():
        top_s[...] = jnp.full(top_s.shape, floor_score, jnp.float32)
        sum_s[...] = jnp.zeros(sum_s.shape, jnp.float32)

    @pl.when(info_ref[seq_count] != 0)
    def _():
        for b in range(seq_count):
            rows = slice(b * seq_rows, (b + 1) * seq_rows)
            query = query_s[rows, :]
            scores = []
            for t in range(depth):
                bias = bias_refs[t][b * node_count:(b + 1) * node_count, :]
                score = score_dot(query, key_refs[t][...])
                scores.append(score * TO_LOG2 + jnp.concatenate([bias] * (2 * half_heads), axis=0))
            top = functools.reduce(jnp.maximum, scores)
            top = jnp.broadcast_to(jnp.max(top, axis=1, keepdims=True), top.shape)
            gathered = jnp.zeros((seq_rows, 2 * HD), jnp.float32)
            for t in range(depth):
                weight = jnp.exp2(scores[t] - top).astype(jnp.bfloat16)
                value = value_refs[t][...]
                value = jnp.concatenate([value, jnp.ones_like(value)], axis=1)
                gathered = gathered + jnp.dot(weight, value, preferred_element_type=jnp.float32)
            top_s[rows, :] = top
            sum_s[rows, :] = gathered

    def patch(i):
        left = left_of(i)
        slot = lax.rem(i, slots)

        @pl.when(left < BLOCK)
        def _():
            inside = lax.broadcasted_iota(jnp.int32, (BLOCK, HD), 0) < left
            key = cache_s[slot, :, :HD].astype(jnp.float32)
            value = cache_s[slot, :, HD:].astype(jnp.float32)
            key = jnp.where(inside, key, jnp.broadcast_to(key[:1, :], key.shape))
            cache_s[slot, :, :HD] = key.astype(jnp.bfloat16)
            cache_s[slot, :, HD:] = jnp.where(inside, value, 0.0).astype(jnp.bfloat16)

    def score_chunk(seq, slot, sub, c):
        rows = pl.ds(pl.multiple_of(seq * seq_rows, seq_rows), seq_rows)
        at = sub * SUB + c
        score_s[sub][:, c:c + CHUNK] = score_dot(query_s[rows, :], cache_s[slot, at:at + CHUNK, :HD])

    def weigh(seq, slot, part, sub, half, between):
        rows = pl.ds(pl.multiple_of(seq * seq_rows + half * half_rows, half_rows), half_rows)
        here = slice(half * half_rows, (half + 1) * half_rows)
        high = score_s[sub][here, :HD]
        for c in range(HD, SUB, HD):
            high = jnp.maximum(high, score_s[sub][here, c:c + HD])
        high = jnp.broadcast_to(jnp.max(high, axis=1, keepdims=True), high.shape) * TO_LOG2
        old = top_s[rows, :]
        top = jnp.maximum(old, high)
        top_s[rows, :] = top
        factor = jnp.exp2(old - top)
        between[0]()
        tops = wide(top, CHUNK)
        for c in range(0, SUB, CHUNK):
            weight = jnp.exp2(score_s[sub][here, c:c + CHUNK] * TO_LOG2 - tops)
            weight_s[sub][here, c:c + CHUNK] = weight.astype(jnp.bfloat16)
            if c == SUB // 2:
                between[1]()
        keys = slice(sub * SUB, (sub + 1) * SUB)
        value = jnp.concatenate([cache_s[slot, keys, HD:], live_s[part, keys, :]], axis=1)
        sum_s[rows, :] = sum_s[rows, :] * wide(factor, 2 * HD) + jnp.dot(
            weight_s[sub][here, :], value, preferred_element_type=jnp.float32
        )

    def phase(seq, slot, part, sub, next_seq, next_slot):
        ahead = [
            functools.partial(score_chunk, next_seq, next_slot, 1 - sub, c)
            for c in range(0, SUB, CHUNK)
        ]
        weigh(seq, slot, part, sub, 0, ahead[:2])
        weigh(seq, slot, part, sub, 1, ahead[2:])

    @pl.when(total > 0)
    def _():
        fetch(jnp.int32(0)).wait()
        patch(jnp.int32(0))
        seq, _ = place(jnp.int32(0))
        for c in range(0, SUB, CHUNK):
            score_chunk(seq, 0, 0, c)

    @pl.loop(0, total)
    def _(i):
        slot = lax.rem(i, slots)
        more = i + 1 < total

        @pl.when(more)
        def _():
            fetch(i + 1).wait()
            patch(i + 1)

        pl.when(i + 2 < total)(lambda: fetch(i + 2).start())
        seq, _ = place(i)
        left = left_of(i)
        part = jnp.where(left < BLOCK, 1, 0)

        @pl.when(left < BLOCK)
        def _():
            inside = lax.broadcasted_iota(jnp.int32, (BLOCK, HD), 0) < left
            live_s[1] = jnp.where(inside, 1.0, 0.0).astype(jnp.bfloat16)

        next_slot = jnp.where(more, lax.rem(i + 1, slots), slot)
        next_seq, _ = place(jnp.where(more, i + 1, i))
        phase(seq, slot, part, 0, seq, slot)
        phase(seq, slot, part, 1, next_seq, next_slot)

    for b in range(seq_count):
        rows = slice(b * node_count, (b + 1) * node_count)
        for h in range(2 * half_heads):
            row = b * seq_rows + h * node_count
            weight_sum = jnp.maximum(sum_s[row:row + node_count, HD:], 1e-30)
            result = sum_s[row:row + node_count, :HD] / weight_sum
            lse = top_s[row:row + node_count, :] + jnp.log2(weight_sum)
            col = h % half_heads * HD
            if h < half_heads:
                keep_ref[rows, col:col + HD] = result
                keep_lse_ref[rows, col:col + HD] = lse
            else:
                send_ref[rows, col:col + HD] = result
                send_ref[rows, half_heads * HD + col:half_heads * HD + col + HD] = lse


def attend(info, mine, other, keys, values, biases, cache):
    depth = len(keys)
    row_count, width = mine.shape
    seq_count, slot_count = cache.shape[:2]
    all_rows = 2 * width // HD * row_count
    seq_rows = all_rows // seq_count
    vmem = pl.BlockSpec(memory_space=pltpu.VMEM)
    return pl.pallas_call(
        functools.partial(attend_kernel, depth),
        out_shape=(
            jax.ShapeDtypeStruct((row_count, width), jnp.float32),
            jax.ShapeDtypeStruct((row_count, width), jnp.float32),
            jax.ShapeDtypeStruct((row_count, 2 * width), jnp.float32),
        ),
        in_specs=[pl.BlockSpec(memory_space=pltpu.SMEM)]
        + [vmem] * (2 + 3 * depth)
        + [pl.BlockSpec(memory_space=pltpu.HBM)],
        out_specs=(vmem, vmem, vmem),
        scratch_shapes=[
            pltpu.VMEM((all_rows, HD), jnp.bfloat16),
            pltpu.VMEM((seq_rows, SUB), jnp.float32),
            pltpu.VMEM((seq_rows, SUB), jnp.float32),
            pltpu.VMEM((seq_rows, SUB), jnp.bfloat16),
            pltpu.VMEM((seq_rows, SUB), jnp.bfloat16),
            pltpu.VMEM((all_rows, HD), jnp.float32),
            pltpu.VMEM((all_rows, 2 * HD), jnp.float32),
            pltpu.VMEM((3, BLOCK, 2 * HD), jnp.bfloat16),
            pltpu.VMEM((2, BLOCK, HD), jnp.bfloat16),
            pltpu.SemaphoreType.DMA((3,)),
        ],
        compiler_params=pltpu.CompilerParams(vmem_limit_bytes=24 * 1024 * 1024),
        cost_estimate=pl.CostEstimate(
            flops=4 * all_rows * slot_count * HD,
            bytes_accessed=2 * cache.size,
            transcendentals=all_rows * slot_count,
        ),
        name="attend",
    )(
        info, mine, other, *keys, *values, *biases,
        pltpu.with_memory_space_constraint(cache, pltpu.HBM),
    )


STRIP = 256
STRIPS = 4
TILE = 512


def join_kernel(start, side_ref, x_ref, weight_ref, keep_ref, send_ref, x_s, strip_s, total_s, x_sem, sems):
    side = side_ref[0]
    depth = x_s.shape[1]
    columns = total_s.shape[1]
    count = depth // STRIP
    own = 8

    def strip(i):
        slot = lax.rem(i, STRIPS)
        rows = pl.ds(pl.multiple_of(i * STRIP, STRIP), STRIP)
        return pltpu.make_async_copy(
            weight_ref.at[rows, pl.ds(start, columns)], strip_s.at[slot], sems.at[slot]
        )

    x_copy = pltpu.make_async_copy(x_ref, x_s, x_sem)
    x_copy.start()
    for i in range(STRIPS - 1):
        strip(jnp.int32(i)).start()
    total_s[...] = jnp.zeros(total_s.shape, jnp.float32)
    x_copy.wait()

    @pl.loop(0, count)
    def _(i):
        slot = lax.rem(i, STRIPS)
        pl.when(i + STRIPS - 1 < count)(lambda: strip(i + STRIPS - 1).start())
        strip(i).wait()
        x = x_s[:, pl.ds(pl.multiple_of(i * STRIP, STRIP), STRIP)]
        for c in range(0, columns, TILE):
            total_s[:, c:c + TILE] += jnp.dot(
                x, strip_s[slot, :, c:c + TILE], preferred_element_type=jnp.float32
            )

    for block in range(keep_ref.shape[0] // own):
        rows = slice(block * own, (block + 1) * own)
        keep_at = pl.multiple_of(2 * block * own + side * own, own)
        send_at = pl.multiple_of(2 * block * own + (1 - side) * own, own)
        keep_ref[rows, :] = total_s[pl.ds(keep_at, own), :]
        send_ref[rows, :] = total_s[pl.ds(send_at, own), :]


def join(side, x, weight, start, columns):
    rows, depth = x.shape
    out = jax.ShapeDtypeStruct((rows // 2, columns), jnp.float32)
    vmem = pl.BlockSpec(memory_space=pltpu.VMEM)
    return pl.pallas_call(
        functools.partial(join_kernel, start),
        out_shape=(out, out),
        in_specs=[
            pl.BlockSpec(memory_space=pltpu.SMEM),
            pl.BlockSpec(memory_space=pl.ANY),
            pl.BlockSpec(memory_space=pl.ANY),
        ],
        out_specs=(vmem, vmem),
        scratch_shapes=[
            pltpu.VMEM((rows, depth), x.dtype),
            pltpu.VMEM((STRIPS, STRIP, columns), weight.dtype),
            pltpu.VMEM((rows, columns), jnp.float32),
            pltpu.SemaphoreType.DMA,
            pltpu.SemaphoreType.DMA((STRIPS,)),
        ],
        compiler_params=pltpu.CompilerParams(vmem_limit_bytes=32 * 1024 * 1024),
        cost_estimate=pl.CostEstimate(
            flops=2 * rows * depth * columns, bytes_accessed=2 * depth * columns, transcendentals=0
        ),
        name="join",
    )(side[None], x, weight)


CORE, ACROSS, DEEP = range(3)


def bit_of(distance):
    return lax.axis_index("tensor") // (1 << distance) % 2


def fold(x, axis, distance, kind=jnp.bfloat16):
    bit = bit_of(distance)
    keep = lax.dynamic_index_in_dim(x, bit, axis, keepdims=False)
    send = lax.dynamic_index_in_dim(x, 1 - bit, axis, keepdims=False).astype(kind)
    return keep + partner(send, "tensor", distance).astype(jnp.float32)


def unfold(x, axis, distance):
    other = partner(x, "tensor", distance)
    upper = bit_of(distance) == 1
    return jnp.where(upper, jnp.stack([other, x], axis), jnp.stack([x, other], axis))


def depth_index():
    return lax.axis_index("tensor") >> DEEP


def depth_size():
    return lax.axis_size("tensor") >> DEEP


def across_depth(x, k):
    return lax.ppermute(x, "tensor", [(i, i ^ k << DEEP) for i in range(lax.axis_size("tensor"))])


def unfold_depth(x, axis):
    at = depth_index()
    got = [x] + [across_depth(x, k) for k in range(1, depth_size())]
    parts = []
    for place in range(depth_size()):
        part = got[-1]
        for k in range(depth_size() - 1):
            part = jnp.where(at ^ place == k, got[k], part)
        parts.append(part)
    return jnp.stack(parts, axis)


def depth_parts(x):
    at = depth_index()
    parts = [lax.dynamic_index_in_dim(x, at ^ k, 0, keepdims=False) for k in range(depth_size())]
    return parts[0], [part.astype(jnp.bfloat16) for part in parts[1:]]


def sent_down(sends):
    return [across_depth(send, k + 1) for k, send in enumerate(sends)]


def add_all(total, came):
    for part in came:
        total = total + part.astype(jnp.float32)
    return total


def sum_chips(first, second):
    first, second = lax.optimization_barrier((first, second))
    first = fold(first, 1, ACROSS)
    total, sends = depth_parts(first)
    second_total, second_sends = depth_parts(second)
    came, _ = lax.optimization_barrier((sent_down(second_sends), sends))
    second = fold(add_all(second_total, came), 0, ACROSS)
    return jnp.concatenate([add_all(total, sent_down(sends)), second], axis=-1)


def collect(rows, cut):
    first = unfold(unfold_depth(rows[:, :cut], 0), 1, ACROSS)
    second = unfold_depth(unfold(rows[:, cut:], 0, ACROSS), 0)
    both = unfold(jnp.concatenate([first, second], axis=-1), 2, CORE)
    return both.reshape(-1, both.shape[-1])


def local_pairs(
    tapped, join_weight, norm_gain, query_weight, kv_weight, out_weight, kv_cache, lengths, parents
):
    side = (lax.axis_index("tensor") % 2).astype(jnp.int32)
    row_count = tapped.shape[0]
    columns = join_weight.shape[1]
    sum_cut, cut = columns * 11 // 16, columns * 5 // 8
    spans = ((0, sum_cut), (sum_cut, columns))
    seq_count, piece_len = kv_cache.shape[:2]
    node_count = row_count // seq_count
    own_rows = row_count // 16
    row_ids = jnp.arange(row_count, dtype=jnp.int32)
    valid = jnp.clip(lengths - side * piece_len, 0, piece_len)
    info = jnp.concatenate([valid, side[None]]).astype(jnp.int32)
    parent_rows = row_ids // node_count * node_count + parents
    from_row = (parent_rows[:, :, None] == row_ids).astype(jnp.float32)
    hops = {}
    for step in range(STEPS):
        hops[step, step] = jnp.eye(row_count, dtype=jnp.float32)
        for earlier in range(step - 1, -1, -1):
            hops[step, earlier] = jnp.dot(hops[step, earlier + 1], from_row[earlier])
    bias = {at: (hop - 1.0) * -floor_score for at, hop in hops.items()}

    folded = []
    for start, end in spans:
        kept, sent = join(side, tapped, join_weight, start, end - start)
        part = kept + partner(sent, "tensor", CORE)
        folded.append(part.reshape(-1, 2, own_rows, end - start))
    hidden = sum_chips(*folded)

    keys, values = [], []
    for step in range(STEPS):
        normed = collect(normalize(hidden, norm_gain), cut)
        new_kv = jnp.dot(normed, kv_weight, preferred_element_type=jnp.float32)
        new_kv = new_kv.astype(jnp.bfloat16)
        query = jnp.dot(normed, query_weight, preferred_element_type=jnp.float32)
        query = query.astype(jnp.bfloat16)
        keys.append(partner(new_kv, "tensor", CORE))
        values.append(new_kv)
        kept, kept_lse, sent = attend(
            info, query, partner(query, "tensor", CORE), keys, values,
            [bias[step, t] for t in range(step + 1)], kv_cache,
        )
        came = partner(sent, "tensor", CORE)
        width = kept.shape[1]
        top = jnp.maximum(kept_lse, came[:, width:])
        mine = jnp.exp2(kept_lse - top)
        theirs = jnp.exp2(came[:, width:] - top)
        attended = (mine * kept + theirs * came[:, :width]) / (mine + theirs)
        update = jnp.dot(
            attended.astype(jnp.bfloat16), out_weight, preferred_element_type=jnp.float32
        ).reshape(-1, 2, 2, own_rows, columns)
        update = fold(update, 2, CORE)
        hidden = hidden + sum_chips(*[update[..., start:end] for start, end in spans])
    return hidden


def solution(mesh):
    body = local_pairs if mesh.shape["tensor"] == 2 * KVH else local_general
    placed = (
        P("groups", "tensor"),
        P("tensor", None),
        P(),
        P(None, "tensor"),
        P(None, "tensor"),
        P("tensor", None),
        P("groups", "tensor", None),
        P("groups"),
        P(None, "groups"),
    )
    return jax.shard_map(
        body, mesh=mesh, in_specs=placed, out_specs=P(("groups", "tensor"), None), check_vma=False
    )
```

```python
import functools
import math

import jax
import jax.numpy as jnp
from jax import lax
from jax.experimental import pallas as pl
from jax.experimental.pallas import tpu as pltpu
from jax.sharding import PartitionSpec as P

KVH = 8
HD = 128
QPK = 8
STEPS = 3


epsilon = 1e-05
floor_score = -1e30


def partner(x, axis, distance):
    return lax.ppermute(x, axis, [(i, i ^ 1 << distance) for i in range(lax.axis_size(axis))])


def as_sent(x):

    def short(part):
        return part.astype(jnp.bfloat16) if part.dtype == jnp.float32 else part

    return jax.tree.map(short, x)


def normalize(values, norm_gain):
    mean_square = jnp.mean(values * values, axis=-1, keepdims=True)
    return (values * lax.rsqrt(mean_square + epsilon) * norm_gain).astype(jnp.bfloat16)


def merge_parts(mine, theirs):
    row_top = jnp.maximum(mine[0], theirs[0])
    mine_factor = jnp.exp(mine[0] - row_top)
    their_factor = jnp.exp(theirs[0] - row_top)
    row_sum = mine_factor * mine[1] + their_factor * theirs[1]
    numerator = mine_factor[..., None] * mine[2] + their_factor[..., None] * theirs[2]
    return (row_top, row_sum, numerator)


def local_general(
    tapped, join_weight, norm_gain, query_weight, kv_weight, out_weight, kv_cache, lengths, parents
):
    tensor_size = lax.axis_size("tensor")
    device = lax.axis_index("tensor")
    group_size = tensor_size // KVH
    hop_count = group_size.bit_length() - 1
    piece_index = device % group_size
    row_count_all = tapped.shape[0]
    seq_count = kv_cache.shape[0]
    node_count = row_count_all // seq_count
    query_cols = query_weight.shape[1]
    proj_weight = jnp.concatenate([query_weight, kv_weight], axis=1)
    score_scale = 1.0 / math.sqrt(HD)
    hidden_rows = lax.psum_scatter(
        jnp.dot(tapped, join_weight, preferred_element_type=jnp.float32),
        "tensor",
        scatter_dimension=0,
        tiled=True,
    )
    piece_len = kv_cache.shape[1]
    positions = piece_index * piece_len + jnp.arange(piece_len, dtype=jnp.int32)
    visible = positions[None, :] < lengths[:, None]
    is_first = piece_index == 0
    keys_cache = kv_cache[:, :, :HD]
    values_cache = kv_cache[:, :, HD:]
    row_ids = jnp.arange(row_count_all, dtype=jnp.int32)
    seq_base = row_ids // node_count * node_count
    head_rows = node_count * QPK
    width = out_weight.shape[0]
    history = []
    for step_num in range(STEPS):
        projected = jnp.dot(
            lax.all_gather(normalize(hidden_rows, norm_gain), "tensor", axis=0, tiled=True),
            proj_weight,
            preferred_element_type=jnp.float32,
        ).astype(jnp.bfloat16)
        query_group = projected[:, :query_cols]
        kv_group = projected[:, query_cols:]
        for bit_num in range(hop_count):
            other_query, other_kv = partner((query_group, kv_group), "tensor", bit_num)
            is_upper = device // (1 << bit_num) % 2 == 1
            query_group = jnp.where(
                is_upper,
                jnp.concatenate([other_query, query_group], axis=1),
                jnp.concatenate([query_group, other_query], axis=1),
            )
            kv_group = jnp.where(
                is_upper,
                jnp.concatenate([other_kv, kv_group], axis=1),
                jnp.concatenate([kv_group, other_kv], axis=1),
            )
        history.append(kv_group)
        ancestors = [row_ids]
        current = row_ids
        for earlier in range(step_num - 1, -1, -1):
            current = seq_base + jnp.take(parents[earlier], current, axis=0)
            ancestors.insert(0, current)
        new_depth = step_num + 1
        new_kv = jnp.stack(
            [
                jnp.take(history[earlier], ancestors[earlier], axis=0)
                for earlier in range(new_depth)
            ],
            axis=1,
        )
        new_keys = new_kv[..., :HD].reshape(seq_count, node_count, new_depth, HD)
        new_values = new_kv[..., HD:].reshape(seq_count, node_count, new_depth, HD)
        query_blocks = query_group.reshape(seq_count, head_rows, HD)
        scores = (
            jnp.einsum("brd,bcd->brc", query_blocks, keys_cache, preferred_element_type=jnp.float32)
            * score_scale
        )
        scores = jnp.where(visible[:, None, :], scores, floor_score)
        query_nodes = query_group.reshape(seq_count, node_count, QPK, HD)
        new_scores = (
            jnp.einsum("bnqd,bntd->bnqt", query_nodes, new_keys, preferred_element_type=jnp.float32)
            * score_scale
        )
        new_scores = jnp.where(is_first, new_scores, floor_score)
        row_top = jnp.maximum(
            jnp.max(scores, axis=-1), jnp.max(new_scores, axis=-1).reshape(seq_count, head_rows)
        )
        weights = jnp.where(visible[:, None, :], jnp.exp(scores - row_top[..., None]), 0.0)
        top_nodes = row_top.reshape(seq_count, node_count, QPK)
        new_weights = jnp.where(is_first, jnp.exp(new_scores - top_nodes[..., None]), 0.0)
        row_sum = jnp.sum(weights, axis=-1) + jnp.sum(new_weights, axis=-1).reshape(
            seq_count, head_rows
        )
        numerator = jnp.einsum(
            "brc,bcd->brd",
            weights.astype(jnp.bfloat16),
            values_cache,
            preferred_element_type=jnp.float32,
        )
        new_part = jnp.einsum(
            "bnqt,bntd->bnqd",
            new_weights.astype(jnp.bfloat16),
            new_values,
            preferred_element_type=jnp.float32,
        )
        numerator = numerator + new_part.reshape(seq_count, head_rows, HD)
        partial_value = (row_top, row_sum, numerator)
        for bit_num in range(hop_count):
            theirs = partner(
                (as_sent(partial_value[0]), as_sent(partial_value[1]), as_sent(partial_value[2])),
                "tensor",
                bit_num,
            )
            partial_value = merge_parts(partial_value, theirs)
        attended = (
            (partial_value[2] / partial_value[1][..., None])
            .astype(jnp.bfloat16)
            .reshape(row_count_all, QPK * HD)
        )
        attended_mine = lax.dynamic_slice_in_dim(attended, piece_index * width, width, 1)
        hidden_rows = hidden_rows + lax.psum_scatter(
            jnp.dot(attended_mine, out_weight, preferred_element_type=jnp.float32),
            "tensor",
            scatter_dimension=0,
            tiled=True,
        )
    return hidden_rows


BLOCK = 2048
SUB = BLOCK // 2
CHUNK = 256
TO_LOG2 = math.log2(math.e) / math.sqrt(HD)


def score_dot(query, key):
    return lax.dot_general(
        query, key, (((1,), (1,)), ((), ())), preferred_element_type=jnp.float32
    )


def wide(x, width):
    return jnp.concatenate([x] * (width // HD), axis=1)


def attend_kernel(depth, info_ref, mine_ref, other_ref, *refs):
    key_refs, value_refs, bias_refs = refs[:depth], refs[depth:2 * depth], refs[2 * depth:3 * depth]
    cache_ref, keep_ref, keep_lse_ref, send_ref, query_s = refs[3 * depth:3 * depth + 5]
    score_s, weight_s = refs[3 * depth + 5:3 * depth + 7], refs[3 * depth + 7:3 * depth + 9]
    top_s, sum_s, cache_s, live_s, sems = refs[3 * depth + 9:]
    seq_count = cache_ref.shape[0]
    node_count = mine_ref.shape[0] // seq_count
    half_heads = mine_ref.shape[1] // HD
    seq_rows = 2 * half_heads * node_count
    half_rows = seq_rows // 2
    slots = cache_s.shape[0]
    steps = [lax.div(info_ref[b] + BLOCK - 1, BLOCK) for b in range(seq_count)]
    total = sum(steps)

    def place(i):
        seq = jnp.int32(0)
        block = i
        for b in range(seq_count - 1):
            later = jnp.logical_and(block >= steps[b], seq == b)
            seq = jnp.where(later, b + 1, seq)
            block = jnp.where(later, block - steps[b], block)
        return seq, block

    def left_of(i):
        seq, block = place(i)
        return info_ref[seq] - block * BLOCK

    def fetch(i):
        seq, block = place(i)
        slot = lax.rem(i, slots)
        start = pl.multiple_of(block * BLOCK, BLOCK)
        return pltpu.make_async_copy(
            cache_ref.at[seq, pl.ds(start, BLOCK), :], cache_s.at[slot], sems.at[slot]
        )

    for i in range(2):
        pl.when(i < total)(lambda i=i: fetch(jnp.int32(i)).start())

    for b in range(seq_count):
        rows = slice(b * node_count, (b + 1) * node_count)
        for h in range(2 * half_heads):
            ref = mine_ref if h < half_heads else other_ref
            col = h % half_heads * HD
            row = b * seq_rows + h * node_count
            query_s[row:row + node_count, :] = ref[rows, col:col + HD]
    live_s[0] = jnp.ones((BLOCK, HD), jnp.bfloat16)

    @pl.when(info_ref[seq_count] == 0)
    def _():
        top_s[...] = jnp.full(top_s.shape, floor_score, jnp.float32)
        sum_s[...] = jnp.zeros(sum_s.shape, jnp.float32)

    @pl.when(info_ref[seq_count] != 0)
    def _():
        for b in range(seq_count):
            rows = slice(b * seq_rows, (b + 1) * seq_rows)
            query = query_s[rows, :]
            scores = []
            for t in range(depth):
                bias = bias_refs[t][b * node_count:(b + 1) * node_count, :]
                score = score_dot(query, key_refs[t][...])
                scores.append(score * TO_LOG2 + jnp.concatenate([bias] * (2 * half_heads), axis=0))
            top = functools.reduce(jnp.maximum, scores)
            top = jnp.broadcast_to(jnp.max(top, axis=1, keepdims=True), top.shape)
            gathered = jnp.zeros((seq_rows, 2 * HD), jnp.float32)
            for t in range(depth):
                weight = jnp.exp2(scores[t] - top).astype(jnp.bfloat16)
                value = value_refs[t][...]
                value = jnp.concatenate([value, jnp.ones_like(value)], axis=1)
                gathered = gathered + jnp.dot(weight, value, preferred_element_type=jnp.float32)
            top_s[rows, :] = top
            sum_s[rows, :] = gathered

    def patch(i):
        left = left_of(i)
        slot = lax.rem(i, slots)

        @pl.when(left < BLOCK)
        def _():
            inside = lax.broadcasted_iota(jnp.int32, (BLOCK, HD), 0) < left
            key = cache_s[slot, :, :HD].astype(jnp.float32)
            value = cache_s[slot, :, HD:].astype(jnp.float32)
            key = jnp.where(inside, key, jnp.broadcast_to(key[:1, :], key.shape))
            cache_s[slot, :, :HD] = key.astype(jnp.bfloat16)
            cache_s[slot, :, HD:] = jnp.where(inside, value, 0.0).astype(jnp.bfloat16)

    def score_chunk(seq, slot, sub, c):
        rows = pl.ds(pl.multiple_of(seq * seq_rows, seq_rows), seq_rows)
        at = sub * SUB + c
        score_s[sub][:, c:c + CHUNK] = score_dot(query_s[rows, :], cache_s[slot, at:at + CHUNK, :HD])

    def weigh(seq, slot, part, sub, half, between):
        rows = pl.ds(pl.multiple_of(seq * seq_rows + half * half_rows, half_rows), half_rows)
        here = slice(half * half_rows, (half + 1) * half_rows)
        high = score_s[sub][here, :HD]
        for c in range(HD, SUB, HD):
            high = jnp.maximum(high, score_s[sub][here, c:c + HD])
        high = jnp.broadcast_to(jnp.max(high, axis=1, keepdims=True), high.shape) * TO_LOG2
        old = top_s[rows, :]
        top = jnp.maximum(old, high)
        top_s[rows, :] = top
        factor = jnp.exp2(old - top)
        between[0]()
        tops = wide(top, CHUNK)
        for c in range(0, SUB, CHUNK):
            weight = jnp.exp2(score_s[sub][here, c:c + CHUNK] * TO_LOG2 - tops)
            weight_s[sub][here, c:c + CHUNK] = weight.astype(jnp.bfloat16)
            if c == SUB // 2:
                between[1]()
        keys = slice(sub * SUB, (sub + 1) * SUB)
        value = jnp.concatenate([cache_s[slot, keys, HD:], live_s[part, keys, :]], axis=1)
        sum_s[rows, :] = sum_s[rows, :] * wide(factor, 2 * HD) + jnp.dot(
            weight_s[sub][here, :], value, preferred_element_type=jnp.float32
        )

    def phase(seq, slot, part, sub, next_seq, next_slot):
        ahead = [
            functools.partial(score_chunk, next_seq, next_slot, 1 - sub, c)
            for c in range(0, SUB, CHUNK)
        ]
        weigh(seq, slot, part, sub, 0, ahead[:2])
        weigh(seq, slot, part, sub, 1, ahead[2:])

    @pl.when(total > 0)
    def _():
        fetch(jnp.int32(0)).wait()
        patch(jnp.int32(0))
        seq, _ = place(jnp.int32(0))
        for c in range(0, SUB, CHUNK):
            score_chunk(seq, 0, 0, c)

    @pl.loop(0, total)
    def _(i):
        slot = lax.rem(i, slots)
        more = i + 1 < total

        @pl.when(more)
        def _():
            fetch(i + 1).wait()
            patch(i + 1)

        pl.when(i + 2 < total)(lambda: fetch(i + 2).start())
        seq, _ = place(i)
        left = left_of(i)
        part = jnp.where(left < BLOCK, 1, 0)

        @pl.when(left < BLOCK)
        def _():
            inside = lax.broadcasted_iota(jnp.int32, (BLOCK, HD), 0) < left
            live_s[1] = jnp.where(inside, 1.0, 0.0).astype(jnp.bfloat16)

        next_slot = jnp.where(more, lax.rem(i + 1, slots), slot)
        next_seq, _ = place(jnp.where(more, i + 1, i))
        phase(seq, slot, part, 0, seq, slot)
        phase(seq, slot, part, 1, next_seq, next_slot)

    for b in range(seq_count):
        rows = slice(b * node_count, (b + 1) * node_count)
        for h in range(2 * half_heads):
            row = b * seq_rows + h * node_count
            weight_sum = jnp.maximum(sum_s[row:row + node_count, HD:], 1e-30)
            result = sum_s[row:row + node_count, :HD] / weight_sum
            lse = top_s[row:row + node_count, :] + jnp.log2(weight_sum)
            col = h % half_heads * HD
            if h < half_heads:
                keep_ref[rows, col:col + HD] = result
                keep_lse_ref[rows, col:col + HD] = lse
            else:
                send_ref[rows, col:col + HD] = result
                send_ref[rows, half_heads * HD + col:half_heads * HD + col + HD] = lse


def attend(info, mine, other, keys, values, biases, cache):
    depth = len(keys)
    row_count, width = mine.shape
    seq_count, slot_count = cache.shape[:2]
    all_rows = 2 * width // HD * row_count
    seq_rows = all_rows // seq_count
    vmem = pl.BlockSpec(memory_space=pltpu.VMEM)
    return pl.pallas_call(
        functools.partial(attend_kernel, depth),
        out_shape=(
            jax.ShapeDtypeStruct((row_count, width), jnp.float32),
            jax.ShapeDtypeStruct((row_count, width), jnp.float32),
            jax.ShapeDtypeStruct((row_count, 2 * width), jnp.float32),
        ),
        in_specs=[pl.BlockSpec(memory_space=pltpu.SMEM)]
        + [vmem] * (2 + 3 * depth)
        + [pl.BlockSpec(memory_space=pltpu.HBM)],
        out_specs=(vmem, vmem, vmem),
        scratch_shapes=[
            pltpu.VMEM((all_rows, HD), jnp.bfloat16),
            pltpu.VMEM((seq_rows, SUB), jnp.float32),
            pltpu.VMEM((seq_rows, SUB), jnp.float32),
            pltpu.VMEM((seq_rows, SUB), jnp.bfloat16),
            pltpu.VMEM((seq_rows, SUB), jnp.bfloat16),
            pltpu.VMEM((all_rows, HD), jnp.float32),
            pltpu.VMEM((all_rows, 2 * HD), jnp.float32),
            pltpu.VMEM((3, BLOCK, 2 * HD), jnp.bfloat16),
            pltpu.VMEM((2, BLOCK, HD), jnp.bfloat16),
            pltpu.SemaphoreType.DMA((3,)),
        ],
        compiler_params=pltpu.CompilerParams(vmem_limit_bytes=18 * 1024 * 1024),
        cost_estimate=pl.CostEstimate(
            flops=4 * all_rows * slot_count * HD,
            bytes_accessed=2 * cache.size,
            transcendentals=all_rows * slot_count,
        ),
        name="attend",
    )(
        info, mine, other, *keys, *values, *biases,
        pltpu.with_memory_space_constraint(cache, pltpu.HBM),
    )


STRIP = 256
STRIPS = 3
TILE = 512


def join_kernel(start, side_ref, x_ref, weight_ref, keep_ref, send_ref, x_s, strip_s, total_s, x_sem, sems):
    side = side_ref[0]
    depth = x_s.shape[1]
    columns = total_s.shape[1]
    count = depth // STRIP
    own = 8

    def strip(i):
        slot = lax.rem(i, STRIPS)
        rows = pl.ds(pl.multiple_of(i * STRIP, STRIP), STRIP)
        return pltpu.make_async_copy(
            weight_ref.at[rows, pl.ds(start, columns)], strip_s.at[slot], sems.at[slot]
        )

    x_copy = pltpu.make_async_copy(x_ref, x_s, x_sem)
    x_copy.start()
    for i in range(STRIPS - 1):
        strip(jnp.int32(i)).start()
    total_s[...] = jnp.zeros(total_s.shape, jnp.float32)
    x_copy.wait()

    @pl.loop(0, count)
    def _(i):
        slot = lax.rem(i, STRIPS)
        pl.when(i + STRIPS - 1 < count)(lambda: strip(i + STRIPS - 1).start())
        strip(i).wait()
        x = x_s[:, pl.ds(pl.multiple_of(i * STRIP, STRIP), STRIP)]
        for c in range(0, columns, TILE):
            total_s[:, c:c + TILE] += jnp.dot(
                x, strip_s[slot, :, c:c + TILE], preferred_element_type=jnp.float32
            )

    for block in range(keep_ref.shape[0] // own):
        rows = slice(block * own, (block + 1) * own)
        keep_at = pl.multiple_of(2 * block * own + side * own, own)
        send_at = pl.multiple_of(2 * block * own + (1 - side) * own, own)
        keep_ref[rows, :] = total_s[pl.ds(keep_at, own), :]
        send_ref[rows, :] = total_s[pl.ds(send_at, own), :]


def join(side, x, weight, start, columns):
    rows, depth = x.shape
    out = jax.ShapeDtypeStruct((rows // 2, columns), jnp.float32)
    vmem = pl.BlockSpec(memory_space=pltpu.VMEM)
    return pl.pallas_call(
        functools.partial(join_kernel, start),
        out_shape=(out, out),
        in_specs=[
            pl.BlockSpec(memory_space=pltpu.SMEM),
            pl.BlockSpec(memory_space=pl.ANY),
            pl.BlockSpec(memory_space=pl.ANY),
        ],
        out_specs=(vmem, vmem),
        scratch_shapes=[
            pltpu.VMEM((rows, depth), x.dtype),
            pltpu.VMEM((STRIPS, STRIP, columns), weight.dtype),
            pltpu.VMEM((rows, columns), jnp.float32),
            pltpu.SemaphoreType.DMA,
            pltpu.SemaphoreType.DMA((STRIPS,)),
        ],
        compiler_params=pltpu.CompilerParams(vmem_limit_bytes=20 * 1024 * 1024),
        cost_estimate=pl.CostEstimate(
            flops=2 * rows * depth * columns, bytes_accessed=2 * depth * columns, transcendentals=0
        ),
        name="join",
    )(side[None], x, weight)


CORE, ACROSS, DEEP = range(3)


def bit_of(distance):
    return lax.axis_index("tensor") // (1 << distance) % 2


def fold(x, axis, distance, kind=jnp.bfloat16):
    bit = bit_of(distance)
    keep = lax.dynamic_index_in_dim(x, bit, axis, keepdims=False)
    send = lax.dynamic_index_in_dim(x, 1 - bit, axis, keepdims=False).astype(kind)
    return keep + partner(send, "tensor", distance).astype(jnp.float32)


def unfold(x, axis, distance):
    other = partner(x, "tensor", distance)
    upper = bit_of(distance) == 1
    return jnp.where(upper, jnp.stack([other, x], axis), jnp.stack([x, other], axis))


def depth_index():
    return lax.axis_index("tensor") >> DEEP


def depth_size():
    return lax.axis_size("tensor") >> DEEP


def across_depth(x, k):
    return lax.ppermute(x, "tensor", [(i, i ^ k << DEEP) for i in range(lax.axis_size("tensor"))])


def unfold_depth(x, axis):
    at = depth_index()
    got = [x] + [across_depth(x, k) for k in range(1, depth_size())]
    parts = []
    for place in range(depth_size()):
        part = got[-1]
        for k in range(depth_size() - 1):
            part = jnp.where(at ^ place == k, got[k], part)
        parts.append(part)
    return jnp.stack(parts, axis)


def depth_parts(x):
    at = depth_index()
    parts = [lax.dynamic_index_in_dim(x, at ^ k, 0, keepdims=False) for k in range(depth_size())]
    return parts[0], [part.astype(jnp.bfloat16) for part in parts[1:]]


def sent_down(sends):
    return [across_depth(send, k + 1) for k, send in enumerate(sends)]


def add_all(total, came):
    for part in came:
        total = total + part.astype(jnp.float32)
    return total


def sum_chips(first, second):
    first, second = lax.optimization_barrier((first, second))
    first = fold(first, 1, ACROSS)
    total, sends = depth_parts(first)
    second_total, second_sends = depth_parts(second)
    came, _ = lax.optimization_barrier((sent_down(second_sends), sends))
    second = fold(add_all(second_total, came), 0, ACROSS)
    return jnp.concatenate([add_all(total, sent_down(sends)), second], axis=-1)


def collect(rows, cut):
    first = unfold(unfold_depth(rows[:, :cut], 0), 1, ACROSS)
    second = unfold_depth(unfold(rows[:, cut:], 0, ACROSS), 0)
    both = unfold(jnp.concatenate([first, second], axis=-1), 2, CORE)
    return both.reshape(-1, both.shape[-1])


def local_pairs(
    tapped, join_weight, norm_gain, query_weight, kv_weight, out_weight, kv_cache, lengths, parents
):
    side = (lax.axis_index("tensor") % 2).astype(jnp.int32)
    row_count = tapped.shape[0]
    columns = join_weight.shape[1]
    sum_cut, cut = columns * 11 // 16, columns * 5 // 8
    spans = ((0, sum_cut), (sum_cut, columns))
    seq_count, piece_len = kv_cache.shape[:2]
    node_count = row_count // seq_count
    own_rows = row_count // 16
    row_ids = jnp.arange(row_count, dtype=jnp.int32)
    valid = jnp.clip(lengths - side * piece_len, 0, piece_len)
    info = jnp.concatenate([valid, side[None]]).astype(jnp.int32)
    parent_rows = row_ids // node_count * node_count + parents
    from_row = (parent_rows[:, :, None] == row_ids).astype(jnp.float32)
    hops = {}
    for step in range(STEPS):
        hops[step, step] = jnp.eye(row_count, dtype=jnp.float32)
        for earlier in range(step - 1, -1, -1):
            hops[step, earlier] = jnp.dot(hops[step, earlier + 1], from_row[earlier])
    bias = {at: (hop - 1.0) * -floor_score for at, hop in hops.items()}

    folded = []
    for start, end in spans:
        kept, sent = join(side, tapped, join_weight, start, end - start)
        part = kept + partner(sent, "tensor", CORE)
        folded.append(part.reshape(-1, 2, own_rows, end - start))
    hidden = sum_chips(*folded)

    keys, values = [], []
    for step in range(STEPS):
        normed = collect(normalize(hidden, norm_gain), cut)
        new_kv = jnp.dot(normed, kv_weight, preferred_element_type=jnp.float32)
        new_kv = new_kv.astype(jnp.bfloat16)
        query = jnp.dot(normed, query_weight, preferred_element_type=jnp.float32)
        query = query.astype(jnp.bfloat16)
        keys.append(partner(new_kv, "tensor", CORE))
        values.append(new_kv)
        kept, kept_lse, sent = attend(
            info, query, partner(query, "tensor", CORE), keys, values,
            [bias[step, t] for t in range(step + 1)], kv_cache,
        )
        came = partner(sent, "tensor", CORE)
        width = kept.shape[1]
        top = jnp.maximum(kept_lse, came[:, width:])
        mine = jnp.exp2(kept_lse - top)
        theirs = jnp.exp2(came[:, width:] - top)
        attended = (mine * kept + theirs * came[:, :width]) / (mine + theirs)
        update = jnp.dot(
            attended.astype(jnp.bfloat16), out_weight, preferred_element_type=jnp.float32
        ).reshape(-1, 2, 2, own_rows, columns)
        update = fold(update, 2, CORE)
        hidden = hidden + sum_chips(*[update[..., start:end] for start, end in spans])
    return hidden


def solution(mesh):
    body = local_pairs if mesh.shape["tensor"] == 2 * KVH else local_general
    placed = (
        P("groups", "tensor"),
        P("tensor", None),
        P(),
        P(None, "tensor"),
        P(None, "tensor"),
        P("tensor", None),
        P("groups", "tensor", None),
        P("groups"),
        P(None, "groups"),
    )
    return jax.shard_map(
        body, mesh=mesh, in_specs=placed, out_specs=P(("groups", "tensor"), None), check_vma=False
    )
```

```python
import functools
import math

import jax
import jax.numpy as jnp
from jax import lax
from jax.experimental import pallas as pl
from jax.experimental.pallas import tpu as pltpu
from jax.sharding import PartitionSpec as P

KVH = 8
HD = 128
QPK = 8
STEPS = 3


epsilon = 1e-05
floor_score = -1e30


def partner(x, axis, distance):
    return lax.ppermute(x, axis, [(i, i ^ 1 << distance) for i in range(lax.axis_size(axis))])


def as_sent(x):

    def short(part):
        return part.astype(jnp.bfloat16) if part.dtype == jnp.float32 else part

    return jax.tree.map(short, x)


def normalize(values, norm_gain):
    mean_square = jnp.mean(values * values, axis=-1, keepdims=True)
    return (values * lax.rsqrt(mean_square + epsilon) * norm_gain).astype(jnp.bfloat16)


def merge_parts(mine, theirs):
    row_top = jnp.maximum(mine[0], theirs[0])
    mine_factor = jnp.exp(mine[0] - row_top)
    their_factor = jnp.exp(theirs[0] - row_top)
    row_sum = mine_factor * mine[1] + their_factor * theirs[1]
    numerator = mine_factor[..., None] * mine[2] + their_factor[..., None] * theirs[2]
    return (row_top, row_sum, numerator)


def local_general(
    tapped, join_weight, norm_gain, query_weight, kv_weight, out_weight, kv_cache, lengths, parents
):
    tensor_size = lax.axis_size("tensor")
    device = lax.axis_index("tensor")
    group_size = tensor_size // KVH
    hop_count = group_size.bit_length() - 1
    piece_index = device % group_size
    row_count_all = tapped.shape[0]
    seq_count = kv_cache.shape[0]
    node_count = row_count_all // seq_count
    query_cols = query_weight.shape[1]
    proj_weight = jnp.concatenate([query_weight, kv_weight], axis=1)
    score_scale = 1.0 / math.sqrt(HD)
    hidden_rows = lax.psum_scatter(
        jnp.dot(tapped, join_weight, preferred_element_type=jnp.float32),
        "tensor",
        scatter_dimension=0,
        tiled=True,
    )
    piece_len = kv_cache.shape[1]
    positions = piece_index * piece_len + jnp.arange(piece_len, dtype=jnp.int32)
    visible = positions[None, :] < lengths[:, None]
    is_first = piece_index == 0
    keys_cache = kv_cache[:, :, :HD]
    values_cache = kv_cache[:, :, HD:]
    row_ids = jnp.arange(row_count_all, dtype=jnp.int32)
    seq_base = row_ids // node_count * node_count
    head_rows = node_count * QPK
    width = out_weight.shape[0]
    history = []
    for step_num in range(STEPS):
        projected = jnp.dot(
            lax.all_gather(normalize(hidden_rows, norm_gain), "tensor", axis=0, tiled=True),
            proj_weight,
            preferred_element_type=jnp.float32,
        ).astype(jnp.bfloat16)
        query_group = projected[:, :query_cols]
        kv_group = projected[:, query_cols:]
        for bit_num in range(hop_count):
            other_query, other_kv = partner((query_group, kv_group), "tensor", bit_num)
            is_upper = device // (1 << bit_num) % 2 == 1
            query_group = jnp.where(
                is_upper,
                jnp.concatenate([other_query, query_group], axis=1),
                jnp.concatenate([query_group, other_query], axis=1),
            )
            kv_group = jnp.where(
                is_upper,
                jnp.concatenate([other_kv, kv_group], axis=1),
                jnp.concatenate([kv_group, other_kv], axis=1),
            )
        history.append(kv_group)
        ancestors = [row_ids]
        current = row_ids
        for earlier in range(step_num - 1, -1, -1):
            current = seq_base + jnp.take(parents[earlier], current, axis=0)
            ancestors.insert(0, current)
        new_depth = step_num + 1
        new_kv = jnp.stack(
            [
                jnp.take(history[earlier], ancestors[earlier], axis=0)
                for earlier in range(new_depth)
            ],
            axis=1,
        )
        new_keys = new_kv[..., :HD].reshape(seq_count, node_count, new_depth, HD)
        new_values = new_kv[..., HD:].reshape(seq_count, node_count, new_depth, HD)
        query_blocks = query_group.reshape(seq_count, head_rows, HD)
        scores = (
            jnp.einsum("brd,bcd->brc", query_blocks, keys_cache, preferred_element_type=jnp.float32)
            * score_scale
        )
        scores = jnp.where(visible[:, None, :], scores, floor_score)
        query_nodes = query_group.reshape(seq_count, node_count, QPK, HD)
        new_scores = (
            jnp.einsum("bnqd,bntd->bnqt", query_nodes, new_keys, preferred_element_type=jnp.float32)
            * score_scale
        )
        new_scores = jnp.where(is_first, new_scores, floor_score)
        row_top = jnp.maximum(
            jnp.max(scores, axis=-1), jnp.max(new_scores, axis=-1).reshape(seq_count, head_rows)
        )
        weights = jnp.where(visible[:, None, :], jnp.exp(scores - row_top[..., None]), 0.0)
        top_nodes = row_top.reshape(seq_count, node_count, QPK)
        new_weights = jnp.where(is_first, jnp.exp(new_scores - top_nodes[..., None]), 0.0)
        row_sum = jnp.sum(weights, axis=-1) + jnp.sum(new_weights, axis=-1).reshape(
            seq_count, head_rows
        )
        numerator = jnp.einsum(
            "brc,bcd->brd",
            weights.astype(jnp.bfloat16),
            values_cache,
            preferred_element_type=jnp.float32,
        )
        new_part = jnp.einsum(
            "bnqt,bntd->bnqd",
            new_weights.astype(jnp.bfloat16),
            new_values,
            preferred_element_type=jnp.float32,
        )
        numerator = numerator + new_part.reshape(seq_count, head_rows, HD)
        partial_value = (row_top, row_sum, numerator)
        for bit_num in range(hop_count):
            theirs = partner(
                (as_sent(partial_value[0]), as_sent(partial_value[1]), as_sent(partial_value[2])),
                "tensor",
                bit_num,
            )
            partial_value = merge_parts(partial_value, theirs)
        attended = (
            (partial_value[2] / partial_value[1][..., None])
            .astype(jnp.bfloat16)
            .reshape(row_count_all, QPK * HD)
        )
        attended_mine = lax.dynamic_slice_in_dim(attended, piece_index * width, width, 1)
        hidden_rows = hidden_rows + lax.psum_scatter(
            jnp.dot(attended_mine, out_weight, preferred_element_type=jnp.float32),
            "tensor",
            scatter_dimension=0,
            tiled=True,
        )
    return hidden_rows


BLOCK = 2048
SUB = BLOCK // 2
CHUNK = 256
TO_LOG2 = math.log2(math.e) / math.sqrt(HD)


def score_dot(query, key):
    return lax.dot_general(
        query, key, (((1,), (1,)), ((), ())), preferred_element_type=jnp.float32
    )


def wide(x, width):
    return jnp.concatenate([x] * (width // HD), axis=1)


def attend_kernel(depth, info_ref, mine_ref, other_ref, *refs):
    key_refs, value_refs, bias_refs = refs[:depth], refs[depth:2 * depth], refs[2 * depth:3 * depth]
    cache_ref, keep_ref, keep_lse_ref, send_ref, query_s = refs[3 * depth:3 * depth + 5]
    score_s, weight_s = refs[3 * depth + 5:3 * depth + 7], refs[3 * depth + 7:3 * depth + 9]
    top_s, sum_s, cache_s, live_s, sems = refs[3 * depth + 9:]
    seq_count = cache_ref.shape[0]
    node_count = mine_ref.shape[0] // seq_count
    half_heads = mine_ref.shape[1] // HD
    seq_rows = 2 * half_heads * node_count
    half_rows = seq_rows // 2
    slots = cache_s.shape[0]
    steps = [lax.div(info_ref[b] + BLOCK - 1, BLOCK) for b in range(seq_count)]
    total = sum(steps)

    def place(i):
        seq = jnp.int32(0)
        block = i
        for b in range(seq_count - 1):
            later = jnp.logical_and(block >= steps[b], seq == b)
            seq = jnp.where(later, b + 1, seq)
            block = jnp.where(later, block - steps[b], block)
        return seq, block

    def left_of(i):
        seq, block = place(i)
        return info_ref[seq] - block * BLOCK

    def fetch(i):
        seq, block = place(i)
        slot = lax.rem(i, slots)
        start = pl.multiple_of(block * BLOCK, BLOCK)
        return pltpu.make_async_copy(
            cache_ref.at[seq, pl.ds(start, BLOCK), :], cache_s.at[slot], sems.at[slot]
        )

    for i in range(2):
        pl.when(i < total)(lambda i=i: fetch(jnp.int32(i)).start())

    for b in range(seq_count):
        rows = slice(b * node_count, (b + 1) * node_count)
        for h in range(2 * half_heads):
            ref = mine_ref if h < half_heads else other_ref
            col = h % half_heads * HD
            row = b * seq_rows + h * node_count
            query_s[row:row + node_count, :] = ref[rows, col:col + HD]
    live_s[0] = jnp.ones((BLOCK, HD), jnp.bfloat16)

    @pl.when(info_ref[seq_count] == 0)
    def _():
        top_s[...] = jnp.full(top_s.shape, floor_score, jnp.float32)
        sum_s[...] = jnp.zeros(sum_s.shape, jnp.float32)

    @pl.when(info_ref[seq_count] != 0)
    def _():
        for b in range(seq_count):
            rows = slice(b * seq_rows, (b + 1) * seq_rows)
            query = query_s[rows, :]
            scores = []
            for t in range(depth):
                bias = bias_refs[t][b * node_count:(b + 1) * node_count, :]
                score = score_dot(query, key_refs[t][...])
                scores.append(score * TO_LOG2 + jnp.concatenate([bias] * (2 * half_heads), axis=0))
            top = functools.reduce(jnp.maximum, scores)
            top = jnp.broadcast_to(jnp.max(top, axis=1, keepdims=True), top.shape)
            gathered = jnp.zeros((seq_rows, 2 * HD), jnp.float32)
            for t in range(depth):
                weight = jnp.exp2(scores[t] - top).astype(jnp.bfloat16)
                value = value_refs[t][...]
                value = jnp.concatenate([value, jnp.ones_like(value)], axis=1)
                gathered = gathered + jnp.dot(weight, value, preferred_element_type=jnp.float32)
            top_s[rows, :] = top
            sum_s[rows, :] = gathered

    def patch(i):
        left = left_of(i)
        slot = lax.rem(i, slots)

        @pl.when(left < BLOCK)
        def _():
            inside = lax.broadcasted_iota(jnp.int32, (BLOCK, HD), 0) < left
            key = cache_s[slot, :, :HD].astype(jnp.float32)
            value = cache_s[slot, :, HD:].astype(jnp.float32)
            key = jnp.where(inside, key, jnp.broadcast_to(key[:1, :], key.shape))
            cache_s[slot, :, :HD] = key.astype(jnp.bfloat16)
            cache_s[slot, :, HD:] = jnp.where(inside, value, 0.0).astype(jnp.bfloat16)

    def score_chunk(seq, slot, sub, c):
        rows = pl.ds(pl.multiple_of(seq * seq_rows, seq_rows), seq_rows)
        at = sub * SUB + c
        score_s[sub][:, c:c + CHUNK] = score_dot(query_s[rows, :], cache_s[slot, at:at + CHUNK, :HD])

    def weigh(seq, slot, part, sub, half, between):
        rows = pl.ds(pl.multiple_of(seq * seq_rows + half * half_rows, half_rows), half_rows)
        here = slice(half * half_rows, (half + 1) * half_rows)
        high = score_s[sub][here, :HD]
        for c in range(HD, SUB, HD):
            high = jnp.maximum(high, score_s[sub][here, c:c + HD])
        high = jnp.broadcast_to(jnp.max(high, axis=1, keepdims=True), high.shape) * TO_LOG2
        old = top_s[rows, :]
        top = jnp.maximum(old, high)
        top_s[rows, :] = top
        factor = jnp.exp2(old - top)
        between[0]()
        tops = wide(top, CHUNK)
        for c in range(0, SUB, CHUNK):
            weight = jnp.exp2(score_s[sub][here, c:c + CHUNK] * TO_LOG2 - tops)
            weight_s[sub][here, c:c + CHUNK] = weight.astype(jnp.bfloat16)
            if c == SUB // 2:
                between[1]()
        keys = slice(sub * SUB, (sub + 1) * SUB)
        value = jnp.concatenate([cache_s[slot, keys, HD:], live_s[part, keys, :]], axis=1)
        sum_s[rows, :] = sum_s[rows, :] * wide(factor, 2 * HD) + jnp.dot(
            weight_s[sub][here, :], value, preferred_element_type=jnp.float32
        )

    def phase(seq, slot, part, sub, next_seq, next_slot):
        ahead = [
            functools.partial(score_chunk, next_seq, next_slot, 1 - sub, c)
            for c in range(0, SUB, CHUNK)
        ]
        weigh(seq, slot, part, sub, 0, ahead[:2])
        weigh(seq, slot, part, sub, 1, ahead[2:])

    @pl.when(total > 0)
    def _():
        fetch(jnp.int32(0)).wait()
        patch(jnp.int32(0))
        seq, _ = place(jnp.int32(0))
        for c in range(0, SUB, CHUNK):
            score_chunk(seq, 0, 0, c)

    @pl.loop(0, total)
    def _(i):
        slot = lax.rem(i, slots)
        more = i + 1 < total

        @pl.when(more)
        def _():
            fetch(i + 1).wait()
            patch(i + 1)

        pl.when(i + 2 < total)(lambda: fetch(i + 2).start())
        seq, _ = place(i)
        left = left_of(i)
        part = jnp.where(left < BLOCK, 1, 0)

        @pl.when(left < BLOCK)
        def _():
            inside = lax.broadcasted_iota(jnp.int32, (BLOCK, HD), 0) < left
            live_s[1] = jnp.where(inside, 1.0, 0.0).astype(jnp.bfloat16)

        next_slot = jnp.where(more, lax.rem(i + 1, slots), slot)
        next_seq, _ = place(jnp.where(more, i + 1, i))
        phase(seq, slot, part, 0, seq, slot)
        phase(seq, slot, part, 1, next_seq, next_slot)

    for b in range(seq_count):
        rows = slice(b * node_count, (b + 1) * node_count)
        for h in range(2 * half_heads):
            row = b * seq_rows + h * node_count
            weight_sum = jnp.maximum(sum_s[row:row + node_count, HD:], 1e-30)
            result = sum_s[row:row + node_count, :HD] / weight_sum
            lse = top_s[row:row + node_count, :] + jnp.log2(weight_sum)
            col = h % half_heads * HD
            if h < half_heads:
                keep_ref[rows, col:col + HD] = result
                keep_lse_ref[rows, col:col + HD] = lse
            else:
                send_ref[rows, col:col + HD] = result
                send_ref[rows, half_heads * HD + col:half_heads * HD + col + HD] = lse


def attend(info, mine, other, keys, values, biases, cache):
    depth = len(keys)
    row_count, width = mine.shape
    seq_count, slot_count = cache.shape[:2]
    all_rows = 2 * width // HD * row_count
    seq_rows = all_rows // seq_count
    vmem = pl.BlockSpec(memory_space=pltpu.VMEM)
    return pl.pallas_call(
        functools.partial(attend_kernel, depth),
        out_shape=(
            jax.ShapeDtypeStruct((row_count, width), jnp.float32),
            jax.ShapeDtypeStruct((row_count, width), jnp.float32),
            jax.ShapeDtypeStruct((row_count, 2 * width), jnp.float32),
        ),
        in_specs=[pl.BlockSpec(memory_space=pltpu.SMEM)]
        + [vmem] * (2 + 3 * depth)
        + [pl.BlockSpec(memory_space=pltpu.HBM)],
        out_specs=(vmem, vmem, vmem),
        scratch_shapes=[
            pltpu.VMEM((all_rows, HD), jnp.bfloat16),
            pltpu.VMEM((seq_rows, SUB), jnp.float32),
            pltpu.VMEM((seq_rows, SUB), jnp.float32),
            pltpu.VMEM((seq_rows, SUB), jnp.bfloat16),
            pltpu.VMEM((seq_rows, SUB), jnp.bfloat16),
            pltpu.VMEM((all_rows, HD), jnp.float32),
            pltpu.VMEM((all_rows, 2 * HD), jnp.float32),
            pltpu.VMEM((3, BLOCK, 2 * HD), jnp.bfloat16),
            pltpu.VMEM((2, BLOCK, HD), jnp.bfloat16),
            pltpu.SemaphoreType.DMA((3,)),
        ],
        compiler_params=pltpu.CompilerParams(vmem_limit_bytes=24 * 1024 * 1024),
        cost_estimate=pl.CostEstimate(
            flops=4 * all_rows * slot_count * HD,
            bytes_accessed=2 * cache.size,
            transcendentals=all_rows * slot_count,
        ),
        name="attend",
    )(
        info, mine, other, *keys, *values, *biases,
        pltpu.with_memory_space_constraint(cache, pltpu.HBM),
    )


STRIP = 256
STRIPS = 4
TILE = 512


def join_kernel(start, side_ref, x_ref, weight_ref, keep_ref, send_ref, x_s, strip_s, total_s, x_sem, sems):
    side = side_ref[0]
    depth = x_s.shape[1]
    columns = total_s.shape[1]
    count = depth // STRIP
    own = 8

    def strip(i):
        slot = lax.rem(i, STRIPS)
        rows = pl.ds(pl.multiple_of(i * STRIP, STRIP), STRIP)
        return pltpu.make_async_copy(
            weight_ref.at[rows, pl.ds(start, columns)], strip_s.at[slot], sems.at[slot]
        )

    x_copy = pltpu.make_async_copy(x_ref, x_s, x_sem)
    x_copy.start()
    for i in range(STRIPS - 1):
        strip(jnp.int32(i)).start()
    total_s[...] = jnp.zeros(total_s.shape, jnp.float32)
    x_copy.wait()

    @pl.loop(0, count)
    def _(i):
        slot = lax.rem(i, STRIPS)
        pl.when(i + STRIPS - 1 < count)(lambda: strip(i + STRIPS - 1).start())
        strip(i).wait()
        x = x_s[:, pl.ds(pl.multiple_of(i * STRIP, STRIP), STRIP)]
        for c in range(0, columns, TILE):
            total_s[:, c:c + TILE] += jnp.dot(
                x, strip_s[slot, :, c:c + TILE], preferred_element_type=jnp.float32
            )

    for block in range(keep_ref.shape[0] // own):
        rows = slice(block * own, (block + 1) * own)
        keep_at = pl.multiple_of(2 * block * own + side * own, own)
        send_at = pl.multiple_of(2 * block * own + (1 - side) * own, own)
        keep_ref[rows, :] = total_s[pl.ds(keep_at, own), :]
        send_ref[rows, :] = total_s[pl.ds(send_at, own), :]


def join(side, x, weight, start, columns):
    rows, depth = x.shape
    out = jax.ShapeDtypeStruct((rows // 2, columns), jnp.float32)
    vmem = pl.BlockSpec(memory_space=pltpu.VMEM)
    return pl.pallas_call(
        functools.partial(join_kernel, start),
        out_shape=(out, out),
        in_specs=[
            pl.BlockSpec(memory_space=pltpu.SMEM),
            pl.BlockSpec(memory_space=pl.ANY),
            pl.BlockSpec(memory_space=pl.ANY),
        ],
        out_specs=(vmem, vmem),
        scratch_shapes=[
            pltpu.VMEM((rows, depth), x.dtype),
            pltpu.VMEM((STRIPS, STRIP, columns), weight.dtype),
            pltpu.VMEM((rows, columns), jnp.float32),
            pltpu.SemaphoreType.DMA,
            pltpu.SemaphoreType.DMA((STRIPS,)),
        ],
        compiler_params=pltpu.CompilerParams(vmem_limit_bytes=32 * 1024 * 1024),
        cost_estimate=pl.CostEstimate(
            flops=2 * rows * depth * columns, bytes_accessed=2 * depth * columns, transcendentals=0
        ),
        name="join",
    )(side[None], x, weight)


CORE, ACROSS, DEEP = range(3)


def bit_of(distance):
    return lax.axis_index("tensor") // (1 << distance) % 2


def fold(x, axis, distance, kind=jnp.bfloat16):
    bit = bit_of(distance)
    keep = lax.dynamic_index_in_dim(x, bit, axis, keepdims=False)
    send = lax.dynamic_index_in_dim(x, 1 - bit, axis, keepdims=False).astype(kind)
    return keep + partner(send, "tensor", distance).astype(jnp.float32)


def unfold(x, axis, distance):
    other = partner(x, "tensor", distance)
    upper = bit_of(distance) == 1
    return jnp.where(upper, jnp.stack([other, x], axis), jnp.stack([x, other], axis))


def depth_index():
    return lax.axis_index("tensor") >> DEEP


def depth_size():
    return lax.axis_size("tensor") >> DEEP


def across_depth(x, k):
    return lax.ppermute(x, "tensor", [(i, i ^ k << DEEP) for i in range(lax.axis_size("tensor"))])


def unfold_depth(x, axis):
    at = depth_index()
    got = [x] + [across_depth(x, k) for k in range(1, depth_size())]
    parts = []
    for place in range(depth_size()):
        part = got[-1]
        for k in range(depth_size() - 1):
            part = jnp.where(at ^ place == k, got[k], part)
        parts.append(part)
    return jnp.stack(parts, axis)


def depth_parts(x):
    at = depth_index()
    parts = [lax.dynamic_index_in_dim(x, at ^ k, 0, keepdims=False) for k in range(depth_size())]
    return parts[0], [part.astype(jnp.bfloat16) for part in parts[1:]]


def sent_down(sends):
    return [across_depth(send, k + 1) for k, send in enumerate(sends)]


def add_all(total, came):
    for part in came:
        total = total + part.astype(jnp.float32)
    return total


def sum_chips(first, second):
    first, second = lax.optimization_barrier((first, second))
    first = fold(first, 1, ACROSS)
    total, sends = depth_parts(first)
    second_total, second_sends = depth_parts(second)
    came, _ = lax.optimization_barrier((sent_down(second_sends), sends))
    second = fold(add_all(second_total, came), 0, ACROSS)
    return jnp.concatenate([add_all(total, sent_down(sends)), second], axis=-1)


def collect(rows, cut):
    first = unfold(unfold_depth(rows[:, :cut], 0), 1, ACROSS)
    second = unfold_depth(unfold(rows[:, cut:], 0, ACROSS), 0)
    both = unfold(jnp.concatenate([first, second], axis=-1), 2, CORE)
    return both.reshape(-1, both.shape[-1])


def local_pairs(
    tapped, join_weight, norm_gain, query_weight, kv_weight, out_weight, kv_cache, lengths, parents
):
    side = (lax.axis_index("tensor") % 2).astype(jnp.int32)
    row_count = tapped.shape[0]
    columns = join_weight.shape[1]
    sum_cut, cut = columns * 3 // 4, columns * 5 // 8
    spans = ((0, sum_cut), (sum_cut, columns))
    seq_count, piece_len = kv_cache.shape[:2]
    node_count = row_count // seq_count
    own_rows = row_count // 16
    row_ids = jnp.arange(row_count, dtype=jnp.int32)
    valid = jnp.clip(lengths - side * piece_len, 0, piece_len)
    info = jnp.concatenate([valid, side[None]]).astype(jnp.int32)
    parent_rows = row_ids // node_count * node_count + parents
    from_row = (parent_rows[:, :, None] == row_ids).astype(jnp.float32)
    hops = {}
    for step in range(STEPS):
        hops[step, step] = jnp.eye(row_count, dtype=jnp.float32)
        for earlier in range(step - 1, -1, -1):
            hops[step, earlier] = jnp.dot(hops[step, earlier + 1], from_row[earlier])
    bias = {at: (hop - 1.0) * -floor_score for at, hop in hops.items()}

    folded = []
    for start, end in spans:
        kept, sent = join(side, tapped, join_weight, start, end - start)
        part = kept + partner(sent, "tensor", CORE)
        folded.append(part.reshape(-1, 2, own_rows, end - start))
    hidden = sum_chips(*folded)

    keys, values = [], []
    for step in range(STEPS):
        normed = collect(normalize(hidden, norm_gain), cut)
        new_kv = jnp.dot(normed, kv_weight, preferred_element_type=jnp.float32)
        new_kv = new_kv.astype(jnp.bfloat16)
        query = jnp.dot(normed, query_weight, preferred_element_type=jnp.float32)
        query = query.astype(jnp.bfloat16)
        keys.append(partner(new_kv, "tensor", CORE))
        values.append(new_kv)
        kept, kept_lse, sent = attend(
            info, query, partner(query, "tensor", CORE), keys, values,
            [bias[step, t] for t in range(step + 1)], kv_cache,
        )
        came = partner(sent, "tensor", CORE)
        width = kept.shape[1]
        top = jnp.maximum(kept_lse, came[:, width:])
        mine = jnp.exp2(kept_lse - top)
        theirs = jnp.exp2(came[:, width:] - top)
        attended = (mine * kept + theirs * came[:, :width]) / (mine + theirs)
        update = jnp.dot(
            attended.astype(jnp.bfloat16), out_weight, preferred_element_type=jnp.float32
        ).reshape(-1, 2, 2, own_rows, columns)
        update = fold(update, 2, CORE)
        hidden = hidden + sum_chips(*[update[..., start:end] for start, end in spans])
    return hidden


def solution(mesh):
    body = local_pairs if mesh.shape["tensor"] == 2 * KVH else local_general
    placed = (
        P("groups", "tensor"),
        P("tensor", None),
        P(),
        P(None, "tensor"),
        P(None, "tensor"),
        P("tensor", None),
        P("groups", "tensor", None),
        P("groups"),
        P(None, "groups"),
    )
    return jax.shard_map(
        body, mesh=mesh, in_specs=placed, out_specs=P(("groups", "tensor"), None), check_vma=False
    )
```
